512 devices in a mesh: pair: 128 (over x, z, core), harm: 4 (over y).
Axes of the slice: x: 4, y: 4, z: 16, core: 2. Of those that a mesh axis runs over, the one named last changes fastest.
Arguments:
- stick: int32 [256, 65536], P(None, ('pair', 'harm')), may hold values from 0 to 1, as said below
- stiffness: float32 [65536], P(('pair', 'harm')), may hold values from 0.3 to 3
- slip_tangent: float32 [256, 65536], P(None, ('pair', 'harm')), may hold values from 0.02 to 1
- contact_force: float32 [256, 65536], P(None, ('pair', 'harm')), may hold values from -6 to 6
- owner_node: int32 [2, 65536], P(None, ('pair', 'harm')), may hold values from 0 to 16383, as said below
- live_pairs: int32 [512], P(('pair', 'harm')), may hold values from 32 to 128, as said below
Outputs:
- interface_blocks: bfloat16 [67, 68, 16384], P(None, 'harm', 'pair')
The draws below stay inside these ranges and needn't reach their ends.
Inputs may be any that keep to these rules, and one draw needn't show every extreme that they name: `stick`: each value is 0 or 1; each pair sticks at each sample independently, with a probability that is the same for one device's pairs and differs between devices. Pair p lies on device p div 128 of pair+harm (harm minor); node n is owned by device n div 32, which has the same harm index as the devices of the pairs that name it. owner_node[0, p] mod 32 is below 16 and owner_node[1, p] mod 32 is not. Of the 256 nodes named by one device's pairs (live or not), at most 3 are owned by the devices of any one pair index; in every draw, for each harm index, some pair index owns nodes named by every device of that harm index, all named by live pairs. `live_pairs`: some device has all 128 pairs live in every draw.
All inputs are finite; a program needn't handle non-finite values.
Results may differ from the reference program's by a relative error of at most 0.001.
Values may be sent and summed in bfloat16 or wider, within the bound.
No kernel may reach another device: no remote copies, remote signals or barrier semaphores. Data moves between devices by JAX's collectives and lax.ppermute only.
A program may use at most 64 MiB of HBM per device.

```python
import math
import jax
import jax.numpy as jnp
from jax import lax

HARMONICS = 33
SAMPLES = 256
PAIR_DEV = 128
NODE_DEV = 32
CAP = 3
PAIRS = 65536
NODES = 16384
N_PAIR = 128
N_HARM = 4


def draw_stick(key, part):
    devices = N_PAIR * N_HARM
    levels = jax.random.randint(jax.random.fold_in(key, 7), (devices,), 2, 8)
    per_pair = jnp.repeat(levels, PAIR_DEV, total_repeat_length=devices * PAIR_DEV)
    dice_rolls = jax.random.randint(jax.random.fold_in(key, 11), (SAMPLES, devices * PAIR_DEV), 0, 8)
    return (dice_rolls < per_pair[None, :]).astype(jnp.int32)


def draw_live_pairs(key, part):
    devices = N_PAIR * N_HARM
    counts = jax.random.randint(jax.random.fold_in(key, 3), (devices,), PAIR_DEV // 4, PAIR_DEV + 1)
    full_device = jax.random.randint(jax.random.fold_in(key, 5), (), 0, devices)
    return counts.at[full_device].set(PAIR_DEV).astype(jnp.int32)


def draw_owner_node(key, part):
    devices = N_PAIR * N_HARM
    slot_count = N_PAIR * CAP
    send_count = 2 * PAIR_DEV

    def per_device(device):
        dev_key = jax.random.fold_in(key, device)
        harm_index = device % N_HARM
        target = jax.random.randint(jax.random.fold_in(key, 1000003 + harm_index), (), 0, N_PAIR)
        shuffled = jax.random.permutation(jax.random.fold_in(dev_key, 1), slot_count).astype(jnp.int32)
        dest_of_slot = jnp.arange(slot_count, dtype=jnp.int32) // CAP
        priority = shuffled + slot_count * (dest_of_slot == target).astype(jnp.int32)
        chosen = jnp.argsort(-priority, stable=True)[:send_count]
        dest_pair = dest_of_slot[chosen]
        local_node = jax.random.randint(jax.random.fold_in(dev_key, 2), (send_count,), 0, NODE_DEV // 2)
        side_index = jnp.arange(send_count, dtype=jnp.int32) % 2
        local_node = local_node + side_index * (NODE_DEV // 2)
        node_index = (dest_pair * N_HARM + harm_index) * NODE_DEV + local_node
        return jnp.transpose(node_index.reshape(PAIR_DEV, 2), (1, 0))
    all_nodes = jax.vmap(per_device)(jnp.arange(devices, dtype=jnp.int32))
    return jnp.transpose(all_nodes, (1, 0, 2)).reshape(2, devices * PAIR_DEV).astype(jnp.int32)


def level_of(key, shape, pieces, low, high):
    def one(position, parts):
        heights = jax.random.uniform(jax.random.fold_in(jax.random.fold_in(key, 6), position), (parts,), jnp.float32, low / len(pieces), high / len(pieces))
        return jnp.repeat(jnp.exp(heights), shape[position] // parts).reshape((-1,) + (1,) * (len(shape) - position - 1))

    gain = one(*pieces[0])
    for cut in pieces[1:]:
        gain = gain * one(*cut)
    return gain


def gaussian(key, shape, spread, reach, split=(), held_as=jnp.bfloat16):
    level = level_of(key, shape, split, -0.22, 0.18) if split else 1.0
    drawn = jax.random.normal(key, shape, jnp.float32) * spread * level
    return jnp.minimum(jnp.maximum(drawn, -reach), reach).astype(held_as)


def setup_inputs(seed: int = 0) -> dict:
    key_of = jax.random.split(jax.random.key(seed), 7)
    return {
        "stick": draw_stick(jax.random.fold_in(key_of[6], 71), 0),
        "stiffness": jnp.clip(jnp.exp(math.log(3.0) - 2.3025851 * jax.random.uniform(key_of[1], (PAIRS,), jnp.float32) ** level_of(key_of[1], (PAIRS,), ((0, 512),), -0.2, 0.2)), 0.3, 3.0),
        "slip_tangent": jnp.clip(jnp.exp(math.log(1.0) - 3.912023 * jax.random.uniform(key_of[2], (SAMPLES, PAIRS), jnp.float32) ** level_of(key_of[2], (SAMPLES, PAIRS), ((1, 512),), -0.2, 0.2)), 0.02, 1.0),
        "contact_force": gaussian(key_of[3], (SAMPLES, PAIRS), 1.0, 6.0, ((1, 512),), jnp.float32),
        "owner_node": draw_owner_node(jax.random.fold_in(key_of[6], 71), 0),
        "live_pairs": draw_live_pairs(jax.random.fold_in(key_of[6], 71), 0),
    }


def fourier_basis(samples, coef_count):
    time_index = jnp.arange(samples, dtype=jnp.int32)[:, None]
    column = jnp.arange(coef_count, dtype=jnp.int32)[None, :]
    harmonic = (column + 1) // 2
    reduced = harmonic * time_index % samples
    phase_angle = reduced.astype(jnp.float32) * (2.0 * math.pi / samples)
    use_sine = jnp.logical_and(column > 0, column % 2 == 0)
    return jnp.where(use_sine, jnp.sin(phase_angle), jnp.cos(phase_angle))

def product_table(fourier, samples):
    coef_count = fourier.shape[1]
    outer = jnp.einsum('ti,tj->ijt', fourier, fourier)
    return outer.reshape(coef_count * coef_count, samples) * (2.0 / samples)

def sandwich(table, fourier, weights, forces):
    coef_count = fourier.shape[1]
    node_count = weights.shape[1]
    stiffness_part = jnp.dot(table, weights, precision=lax.Precision.HIGHEST)
    stiffness_part = stiffness_part.reshape(coef_count, coef_count, node_count)
    force_col = jnp.dot(fourier.T, forces, precision=lax.Precision.HIGHEST) / math.sqrt(fourier.shape[0])
    merged = jnp.concatenate([stiffness_part, force_col[:, None, :]], axis=1)
    return merged.reshape(coef_count * (coef_count + 1), node_count)

def reference(stick, stiffness, slip_tangent, contact_force, owner_node, live_pairs):
    samples, pairs = stick.shape
    coef_count = 2 * HARMONICS + 1
    pair_index = jnp.arange(pairs, dtype=jnp.int32)
    live_mask = (pair_index % PAIR_DEV < jnp.take(live_pairs, pair_index // PAIR_DEV)).astype(jnp.float32)
    stick_float = stick.astype(jnp.float32)
    weights = (stiffness * live_mask)[None, :] * (stick_float + (1.0 - stick_float) * slip_tangent)
    forces = contact_force * live_mask[None, :]
    stacked = jnp.concatenate([weights, forces], axis=0)
    node_data = jnp.zeros((2 * samples, NODES), jnp.float32)
    node_data = node_data.at[:, owner_node[0]].add(stacked)
    node_data = node_data.at[:, owner_node[1]].add(stacked)
    fourier = fourier_basis(samples, coef_count)
    table = product_table(fourier, samples)
    grouped = jnp.transpose(node_data.reshape(2 * samples, NODES // NODE_DEV, NODE_DEV), (1, 0, 2))

    def per_group(group_data):
        blocks = sandwich(table, fourier, group_data[:samples], group_data[samples:])
        return blocks.astype(jnp.bfloat16).reshape(coef_count, coef_count + 1, NODE_DEV)
    blocks = lax.map(per_group, grouped)
    return jnp.transpose(blocks, (1, 2, 0, 3)).reshape(coef_count, coef_count + 1, NODES)
```

```python
import functools
import math

import jax
import jax.numpy as jnp
import numpy as np
from jax import lax
from jax.experimental import pallas as pl
from jax.experimental.pallas import tpu as pltpu
from jax.sharding import Mesh
from jax.sharding import PartitionSpec as P

HARMONICS = 33
COEFS = 2 * HARMONICS + 1
SAMPLES = 256
NODE_DEV = 32
CAP = 3
SIZES = {"x": 4, "z": 16, "c": 2, "h": 4}
FIRST = ("x", "z")
REST = tuple(axis for axis in ("x", "z", "c") if axis not in FIRST)
N_FIRST = math.prod(SIZES[axis] for axis in FIRST)
N_REST = math.prod(SIZES[axis] for axis in REST)
N_HARM = SIZES["h"]
GROUP = -(-N_REST * CAP // 8) * 8
SLOTS = N_FIRST * GROUP

LANES = 128
W_LANES = 72
F_LOW = 34
MEAN, EXP_W, EXP_F, NODE = 112, 113, 114, 115
STEPS = 16.0
TOP = 32766.0
MEAN_PAIR = 2.0**21
MEAN_NODE = 2.0**31 / (1024.0 * CAP * N_FIRST)
PER = (COEFS + 1) // N_HARM
PAD = 72
T_ROWS = PER * PAD


def analysis_table():
    k = np.arange(HARMONICS * 2 + 1)[:, None]
    angle = (k * np.arange(SAMPLES)[None, :] % SAMPLES) * (2.0 * np.pi / SAMPLES)
    cosine, sine = np.cos(angle), np.sin(angle)
    basis = np.zeros((COEFS, SAMPLES))
    basis[0] = 1.0
    basis[1::2] = cosine[1 : HARMONICS + 1]
    basis[2::2] = sine[1 : HARMONICS + 1]
    table = np.zeros((2 * LANES, 2 * SAMPLES))
    top = 2 * HARMONICS
    table[:top, :SAMPLES] = cosine[1:]
    table[LANES : LANES + top, :SAMPLES] = sine[1:]
    table[MEAN, :SAMPLES] = 1.0
    table[W_LANES : W_LANES + F_LOW, SAMPLES:] = basis[:F_LOW]
    table[LANES + W_LANES : LANES + W_LANES + COEFS - F_LOW, SAMPLES:] = basis[F_LOW:]
    return table.astype(np.float32)


def synthesis_table():
    table = np.zeros((N_HARM, PER, PAD, 2 * LANES), np.float32)

    def add(row, kind, k, value):
        if kind == "s":
            if k == 0:
                return
            row[LANES + abs(k) - 1] += value if k > 0 else -value
        elif k == 0:
            row[MEAN] += value
        else:
            row[abs(k) - 1] += value

    for i in range(COEFS):
        a, i_sine = (i + 1) // 2, i > 0 and i % 2 == 0
        for j in range(COEFS + 1):
            row = table[j // PER, j % PER, i]
            if j == COEFS:
                lane = W_LANES + i if i < F_LOW else LANES + W_LANES + i - F_LOW
                row[lane] = 1.0 / math.sqrt(SAMPLES)
                continue
            b, j_sine = (j + 1) // 2, j > 0 and j % 2 == 0
            half = 1.0 / SAMPLES
            if i_sine and j_sine:
                add(row, "c", a - b, half)
                add(row, "c", a + b, -half)
            elif not i_sine and not j_sine:
                add(row, "c", a - b, half)
                add(row, "c", a + b, half)
            elif i_sine:
                add(row, "s", a + b, half)
                add(row, "s", a - b, half)
            else:
                add(row, "s", a + b, half)
                add(row, "s", b - a, half)
    return table.reshape(N_HARM, T_ROWS, 2 * LANES).astype(jnp.bfloat16)


def index_along(axes, part):
    index = 0
    for axis in axes:
        index = index * SIZES[axis] + part[axis]
    return index


def scale_step(largest):
    return jnp.ceil(jnp.log2(jnp.maximum(largest, 1e-30)) * STEPS + 0.01)


def send_kernel(live_ref, stick_ref, stiff_ref, slip_ref, force_ref, owner_ref, table_ref, out_ref):
    pairs = stick_ref.shape[1]
    live = (lax.broadcasted_iota(jnp.int32, (1, pairs), 1) < live_ref[0]).astype(jnp.float32)
    stick = stick_ref[...].astype(jnp.float32)
    weights = (stiff_ref[...] * live) * (stick + (1.0 - stick) * slip_ref[...])
    forces = force_ref[...] * live
    sums = jnp.dot(
        table_ref[...],
        jnp.concatenate([weights, forces], axis=0),
        precision=lax.Precision.HIGHEST,
        preferred_element_type=jnp.float32,
    )
    low, high = sums[:LANES], sums[LANES:]
    size = jnp.maximum(jnp.abs(low), jnp.abs(high))
    step_w = scale_step(jnp.max(size[:W_LANES], axis=0, keepdims=True))
    step_f = scale_step(jnp.max(size[W_LANES:MEAN], axis=0, keepdims=True))
    lane = lax.broadcasted_iota(jnp.int32, (LANES, pairs), 0)
    factor = jnp.where(
        lane < W_LANES, jnp.exp2(step_w * (-1.0 / STEPS)) * TOP, jnp.exp2(step_f * (-1.0 / STEPS)) * TOP
    )
    mean = jnp.round(sums[MEAN : MEAN + 1] * MEAN_PAIR).astype(jnp.int32)
    low = jnp.round(low * jnp.where(lane < MEAN, factor, 0.0)).astype(jnp.int32)
    low = jnp.where(lane == MEAN, ((mean & 0xFFFF) ^ 0x8000) - 0x8000, low)
    low = jnp.where(lane == EXP_W, step_w.astype(jnp.int32), low)
    low = jnp.where(lane == EXP_F, step_f.astype(jnp.int32), low)
    high = jnp.round(high * jnp.where(lane < MEAN, factor, 0.0)).astype(jnp.int32)
    high = jnp.where(lane == MEAN, mean >> 16, high)
    both = jnp.concatenate([low, high], axis=0)
    digits = jnp.concatenate([both >> 8, both & 255], axis=0).astype(jnp.float32).astype(jnp.bfloat16)

    owner = owner_ref[...]
    local = owner & (NODE_DEV - 1)
    target = owner // (N_HARM * NODE_DEV)
    first, second = target[0:1], target[1:2]
    square = (pairs, pairs)
    row_first = jnp.broadcast_to(first, square)
    row_second = jnp.broadcast_to(second, square)
    column_first = row_first.T
    column_second = row_second.T
    before = lax.broadcasted_iota(jnp.int32, square, 0) < lax.broadcasted_iota(jnp.int32, square, 1)
    count_first = jnp.where(before & (column_first == row_first), 1, 0)
    count_second = jnp.where(column_first == row_second, 1, 0) + jnp.where(
        before & (column_second == row_second), 1, 0
    )
    place_first = jnp.sum(count_first, axis=0, keepdims=True)
    place_second = jnp.sum(count_second, axis=0, keepdims=True)

    def slot_of(dest, place):
        part = {
            "x": dest // (SIZES["z"] * SIZES["c"]),
            "z": dest // SIZES["c"] % SIZES["z"],
            "c": dest % SIZES["c"],
        }
        return index_along(FIRST, part) * GROUP + index_along(REST, part) * CAP + place

    slot = lax.broadcasted_iota(jnp.int32, (SLOTS, pairs), 0)
    hit_first = slot == slot_of(first, place_first)
    hit_second = slot == slot_of(second, place_second)
    node = jnp.where(hit_first, local[0:1] + 1, 0) + jnp.where(hit_second, local[1:2] + 1, 0)
    node = jnp.sum(node, axis=1, keepdims=True) - 1
    pick = jnp.where(hit_first | hit_second, 1.0, 0.0).astype(jnp.bfloat16)
    sent = lax.dot_general(
        pick, digits, (((1,), (1,)), ((), ())), preferred_element_type=jnp.float32
    )
    value_low = (sent[:, :LANES] * 256.0 + sent[:, 2 * LANES : 3 * LANES]).astype(jnp.int32)
    value_high = (sent[:, LANES : 2 * LANES] * 256.0 + sent[:, 3 * LANES :]).astype(jnp.int32)
    words = (value_high << 16) | (value_low & 0xFFFF)
    word_lane = lax.broadcasted_iota(jnp.int32, (SLOTS, LANES), 1)
    out_ref[...] = jnp.where(word_lane == NODE, node, words)


def decode(words, mean_unit):
    lane = lax.broadcasted_iota(jnp.int32, words.shape, words.ndim - 1)
    low = ((words & 0xFFFF) ^ 0x8000) - 0x8000
    high = words >> 16
    step = jnp.where(
        lane < W_LANES, ((words[:, EXP_W : EXP_W + 1] & 0xFFFF) ^ 0x8000) - 0x8000,
        ((words[:, EXP_F : EXP_F + 1] & 0xFFFF) ^ 0x8000) - 0x8000,
    )
    scale = jnp.exp2(step.astype(jnp.float32) * (1.0 / STEPS)) * (1.0 / TOP)
    scale = jnp.where(lane < MEAN, scale, jnp.where(lane == MEAN, 1.0 / mean_unit, 0.0))
    low = jnp.where(lane == MEAN, words, low).astype(jnp.float32) * scale
    high = high.astype(jnp.float32) * jnp.where(lane < MEAN, scale, 0.0)
    return jnp.concatenate([low, high], axis=1)


def split_terms(values, count):
    terms = []
    for _ in range(count):
        term = values.astype(jnp.bfloat16)
        terms.append(term)
        values = values - term.astype(jnp.float32)
    return terms


def merge_kernel(words_ref, out_ref):
    words = words_ref[...]
    values = decode(words, MEAN_PAIR)
    rows = N_REST * NODE_DEV
    place = lax.broadcasted_iota(jnp.int32, (SLOTS, 1), 0) % GROUP // CAP
    node = words[:, NODE : NODE + 1]
    node = jnp.where(node >= 0, node + place * NODE_DEV, -1)
    owner = lax.broadcasted_iota(jnp.int32, (SLOTS, rows), 1) == node
    owner = jnp.where(owner, 1.0, 0.0).astype(jnp.bfloat16)
    terms = jnp.concatenate(split_terms(values, 3), axis=1)
    total = lax.dot_general(
        owner, terms, (((0,), (0,)), ((), ())), preferred_element_type=jnp.float32
    )
    low = total[:, :LANES] + (total[:, 2 * LANES : 3 * LANES] + total[:, 4 * LANES : 5 * LANES])
    high = total[:, LANES : 2 * LANES] + (total[:, 3 * LANES : 4 * LANES] + total[:, 5 * LANES :])
    size = jnp.maximum(jnp.abs(low), jnp.abs(high))
    lane = lax.broadcasted_iota(jnp.int32, size.shape, 1)
    step_w = scale_step(jnp.max(jnp.where(lane < W_LANES, size, 0.0), axis=1, keepdims=True))
    step_f = scale_step(
        jnp.max(jnp.where((lane >= W_LANES) & (lane < MEAN), size, 0.0), axis=1, keepdims=True)
    )
    factor = jnp.exp2(jnp.where(lane < W_LANES, step_w, step_f) * (-1.0 / STEPS)) * TOP
    factor = jnp.where(lane < MEAN, factor, 0.0)
    words = (jnp.round(high * factor).astype(jnp.int32) << 16) | (
        jnp.round(low * factor).astype(jnp.int32) & 0xFFFF
    )
    words = jnp.where(lane == MEAN, jnp.round(low * MEAN_NODE).astype(jnp.int32), words)
    words = jnp.where(lane == EXP_W, step_w.astype(jnp.int32), words)
    words = jnp.where(lane == EXP_F, step_f.astype(jnp.int32), words)
    for part in range(N_REST):
        for harm in range(N_HARM):
            start = (part * N_HARM + harm) * NODE_DEV
            out_ref[start : start + NODE_DEV] = words[part * NODE_DEV : (part + 1) * NODE_DEV]


def expand_kernel(words_ref, table_ref, out_ref, held_ref, sem):
    harm = lax.axis_index("h")
    copy = pltpu.make_async_copy(table_ref.at[harm], held_ref, sem)
    copy.start()
    nodes = N_HARM * NODE_DEV
    values = decode(words_ref[:nodes], MEAN_NODE)
    for part in range(1, N_REST):
        values += decode(words_ref[part * nodes : (part + 1) * nodes], MEAN_NODE)
    terms = jnp.concatenate(split_terms(values, 2), axis=0)
    copy.wait()
    blocks = lax.dot_general(
        held_ref[...], terms, (((1,), (1,)), ((), ())), preferred_element_type=jnp.float32
    )
    blocks = (blocks[:, :nodes] + blocks[:, nodes:]).reshape(PER, PAD, nodes)
    out_ref[...] = blocks[:, :COEFS].astype(jnp.bfloat16)


def on_device(stick, stiffness, slip_tangent, contact_force, owner_node, live_pairs):
    pairs = stick.shape[1]
    vmem = pl.BlockSpec(memory_space=pltpu.VMEM)
    params = pltpu.CompilerParams(vmem_limit_bytes=32 * 1024 * 1024)
    slots = pl.pallas_call(
        send_kernel,
        out_shape=jax.ShapeDtypeStruct((SLOTS, LANES), jnp.int32),
        in_specs=[pl.BlockSpec(memory_space=pltpu.SMEM)] + [vmem] * 6,
        out_specs=vmem,
        compiler_params=params,
    )(
        live_pairs,
        stick,
        stiffness.reshape(1, pairs),
        slip_tangent,
        contact_force,
        owner_node,
        jnp.asarray(analysis_table()),
    )
    slots = lax.all_to_all(slots.reshape(N_FIRST, GROUP, LANES), FIRST, 0, 0, tiled=True)
    sums = pl.pallas_call(
        merge_kernel,
        out_shape=jax.ShapeDtypeStruct((N_REST * N_HARM * NODE_DEV, LANES), jnp.int32),
        in_specs=[vmem],
        out_specs=vmem,
        compiler_params=params,
    )(slots.reshape(SLOTS, LANES))
    sums = lax.all_to_all(
        sums.reshape(N_REST * N_HARM, NODE_DEV, LANES), REST + ("h",), 0, 0, tiled=True
    )
    blocks = pl.pallas_call(
        expand_kernel,
        out_shape=jax.ShapeDtypeStruct((PER, COEFS, N_HARM * NODE_DEV), jnp.bfloat16),
        in_specs=[vmem, pl.BlockSpec(memory_space=pl.ANY)],
        out_specs=vmem,
        scratch_shapes=[pltpu.VMEM((T_ROWS, 2 * LANES), jnp.bfloat16), pltpu.SemaphoreType.DMA],
        compiler_params=params,
    )(sums.reshape(N_REST * N_HARM * NODE_DEV, LANES), jnp.asarray(synthesis_table()))
    return jnp.transpose(blocks, (1, 0, 2))


def solution(mesh):
    fine = Mesh(mesh.devices.reshape(tuple(SIZES.values())), tuple(SIZES))
    every = ("x", "z", "c", "h")
    return jax.shard_map(
        on_device,
        mesh=fine,
        in_specs=(P(None, every), P(every), P(None, every), P(None, every), P(None, every), P(every)),
        out_specs=P(None, "h", ("x", "z", "c")),
        check_vma=False,
    )
```

```python
import functools
import math

import jax
import jax.numpy as jnp
import numpy as np
from jax import lax
from jax.experimental import pallas as pl
from jax.experimental.pallas import tpu as pltpu
from jax.sharding import Mesh
from jax.sharding import PartitionSpec as P

HARMONICS = 33
COEFS = 2 * HARMONICS + 1
SAMPLES = 256
NODE_DEV = 32
CAP = 3
SIZES = {"x": 4, "z": 16, "c": 2, "h": 4}
FIRST = ("z",)
REST = tuple(axis for axis in ("x", "z", "c") if axis not in FIRST)
N_FIRST = math.prod(SIZES[axis] for axis in FIRST)
N_REST = math.prod(SIZES[axis] for axis in REST)
N_HARM = SIZES["h"]
GROUP = -(-N_REST * CAP // 8) * 8
SLOTS = N_FIRST * GROUP

LANES = 128
W_LANES = 72
F_LOW = 34
MEAN, EXP_W, EXP_F, NODE = 112, 113, 114, 115
STEPS = 16.0
TOP = 32766.0
MEAN_PAIR = 2.0**21
MEAN_NODE = 2.0**31 / (1024.0 * CAP * N_FIRST)
PER = (COEFS + 1) // N_HARM
PAD = 72
T_ROWS = PER * PAD


def analysis_table():
    k = np.arange(HARMONICS * 2 + 1)[:, None]
    angle = (k * np.arange(SAMPLES)[None, :] % SAMPLES) * (2.0 * np.pi / SAMPLES)
    cosine, sine = np.cos(angle), np.sin(angle)
    basis = np.zeros((COEFS, SAMPLES))
    basis[0] = 1.0
    basis[1::2] = cosine[1 : HARMONICS + 1]
    basis[2::2] = sine[1 : HARMONICS + 1]
    table = np.zeros((2 * LANES, 2 * SAMPLES))
    top = 2 * HARMONICS
    table[:top, :SAMPLES] = cosine[1:]
    table[LANES : LANES + top, :SAMPLES] = sine[1:]
    table[MEAN, :SAMPLES] = 1.0
    table[W_LANES : W_LANES + F_LOW, SAMPLES:] = basis[:F_LOW]
    table[LANES + W_LANES : LANES + W_LANES + COEFS - F_LOW, SAMPLES:] = basis[F_LOW:]
    return table.astype(np.float32)


def synthesis_table():
    table = np.zeros((N_HARM, PER, PAD, 2 * LANES), np.float32)

    def add(row, kind, k, value):
        if kind == "s":
            if k == 0:
                return
            row[LANES + abs(k) - 1] += value if k > 0 else -value
        elif k == 0:
            row[MEAN] += value
        else:
            row[abs(k) - 1] += value

    for i in range(COEFS):
        a, i_sine = (i + 1) // 2, i > 0 and i % 2 == 0
        for j in range(COEFS + 1):
            row = table[j // PER, j % PER, i]
            if j == COEFS:
                lane = W_LANES + i if i < F_LOW else LANES + W_LANES + i - F_LOW
                row[lane] = 1.0 / math.sqrt(SAMPLES)
                continue
            b, j_sine = (j + 1) // 2, j > 0 and j % 2 == 0
            half = 1.0 / SAMPLES
            if i_sine and j_sine:
                add(row, "c", a - b, half)
                add(row, "c", a + b, -half)
            elif not i_sine and not j_sine:
                add(row, "c", a - b, half)
                add(row, "c", a + b, half)
            elif i_sine:
                add(row, "s", a + b, half)
                add(row, "s", a - b, half)
            else:
                add(row, "s", a + b, half)
                add(row, "s", b - a, half)
    return table.reshape(N_HARM, T_ROWS, 2 * LANES).astype(jnp.bfloat16)


def index_along(axes, part):
    index = 0
    for axis in axes:
        index = index * SIZES[axis] + part[axis]
    return index


def scale_step(largest):
    return jnp.ceil(jnp.log2(jnp.maximum(largest, 1e-30)) * STEPS + 0.01)


def send_kernel(
    live_ref, stick_hbm, stiff_hbm, slip_hbm, force_hbm, owner_hbm, table_hbm, out_ref,
    stick_ref, stiff_ref, slip_ref, force_ref, owner_ref, table_ref, sems,
):
    copies = [
        pltpu.make_async_copy(source, held, sems.at[n])
        for n, (source, held) in enumerate(
            (
                (owner_hbm, owner_ref),
                (stiff_hbm, stiff_ref),
                (stick_hbm, stick_ref),
                (slip_hbm, slip_ref),
                (force_hbm, force_ref),
                (table_hbm, table_ref),
            )
        )
    ]
    for copy in copies:
        copy.start()
    pairs = stick_ref.shape[1]
    copies[0].wait()
    owner = owner_ref[...]
    local = owner & (NODE_DEV - 1)
    target = owner // (N_HARM * NODE_DEV)
    first, second = target[0:1], target[1:2]
    square = (pairs, pairs)
    row_first = jnp.broadcast_to(first, square)
    row_second = jnp.broadcast_to(second, square)
    column_first = row_first.T
    column_second = row_second.T
    before = lax.broadcasted_iota(jnp.int32, square, 0) < lax.broadcasted_iota(jnp.int32, square, 1)
    count_first = jnp.where(before & (column_first == row_first), 1, 0)
    count_second = jnp.where(column_first == row_second, 1, 0) + jnp.where(
        before & (column_second == row_second), 1, 0
    )
    place_first = jnp.sum(count_first, axis=0, keepdims=True)
    place_second = jnp.sum(count_second, axis=0, keepdims=True)

    def slot_of(dest, place):
        part = {
            "x": dest // (SIZES["z"] * SIZES["c"]),
            "z": dest // SIZES["c"] % SIZES["z"],
            "c": dest % SIZES["c"],
        }
        return index_along(FIRST, part) * GROUP + index_along(REST, part) * CAP + place

    slot = lax.broadcasted_iota(jnp.int32, (SLOTS, pairs), 0)
    hit_first = slot == slot_of(first, place_first)
    hit_second = slot == slot_of(second, place_second)
    node = jnp.where(hit_first, local[0:1] + 1, 0) + jnp.where(hit_second, local[1:2] + 1, 0)
    node = jnp.sum(node, axis=1, keepdims=True) - 1
    pick = jnp.where(hit_first | hit_second, 1.0, 0.0).astype(jnp.bfloat16)
    for copy in copies[1:]:
        copy.wait()
    live = (lax.broadcasted_iota(jnp.int32, (1, pairs), 1) < live_ref[0]).astype(jnp.float32)
    stick = stick_ref[...].astype(jnp.float32)
    weights = (stiff_ref[...] * live) * (stick + (1.0 - stick) * slip_ref[...])
    forces = force_ref[...] * live
    sums = jnp.dot(
        table_ref[...],
        jnp.concatenate([weights, forces], axis=0),
        precision=lax.Precision.HIGHEST,
        preferred_element_type=jnp.float32,
    )
    low, high = sums[:LANES], sums[LANES:]
    size = jnp.maximum(jnp.abs(low), jnp.abs(high))
    step_w = scale_step(jnp.max(size[:W_LANES], axis=0, keepdims=True))
    step_f = scale_step(jnp.max(size[W_LANES:MEAN], axis=0, keepdims=True))
    lane = lax.broadcasted_iota(jnp.int32, (LANES, pairs), 0)
    factor = jnp.where(
        lane < W_LANES, jnp.exp2(step_w * (-1.0 / STEPS)) * TOP, jnp.exp2(step_f * (-1.0 / STEPS)) * TOP
    )
    mean = jnp.round(sums[MEAN : MEAN + 1] * MEAN_PAIR).astype(jnp.int32)
    low = jnp.round(low * jnp.where(lane < MEAN, factor, 0.0)).astype(jnp.int32)
    low = jnp.where(lane == MEAN, ((mean & 0xFFFF) ^ 0x8000) - 0x8000, low)
    low = jnp.where(lane == EXP_W, step_w.astype(jnp.int32), low)
    low = jnp.where(lane == EXP_F, step_f.astype(jnp.int32), low)
    high = jnp.round(high * jnp.where(lane < MEAN, factor, 0.0)).astype(jnp.int32)
    high = jnp.where(lane == MEAN, mean >> 16, high)
    both = jnp.concatenate([low, high], axis=0)
    digits = jnp.concatenate([both >> 8, both & 255], axis=0).astype(jnp.float32).astype(jnp.bfloat16)
    sent = lax.dot_general(
        pick, digits, (((1,), (1,)), ((), ())), preferred_element_type=jnp.float32
    )
    value_low = (sent[:, :LANES] * 256.0 + sent[:, 2 * LANES : 3 * LANES]).astype(jnp.int32)
    value_high = (sent[:, LANES : 2 * LANES] * 256.0 + sent[:, 3 * LANES :]).astype(jnp.int32)
    words = (value_high << 16) | (value_low & 0xFFFF)
    word_lane = lax.broadcasted_iota(jnp.int32, (SLOTS, LANES), 1)
    out_ref[...] = jnp.where(word_lane == NODE, node, words)


def decode(words, mean_unit):
    lane = lax.broadcasted_iota(jnp.int32, words.shape, words.ndim - 1)
    low = ((words & 0xFFFF) ^ 0x8000) - 0x8000
    high = words >> 16
    step = jnp.where(
        lane < W_LANES, ((words[:, EXP_W : EXP_W + 1] & 0xFFFF) ^ 0x8000) - 0x8000,
        ((words[:, EXP_F : EXP_F + 1] & 0xFFFF) ^ 0x8000) - 0x8000,
    )
    scale = jnp.exp2(step.astype(jnp.float32) * (1.0 / STEPS)) * (1.0 / TOP)
    scale = jnp.where(lane < MEAN, scale, jnp.where(lane == MEAN, 1.0 / mean_unit, 0.0))
    low = jnp.where(lane == MEAN, words, low).astype(jnp.float32) * scale
    high = high.astype(jnp.float32) * jnp.where(lane < MEAN, scale, 0.0)
    return jnp.concatenate([low, high], axis=1)


def split_terms(values, count):
    terms = []
    for _ in range(count):
        term = values.astype(jnp.bfloat16)
        terms.append(term)
        values = values - term.astype(jnp.float32)
    return terms


def merge_kernel(words_ref, out_ref):
    words = words_ref[...]
    values = decode(words, MEAN_PAIR)
    rows = N_REST * NODE_DEV
    place = lax.broadcasted_iota(jnp.int32, (SLOTS, 1), 0) % GROUP // CAP
    node = words[:, NODE : NODE + 1]
    node = jnp.where(node >= 0, node + place * NODE_DEV, -1)
    owner = lax.broadcasted_iota(jnp.int32, (SLOTS, rows), 1) == node
    owner = jnp.where(owner, 1.0, 0.0).astype(jnp.bfloat16)
    terms = jnp.concatenate(split_terms(values, 3), axis=1)
    total = lax.dot_general(
        owner, terms, (((0,), (0,)), ((), ())), preferred_element_type=jnp.float32
    )
    low = total[:, :LANES] + (total[:, 2 * LANES : 3 * LANES] + total[:, 4 * LANES : 5 * LANES])
    high = total[:, LANES : 2 * LANES] + (total[:, 3 * LANES : 4 * LANES] + total[:, 5 * LANES :])
    size = jnp.maximum(jnp.abs(low), jnp.abs(high))
    lane = lax.broadcasted_iota(jnp.int32, size.shape, 1)
    step_w = scale_step(jnp.max(jnp.where(lane < W_LANES, size, 0.0), axis=1, keepdims=True))
    step_f = scale_step(
        jnp.max(jnp.where((lane >= W_LANES) & (lane < MEAN), size, 0.0), axis=1, keepdims=True)
    )
    factor = jnp.exp2(jnp.where(lane < W_LANES, step_w, step_f) * (-1.0 / STEPS)) * TOP
    factor = jnp.where(lane < MEAN, factor, 0.0)
    words = (jnp.round(high * factor).astype(jnp.int32) << 16) | (
        jnp.round(low * factor).astype(jnp.int32) & 0xFFFF
    )
    words = jnp.where(lane == MEAN, jnp.round(low * MEAN_NODE).astype(jnp.int32), words)
    words = jnp.where(lane == EXP_W, step_w.astype(jnp.int32), words)
    words = jnp.where(lane == EXP_F, step_f.astype(jnp.int32), words)
    for part in range(N_REST):
        for harm in range(N_HARM):
            start = (part * N_HARM + harm) * NODE_DEV
            out_ref[start : start + NODE_DEV] = words[part * NODE_DEV : (part + 1) * NODE_DEV]


def expand_kernel(words_ref, table_ref, out_ref, held_ref, sem):
    harm = lax.axis_index("h")
    copy = pltpu.make_async_copy(table_ref.at[harm], held_ref, sem)
    copy.start()
    nodes = N_HARM * NODE_DEV
    values = decode(words_ref[:nodes], MEAN_NODE)
    for part in range(1, N_REST):
        values += decode(words_ref[part * nodes : (part + 1) * nodes], MEAN_NODE)
    terms = jnp.concatenate(split_terms(values, 2), axis=0)
    copy.wait()
    blocks = lax.dot_general(
        held_ref[...], terms, (((1,), (1,)), ((), ())), preferred_element_type=jnp.float32
    )
    blocks = (blocks[:, :nodes] + blocks[:, nodes:]).reshape(PER, PAD, nodes)
    out_ref[...] = blocks[:, :COEFS].astype(jnp.bfloat16)


def in_hbm(array):
    return pltpu.with_memory_space_constraint(array, pltpu.HBM)


def on_device(stick, stiffness, slip_tangent, contact_force, owner_node, live_pairs):
    pairs = stick.shape[1]
    vmem = pl.BlockSpec(memory_space=pltpu.VMEM)
    hbm = pl.BlockSpec(memory_space=pltpu.HBM)
    params = pltpu.CompilerParams(vmem_limit_bytes=32 * 1024 * 1024)
    slots = pl.pallas_call(
        send_kernel,
        out_shape=jax.ShapeDtypeStruct((SLOTS, LANES), jnp.int32),
        in_specs=[pl.BlockSpec(memory_space=pltpu.SMEM)] + [hbm] * 6,
        out_specs=vmem,
        scratch_shapes=[
            pltpu.VMEM((SAMPLES, pairs), jnp.int32),
            pltpu.VMEM((1, pairs), jnp.float32),
            pltpu.VMEM((SAMPLES, pairs), jnp.float32),
            pltpu.VMEM((SAMPLES, pairs), jnp.float32),
            pltpu.VMEM((2, pairs), jnp.int32),
            pltpu.VMEM((2 * LANES, 2 * SAMPLES), jnp.float32),
            pltpu.SemaphoreType.DMA((6,)),
        ],
        compiler_params=params,
    )(
        live_pairs,
        in_hbm(stick),
        in_hbm(stiffness.reshape(1, pairs)),
        in_hbm(slip_tangent),
        in_hbm(contact_force),
        in_hbm(owner_node),
        in_hbm(jnp.asarray(analysis_table())),
    )
    slots = lax.all_to_all(slots.reshape(N_FIRST, GROUP, LANES), FIRST, 0, 0, tiled=True)
    sums = pl.pallas_call(
        merge_kernel,
        out_shape=jax.ShapeDtypeStruct((N_REST * N_HARM * NODE_DEV, LANES), jnp.int32),
        in_specs=[vmem],
        out_specs=vmem,
        compiler_params=params,
    )(slots.reshape(SLOTS, LANES))
    sums = lax.all_to_all(
        sums.reshape(N_REST * N_HARM, NODE_DEV, LANES), REST + ("h",), 0, 0, tiled=True
    )
    blocks = pl.pallas_call(
        expand_kernel,
        out_shape=jax.ShapeDtypeStruct((PER, COEFS, N_HARM * NODE_DEV), jnp.bfloat16),
        in_specs=[vmem, hbm],
        out_specs=vmem,
        scratch_shapes=[pltpu.VMEM((T_ROWS, 2 * LANES), jnp.bfloat16), pltpu.SemaphoreType.DMA],
        compiler_params=params,
    )(sums.reshape(N_REST * N_HARM * NODE_DEV, LANES), in_hbm(jnp.asarray(synthesis_table())))
    return jnp.transpose(blocks, (1, 0, 2))


def solution(mesh):
    fine = Mesh(mesh.devices.reshape(tuple(SIZES.values())), tuple(SIZES))
    every = ("x", "z", "c", "h")
    return jax.shard_map(
        on_device,
        mesh=fine,
        in_specs=(P(None, every), P(every), P(None, every), P(None, every), P(None, every), P(every)),
        out_specs=P(None, "h", ("x", "z", "c")),
        check_vma=False,
    )
```

```python
import functools
import math

import jax
import jax.numpy as jnp
import numpy as np
from jax import lax
from jax.experimental import pallas as pl
from jax.experimental.pallas import tpu as pltpu
from jax.sharding import Mesh
from jax.sharding import PartitionSpec as P

HARMONICS = 33
COEFS = 2 * HARMONICS + 1
SAMPLES = 256
NODE_DEV = 32
CAP = 3
SIZES = {"x": 4, "z": 16, "c": 2, "h": 4}
FIRST = ("x", "z")
REST = tuple(axis for axis in ("x", "z", "c") if axis not in FIRST)
N_FIRST = math.prod(SIZES[axis] for axis in FIRST)
N_REST = math.prod(SIZES[axis] for axis in REST)
N_HARM = SIZES["h"]
GROUP = N_REST * CAP
SLOTS = N_FIRST * GROUP

LANES = 128
W_LANES = 72
F_LOW = 34
MEAN, EXP_W, EXP_F, NODE = 112, 113, 114, 115
STEPS = 16.0
TOP = 32766.0
MEAN_PAIR = 2.0**21
MEAN_NODE = 2.0**31 / (1024.0 * CAP * N_FIRST)
PER = (COEFS + 1) // N_HARM
PAD = 72
T_ROWS = PER * PAD


def analysis_table():
    k = np.arange(HARMONICS * 2 + 1)[:, None]
    angle = (k * np.arange(SAMPLES)[None, :] % SAMPLES) * (2.0 * np.pi / SAMPLES)
    cosine, sine = np.cos(angle), np.sin(angle)
    basis = np.zeros((COEFS, SAMPLES))
    basis[0] = 1.0
    basis[1::2] = cosine[1 : HARMONICS + 1]
    basis[2::2] = sine[1 : HARMONICS + 1]
    table = np.zeros((2 * LANES, 2 * SAMPLES))
    top = 2 * HARMONICS
    table[:top, :SAMPLES] = cosine[1:]
    table[LANES : LANES + top, :SAMPLES] = sine[1:]
    table[MEAN, :SAMPLES] = 1.0
    table[W_LANES : W_LANES + F_LOW, SAMPLES:] = basis[:F_LOW]
    table[LANES + W_LANES : LANES + W_LANES + COEFS - F_LOW, SAMPLES:] = basis[F_LOW:]
    return table.astype(np.float32)


def synthesis_table():
    table = np.zeros((N_HARM, PER, PAD, 2 * LANES), np.float32)

    def add(row, kind, k, value):
        if kind == "s":
            if k == 0:
                return
            row[LANES + abs(k) - 1] += value if k > 0 else -value
        elif k == 0:
            row[MEAN] += value
        else:
            row[abs(k) - 1] += value

    for i in range(COEFS):
        a, i_sine = (i + 1) // 2, i > 0 and i % 2 == 0
        for j in range(COEFS + 1):
            row = table[j // PER, j % PER, i]
            if j == COEFS:
                lane = W_LANES + i if i < F_LOW else LANES + W_LANES + i - F_LOW
                row[lane] = 1.0 / math.sqrt(SAMPLES)
                continue
            b, j_sine = (j + 1) // 2, j > 0 and j % 2 == 0
            half = 1.0 / SAMPLES
            if i_sine and j_sine:
                add(row, "c", a - b, half)
                add(row, "c", a + b, -half)
            elif not i_sine and not j_sine:
                add(row, "c", a - b, half)
                add(row, "c", a + b, half)
            elif i_sine:
                add(row, "s", a + b, half)
                add(row, "s", a - b, half)
            else:
                add(row, "s", a + b, half)
                add(row, "s", b - a, half)
    return table.reshape(N_HARM, T_ROWS, 2 * LANES).astype(jnp.bfloat16)


def index_along(axes, part):
    index = 0
    for axis in axes:
        index = index * SIZES[axis] + part[axis]
    return index


def scale_step(largest):
    return jnp.ceil(jnp.log2(jnp.maximum(largest, 1e-30)) * STEPS + 0.01)


def send_kernel(
    live_ref, stick_hbm, stiff_hbm, slip_hbm, force_hbm, owner_hbm, table_hbm, out_ref,
    stick_ref, stiff_ref, slip_ref, force_ref, owner_ref, table_ref, sems,
):
    copies = [
        pltpu.make_async_copy(source, held, sems.at[n])
        for n, (source, held) in enumerate(
            (
                (owner_hbm, owner_ref),
                (stiff_hbm, stiff_ref),
                (stick_hbm, stick_ref),
                (slip_hbm, slip_ref),
                (force_hbm, force_ref),
                (table_hbm, table_ref),
            )
        )
    ]
    for copy in copies:
        copy.start()
    pairs = stick_ref.shape[1]
    copies[0].wait()
    owner = owner_ref[...]
    local = owner & (NODE_DEV - 1)
    target = owner // (N_HARM * NODE_DEV)
    first, second = target[0:1], target[1:2]
    square = (pairs, pairs)
    row_first = jnp.broadcast_to(first, square)
    row_second = jnp.broadcast_to(second, square)
    column_first = row_first.T
    column_second = row_second.T
    before = lax.broadcasted_iota(jnp.int32, square, 0) < lax.broadcasted_iota(jnp.int32, square, 1)
    count_first = jnp.where(before & (column_first == row_first), 1, 0)
    count_second = jnp.where(column_first == row_second, 1, 0) + jnp.where(
        before & (column_second == row_second), 1, 0
    )
    place_first = jnp.sum(count_first, axis=0, keepdims=True)
    place_second = jnp.sum(count_second, axis=0, keepdims=True)

    def slot_of(dest, place):
        part = {
            "x": dest // (SIZES["z"] * SIZES["c"]),
            "z": dest // SIZES["c"] % SIZES["z"],
            "c": dest % SIZES["c"],
        }
        return index_along(FIRST, part) * GROUP + index_along(REST, part) * CAP + place

    slot = lax.broadcasted_iota(jnp.int32, (SLOTS, pairs), 0)
    hit_first = slot == slot_of(first, place_first)
    hit_second = slot == slot_of(second, place_second)
    node = jnp.where(hit_first, local[0:1] + 1, 0) + jnp.where(hit_second, local[1:2] + 1, 0)
    node = jnp.sum(node, axis=1, keepdims=True) - 1
    pick = jnp.where(hit_first | hit_second, 1.0, 0.0).astype(jnp.bfloat16)
    for copy in copies[1:]:
        copy.wait()
    live = (lax.broadcasted_iota(jnp.int32, (1, pairs), 1) < live_ref[0]).astype(jnp.float32)
    stick = stick_ref[...].astype(jnp.float32)
    weights = (stiff_ref[...] * live) * (stick + (1.0 - stick) * slip_ref[...])
    forces = force_ref[...] * live
    sums = jnp.dot(
        table_ref[...],
        jnp.concatenate([weights, forces], axis=0),
        precision=lax.Precision.HIGHEST,
        preferred_element_type=jnp.float32,
    )
    low, high = sums[:LANES], sums[LANES:]
    size = jnp.maximum(jnp.abs(low), jnp.abs(high))
    step_w = scale_step(jnp.max(size[:W_LANES], axis=0, keepdims=True))
    step_f = scale_step(jnp.max(size[W_LANES:MEAN], axis=0, keepdims=True))
    lane = lax.broadcasted_iota(jnp.int32, (LANES, pairs), 0)
    factor = jnp.where(
        lane < W_LANES, jnp.exp2(step_w * (-1.0 / STEPS)) * TOP, jnp.exp2(step_f * (-1.0 / STEPS)) * TOP
    )
    mean = jnp.round(sums[MEAN : MEAN + 1] * MEAN_PAIR).astype(jnp.int32)
    low = jnp.round(low * jnp.where(lane < MEAN, factor, 0.0)).astype(jnp.int32)
    low = jnp.where(lane == MEAN, ((mean & 0xFFFF) ^ 0x8000) - 0x8000, low)
    low = jnp.where(lane == EXP_W, step_w.astype(jnp.int32), low)
    low = jnp.where(lane == EXP_F, step_f.astype(jnp.int32), low)
    high = jnp.round(high * jnp.where(lane < MEAN, factor, 0.0)).astype(jnp.int32)
    high = jnp.where(lane == MEAN, mean >> 16, high)
    both = jnp.concatenate([low, high], axis=0)
    digits = jnp.concatenate([both >> 8, both & 255], axis=0).astype(jnp.float32).astype(jnp.bfloat16)
    sent = lax.dot_general(
        pick, digits, (((1,), (1,)), ((), ())), preferred_element_type=jnp.float32
    )
    value_low = (sent[:, :LANES] * 256.0 + sent[:, 2 * LANES : 3 * LANES]).astype(jnp.int32)
    value_high = (sent[:, LANES : 2 * LANES] * 256.0 + sent[:, 3 * LANES :]).astype(jnp.int32)
    words = (value_high << 16) | (value_low & 0xFFFF)
    word_lane = lax.broadcasted_iota(jnp.int32, (SLOTS, LANES), 1)
    out_ref[...] = jnp.where(word_lane == NODE, node, words)


def decode(words, mean_unit):
    lane = lax.broadcasted_iota(jnp.int32, words.shape, words.ndim - 1)
    low = ((words & 0xFFFF) ^ 0x8000) - 0x8000
    high = words >> 16
    step = jnp.where(
        lane < W_LANES, ((words[:, EXP_W : EXP_W + 1] & 0xFFFF) ^ 0x8000) - 0x8000,
        ((words[:, EXP_F : EXP_F + 1] & 0xFFFF) ^ 0x8000) - 0x8000,
    )
    scale = jnp.exp2(step.astype(jnp.float32) * (1.0 / STEPS)) * (1.0 / TOP)
    scale = jnp.where(lane < MEAN, scale, jnp.where(lane == MEAN, 1.0 / mean_unit, 0.0))
    low = jnp.where(lane == MEAN, words, low).astype(jnp.float32) * scale
    high = high.astype(jnp.float32) * jnp.where(lane < MEAN, scale, 0.0)
    return jnp.concatenate([low, high], axis=1)


def split_terms(values, count):
    terms = []
    for _ in range(count):
        term = values.astype(jnp.bfloat16)
        terms.append(term)
        values = values - term.astype(jnp.float32)
    return terms


def merge_kernel(words_ref, out_ref):
    words = words_ref[...]
    values = decode(words, MEAN_PAIR)
    rows = N_REST * NODE_DEV
    place = lax.broadcasted_iota(jnp.int32, (SLOTS, 1), 0) % GROUP // CAP
    node = words[:, NODE : NODE + 1]
    node = jnp.where(node >= 0, node + place * NODE_DEV, -1)
    owner = lax.broadcasted_iota(jnp.int32, (SLOTS, rows), 1) == node
    owner = jnp.where(owner, 1.0, 0.0).astype(jnp.bfloat16)
    terms = jnp.concatenate(split_terms(values, 3), axis=1)
    total = lax.dot_general(
        owner, terms, (((0,), (0,)), ((), ())), preferred_element_type=jnp.float32
    )
    low = total[:, :LANES] + (total[:, 2 * LANES : 3 * LANES] + total[:, 4 * LANES : 5 * LANES])
    high = total[:, LANES : 2 * LANES] + (total[:, 3 * LANES : 4 * LANES] + total[:, 5 * LANES :])
    size = jnp.maximum(jnp.abs(low), jnp.abs(high))
    lane = lax.broadcasted_iota(jnp.int32, size.shape, 1)
    step_w = scale_step(jnp.max(jnp.where(lane < W_LANES, size, 0.0), axis=1, keepdims=True))
    step_f = scale_step(
        jnp.max(jnp.where((lane >= W_LANES) & (lane < MEAN), size, 0.0), axis=1, keepdims=True)
    )
    factor = jnp.exp2(jnp.where(lane < W_LANES, step_w, step_f) * (-1.0 / STEPS)) * TOP
    factor = jnp.where(lane < MEAN, factor, 0.0)
    words = (jnp.round(high * factor).astype(jnp.int32) << 16) | (
        jnp.round(low * factor).astype(jnp.int32) & 0xFFFF
    )
    words = jnp.where(lane == MEAN, jnp.round(low * MEAN_NODE).astype(jnp.int32), words)
    words = jnp.where(lane == EXP_W, step_w.astype(jnp.int32), words)
    words = jnp.where(lane == EXP_F, step_f.astype(jnp.int32), words)
    for part in range(N_REST):
        for harm in range(N_HARM):
            start = (part * N_HARM + harm) * NODE_DEV
            out_ref[start : start + NODE_DEV] = words[part * NODE_DEV : (part + 1) * NODE_DEV]


def expand_kernel(words_ref, table_ref, out_ref, held_ref, sem):
    harm = lax.axis_index("h")
    copy = pltpu.make_async_copy(table_ref.at[harm], held_ref, sem)
    copy.start()
    nodes = N_HARM * NODE_DEV
    values = decode(words_ref[:nodes], MEAN_NODE)
    for part in range(1, N_REST):
        values += decode(words_ref[part * nodes : (part + 1) * nodes], MEAN_NODE)
    terms = jnp.concatenate(split_terms(values, 2), axis=0)
    copy.wait()
    blocks = lax.dot_general(
        held_ref[...], terms, (((1,), (1,)), ((), ())), preferred_element_type=jnp.float32
    )
    blocks = (blocks[:, :nodes] + blocks[:, nodes:]).reshape(PER, PAD, nodes)
    out_ref[...] = blocks[:, :COEFS].astype(jnp.bfloat16)


def in_hbm(array):
    return pltpu.with_memory_space_constraint(array, pltpu.HBM)


def on_device(stick, stiffness, slip_tangent, contact_force, owner_node, live_pairs):
    pairs = stick.shape[1]
    vmem = pl.BlockSpec(memory_space=pltpu.VMEM)
    hbm = pl.BlockSpec(memory_space=pltpu.HBM)
    params = pltpu.CompilerParams(vmem_limit_bytes=32 * 1024 * 1024)
    slots = pl.pallas_call(
        send_kernel,
        out_shape=jax.ShapeDtypeStruct((SLOTS, LANES), jnp.int32),
        in_specs=[pl.BlockSpec(memory_space=pltpu.SMEM)] + [hbm] * 6,
        out_specs=vmem,
        scratch_shapes=[
            pltpu.VMEM((SAMPLES, pairs), jnp.int32),
            pltpu.VMEM((1, pairs), jnp.float32),
            pltpu.VMEM((SAMPLES, pairs), jnp.float32),
            pltpu.VMEM((SAMPLES, pairs), jnp.float32),
            pltpu.VMEM((2, pairs), jnp.int32),
            pltpu.VMEM((2 * LANES, 2 * SAMPLES), jnp.float32),
            pltpu.SemaphoreType.DMA((6,)),
        ],
        compiler_params=params,
    )(
        live_pairs,
        in_hbm(stick),
        in_hbm(stiffness.reshape(1, pairs)),
        in_hbm(slip_tangent),
        in_hbm(contact_force),
        in_hbm(owner_node),
        in_hbm(jnp.asarray(analysis_table())),
    )
    slots = lax.all_to_all(slots.reshape(N_FIRST, 1, GROUP * LANES), FIRST, 0, 0, tiled=True)
    sums = pl.pallas_call(
        merge_kernel,
        out_shape=jax.ShapeDtypeStruct((N_REST * N_HARM * NODE_DEV, LANES), jnp.int32),
        in_specs=[vmem],
        out_specs=vmem,
        compiler_params=params,
    )(slots.reshape(SLOTS, LANES))
    sums = lax.all_to_all(
        sums.reshape(N_REST * N_HARM, NODE_DEV, LANES), REST + ("h",), 0, 0, tiled=True
    )
    blocks = pl.pallas_call(
        expand_kernel,
        out_shape=jax.ShapeDtypeStruct((PER, COEFS, N_HARM * NODE_DEV), jnp.bfloat16),
        in_specs=[vmem, hbm],
        out_specs=vmem,
        scratch_shapes=[pltpu.VMEM((T_ROWS, 2 * LANES), jnp.bfloat16), pltpu.SemaphoreType.DMA],
        compiler_params=params,
    )(sums.reshape(N_REST * N_HARM * NODE_DEV, LANES), in_hbm(jnp.asarray(synthesis_table())))
    return jnp.transpose(blocks, (1, 0, 2))


def solution(mesh):
    fine = Mesh(mesh.devices.reshape(tuple(SIZES.values())), tuple(SIZES))
    every = ("x", "z", "c", "h")
    return jax.shard_map(
        on_device,
        mesh=fine,
        in_specs=(P(None, every), P(every), P(None, every), P(None, every), P(None, every), P(every)),
        out_specs=P(None, "h", ("x", "z", "c")),
        check_vma=False,
    )
```

```python
import functools
import math

import jax
import jax.numpy as jnp
import numpy as np
from jax import lax
from jax.experimental import pallas as pl
from jax.experimental.pallas import tpu as pltpu
from jax.sharding import Mesh
from jax.sharding import PartitionSpec as P

HARMONICS = 33
COEFS = 2 * HARMONICS + 1
SAMPLES = 256
NODE_DEV = 32
CAP = 3
SIZES = {"x": 4, "z": 16, "c": 2, "h": 4}
FIRST = ("x", "z", "c")
REST = tuple(axis for axis in ("x", "z", "c") if axis not in FIRST)
N_FIRST = math.prod(SIZES[axis] for axis in FIRST)
N_REST = math.prod(SIZES[axis] for axis in REST)
N_HARM = SIZES["h"]
GROUP = N_REST * CAP
SLOTS = N_FIRST * GROUP

LANES = 128
W_LANES = 72
F_LOW = 34
MEAN, EXP_W, EXP_F, NODE = 112, 113, 114, 115
STEPS = 16.0
TOP = 32766.0
MEAN_PAIR = 2.0**21
MEAN_NODE = 2.0**31 / (1024.0 * CAP * N_FIRST)
PER = (COEFS + 1) // N_HARM
PAD = 72
T_ROWS = PER * PAD


def analysis_table():
    k = np.arange(HARMONICS * 2 + 1)[:, None]
    angle = (k * np.arange(SAMPLES)[None, :] % SAMPLES) * (2.0 * np.pi / SAMPLES)
    cosine, sine = np.cos(angle), np.sin(angle)
    basis = np.zeros((COEFS, SAMPLES))
    basis[0] = 1.0
    basis[1::2] = cosine[1 : HARMONICS + 1]
    basis[2::2] = sine[1 : HARMONICS + 1]
    table = np.zeros((2 * LANES, 2 * SAMPLES))
    top = 2 * HARMONICS
    table[:top, :SAMPLES] = cosine[1:]
    table[LANES : LANES + top, :SAMPLES] = sine[1:]
    table[MEAN, :SAMPLES] = 1.0
    table[W_LANES : W_LANES + F_LOW, SAMPLES:] = basis[:F_LOW]
    table[LANES + W_LANES : LANES + W_LANES + COEFS - F_LOW, SAMPLES:] = basis[F_LOW:]
    return table.astype(np.float32)


def synthesis_table():
    table = np.zeros((N_HARM, PER, PAD, 2 * LANES), np.float32)

    def add(row, kind, k, value):
        if kind == "s":
            if k == 0:
                return
            row[LANES + abs(k) - 1] += value if k > 0 else -value
        elif k == 0:
            row[MEAN] += value
        else:
            row[abs(k) - 1] += value

    for i in range(COEFS):
        a, i_sine = (i + 1) // 2, i > 0 and i % 2 == 0
        for j in range(COEFS + 1):
            row = table[j // PER, j % PER, i]
            if j == COEFS:
                lane = W_LANES + i if i < F_LOW else LANES + W_LANES + i - F_LOW
                row[lane] = 1.0 / math.sqrt(SAMPLES)
                continue
            b, j_sine = (j + 1) // 2, j > 0 and j % 2 == 0
            half = 1.0 / SAMPLES
            if i_sine and j_sine:
                add(row, "c", a - b, half)
                add(row, "c", a + b, -half)
            elif not i_sine and not j_sine:
                add(row, "c", a - b, half)
                add(row, "c", a + b, half)
            elif i_sine:
                add(row, "s", a + b, half)
                add(row, "s", a - b, half)
            else:
                add(row, "s", a + b, half)
                add(row, "s", b - a, half)
    return table.reshape(N_HARM, T_ROWS, 2 * LANES).astype(jnp.bfloat16)


def index_along(axes, part):
    index = 0
    for axis in axes:
        index = index * SIZES[axis] + part[axis]
    return index


def scale_step(largest):
    return jnp.ceil(jnp.log2(jnp.maximum(largest, 1e-30)) * STEPS + 0.01)


def send_kernel(
    live_ref, stick_hbm, stiff_hbm, slip_hbm, force_hbm, owner_hbm, table_hbm, out_ref,
    stick_ref, stiff_ref, slip_ref, force_ref, owner_ref, table_ref, sems,
):
    copies = [
        pltpu.make_async_copy(source, held, sems.at[n])
        for n, (source, held) in enumerate(
            (
                (owner_hbm, owner_ref),
                (stiff_hbm, stiff_ref),
                (stick_hbm, stick_ref),
                (slip_hbm, slip_ref),
                (force_hbm, force_ref),
                (table_hbm, table_ref),
            )
        )
    ]
    for copy in copies:
        copy.start()
    pairs = stick_ref.shape[1]
    copies[0].wait()
    owner = owner_ref[...]
    local = owner & (NODE_DEV - 1)
    target = owner // (N_HARM * NODE_DEV)
    first, second = target[0:1], target[1:2]
    square = (pairs, pairs)
    row_first = jnp.broadcast_to(first, square)
    row_second = jnp.broadcast_to(second, square)
    column_first = row_first.T
    column_second = row_second.T
    before = lax.broadcasted_iota(jnp.int32, square, 0) < lax.broadcasted_iota(jnp.int32, square, 1)
    count_first = jnp.where(before & (column_first == row_first), 1, 0)
    count_second = jnp.where(column_first == row_second, 1, 0) + jnp.where(
        before & (column_second == row_second), 1, 0
    )
    place_first = jnp.sum(count_first, axis=0, keepdims=True)
    place_second = jnp.sum(count_second, axis=0, keepdims=True)

    def slot_of(dest, place):
        part = {
            "x": dest // (SIZES["z"] * SIZES["c"]),
            "z": dest // SIZES["c"] % SIZES["z"],
            "c": dest % SIZES["c"],
        }
        return index_along(FIRST, part) * GROUP + index_along(REST, part) * CAP + place

    slot = lax.broadcasted_iota(jnp.int32, (SLOTS, pairs), 0)
    hit_first = slot == slot_of(first, place_first)
    hit_second = slot == slot_of(second, place_second)
    node = jnp.where(hit_first, local[0:1] + 1, 0) + jnp.where(hit_second, local[1:2] + 1, 0)
    node = jnp.sum(node, axis=1, keepdims=True) - 1
    pick = jnp.where(hit_first | hit_second, 1.0, 0.0).astype(jnp.bfloat16)
    for copy in copies[1:]:
        copy.wait()
    live = (lax.broadcasted_iota(jnp.int32, (1, pairs), 1) < live_ref[0]).astype(jnp.float32)
    stick = stick_ref[...].astype(jnp.float32)
    weights = (stiff_ref[...] * live) * (stick + (1.0 - stick) * slip_ref[...])
    forces = force_ref[...] * live
    sums = jnp.dot(
        table_ref[...],
        jnp.concatenate([weights, forces], axis=0),
        precision=lax.Precision.HIGHEST,
        preferred_element_type=jnp.float32,
    )
    low, high = sums[:LANES], sums[LANES:]
    size = jnp.maximum(jnp.abs(low), jnp.abs(high))
    step_w = scale_step(jnp.max(size[:W_LANES], axis=0, keepdims=True))
    step_f = scale_step(jnp.max(size[W_LANES:MEAN], axis=0, keepdims=True))
    lane = lax.broadcasted_iota(jnp.int32, (LANES, pairs), 0)
    factor = jnp.where(
        lane < W_LANES, jnp.exp2(step_w * (-1.0 / STEPS)) * TOP, jnp.exp2(step_f * (-1.0 / STEPS)) * TOP
    )
    mean = jnp.round(sums[MEAN : MEAN + 1] * MEAN_PAIR).astype(jnp.int32)
    low = jnp.round(low * jnp.where(lane < MEAN, factor, 0.0)).astype(jnp.int32)
    low = jnp.where(lane == MEAN, ((mean & 0xFFFF) ^ 0x8000) - 0x8000, low)
    low = jnp.where(lane == EXP_W, step_w.astype(jnp.int32), low)
    low = jnp.where(lane == EXP_F, step_f.astype(jnp.int32), low)
    high = jnp.round(high * jnp.where(lane < MEAN, factor, 0.0)).astype(jnp.int32)
    high = jnp.where(lane == MEAN, mean >> 16, high)
    both = jnp.concatenate([low, high], axis=0)
    digits = jnp.concatenate([both >> 8, both & 255], axis=0).astype(jnp.float32).astype(jnp.bfloat16)
    sent = lax.dot_general(
        pick, digits, (((1,), (1,)), ((), ())), preferred_element_type=jnp.float32
    )
    value_low = (sent[:, :LANES] * 256.0 + sent[:, 2 * LANES : 3 * LANES]).astype(jnp.int32)
    value_high = (sent[:, LANES : 2 * LANES] * 256.0 + sent[:, 3 * LANES :]).astype(jnp.int32)
    words = (value_high << 16) | (value_low & 0xFFFF)
    word_lane = lax.broadcasted_iota(jnp.int32, (SLOTS, LANES), 1)
    out_ref[...] = jnp.where(word_lane == NODE, node, words)


def decode(words, mean_unit):
    lane = lax.broadcasted_iota(jnp.int32, words.shape, words.ndim - 1)
    low = ((words & 0xFFFF) ^ 0x8000) - 0x8000
    high = words >> 16
    step = jnp.where(
        lane < W_LANES, ((words[:, EXP_W : EXP_W + 1] & 0xFFFF) ^ 0x8000) - 0x8000,
        ((words[:, EXP_F : EXP_F + 1] & 0xFFFF) ^ 0x8000) - 0x8000,
    )
    scale = jnp.exp2(step.astype(jnp.float32) * (1.0 / STEPS)) * (1.0 / TOP)
    scale = jnp.where(lane < MEAN, scale, jnp.where(lane == MEAN, 1.0 / mean_unit, 0.0))
    low = jnp.where(lane == MEAN, words, low).astype(jnp.float32) * scale
    high = high.astype(jnp.float32) * jnp.where(lane < MEAN, scale, 0.0)
    return jnp.concatenate([low, high], axis=1)


def split_terms(values, count):
    terms = []
    for _ in range(count):
        term = values.astype(jnp.bfloat16)
        terms.append(term)
        values = values - term.astype(jnp.float32)
    return terms


def merge_kernel(words_ref, out_ref):
    words = words_ref[...]
    values = decode(words, MEAN_PAIR)
    rows = N_REST * NODE_DEV
    place = lax.broadcasted_iota(jnp.int32, (SLOTS, 1), 0) % GROUP // CAP
    node = words[:, NODE : NODE + 1]
    node = jnp.where(node >= 0, node + place * NODE_DEV, -1)
    owner = lax.broadcasted_iota(jnp.int32, (SLOTS, rows), 1) == node
    owner = jnp.where(owner, 1.0, 0.0).astype(jnp.bfloat16)
    terms = jnp.concatenate(split_terms(values, 3), axis=1)
    total = lax.dot_general(
        owner, terms, (((0,), (0,)), ((), ())), preferred_element_type=jnp.float32
    )
    low = total[:, :LANES] + (total[:, 2 * LANES : 3 * LANES] + total[:, 4 * LANES : 5 * LANES])
    high = total[:, LANES : 2 * LANES] + (total[:, 3 * LANES : 4 * LANES] + total[:, 5 * LANES :])
    size = jnp.maximum(jnp.abs(low), jnp.abs(high))
    lane = lax.broadcasted_iota(jnp.int32, size.shape, 1)
    step_w = scale_step(jnp.max(jnp.where(lane < W_LANES, size, 0.0), axis=1, keepdims=True))
    step_f = scale_step(
        jnp.max(jnp.where((lane >= W_LANES) & (lane < MEAN), size, 0.0), axis=1, keepdims=True)
    )
    factor = jnp.exp2(jnp.where(lane < W_LANES, step_w, step_f) * (-1.0 / STEPS)) * TOP
    factor = jnp.where(lane < MEAN, factor, 0.0)
    words = (jnp.round(high * factor).astype(jnp.int32) << 16) | (
        jnp.round(low * factor).astype(jnp.int32) & 0xFFFF
    )
    words = jnp.where(lane == MEAN, jnp.round(low * MEAN_NODE).astype(jnp.int32), words)
    words = jnp.where(lane == EXP_W, step_w.astype(jnp.int32), words)
    words = jnp.where(lane == EXP_F, step_f.astype(jnp.int32), words)
    for part in range(N_REST):
        for harm in range(N_HARM):
            start = (part * N_HARM + harm) * NODE_DEV
            out_ref[start : start + NODE_DEV] = words[part * NODE_DEV : (part + 1) * NODE_DEV]


def expand_kernel(words_ref, table_ref, out_ref, held_ref, sem):
    harm = lax.axis_index("h")
    copy = pltpu.make_async_copy(table_ref.at[harm], held_ref, sem)
    copy.start()
    nodes = N_HARM * NODE_DEV
    values = decode(words_ref[:nodes], MEAN_NODE)
    for part in range(1, N_REST):
        values += decode(words_ref[part * nodes : (part + 1) * nodes], MEAN_NODE)
    terms = jnp.concatenate(split_terms(values, 2), axis=0)
    copy.wait()
    blocks = lax.dot_general(
        held_ref[...], terms, (((1,), (1,)), ((), ())), preferred_element_type=jnp.float32
    )
    blocks = (blocks[:, :nodes] + blocks[:, nodes:]).reshape(PER, PAD, nodes)
    out_ref[...] = blocks[:, :COEFS].astype(jnp.bfloat16)


def in_hbm(array):
    return pltpu.with_memory_space_constraint(array, pltpu.HBM)


def on_device(stick, stiffness, slip_tangent, contact_force, owner_node, live_pairs):
    pairs = stick.shape[1]
    vmem = pl.BlockSpec(memory_space=pltpu.VMEM)
    hbm = pl.BlockSpec(memory_space=pltpu.HBM)
    params = pltpu.CompilerParams(vmem_limit_bytes=32 * 1024 * 1024)
    slots = pl.pallas_call(
        send_kernel,
        out_shape=jax.ShapeDtypeStruct((SLOTS, LANES), jnp.int32),
        in_specs=[pl.BlockSpec(memory_space=pltpu.SMEM)] + [hbm] * 6,
        out_specs=vmem,
        scratch_shapes=[
            pltpu.VMEM((SAMPLES, pairs), jnp.int32),
            pltpu.VMEM((1, pairs), jnp.float32),
            pltpu.VMEM((SAMPLES, pairs), jnp.float32),
            pltpu.VMEM((SAMPLES, pairs), jnp.float32),
            pltpu.VMEM((2, pairs), jnp.int32),
            pltpu.VMEM((2 * LANES, 2 * SAMPLES), jnp.float32),
            pltpu.SemaphoreType.DMA((6,)),
        ],
        compiler_params=params,
    )(
        live_pairs,
        in_hbm(stick),
        in_hbm(stiffness.reshape(1, pairs)),
        in_hbm(slip_tangent),
        in_hbm(contact_force),
        in_hbm(owner_node),
        in_hbm(jnp.asarray(analysis_table())),
    )
    slots = lax.all_to_all(slots.reshape(N_FIRST, 1, GROUP * LANES), FIRST, 0, 0, tiled=True)
    sums = pl.pallas_call(
        merge_kernel,
        out_shape=jax.ShapeDtypeStruct((N_REST * N_HARM * NODE_DEV, LANES), jnp.int32),
        in_specs=[vmem],
        out_specs=vmem,
        compiler_params=params,
    )(slots.reshape(SLOTS, LANES))
    sums = lax.all_to_all(
        sums.reshape(N_REST * N_HARM, NODE_DEV, LANES), REST + ("h",), 0, 0, tiled=True
    )
    blocks = pl.pallas_call(
        expand_kernel,
        out_shape=jax.ShapeDtypeStruct((PER, COEFS, N_HARM * NODE_DEV), jnp.bfloat16),
        in_specs=[vmem, hbm],
        out_specs=vmem,
        scratch_shapes=[pltpu.VMEM((T_ROWS, 2 * LANES), jnp.bfloat16), pltpu.SemaphoreType.DMA],
        compiler_params=params,
    )(sums.reshape(N_REST * N_HARM * NODE_DEV, LANES), in_hbm(jnp.asarray(synthesis_table())))
    return jnp.transpose(blocks, (1, 0, 2))


def solution(mesh):
    fine = Mesh(mesh.devices.reshape(tuple(SIZES.values())), tuple(SIZES))
    every = ("x", "z", "c", "h")
    return jax.shard_map(
        on_device,
        mesh=fine,
        in_specs=(P(None, every), P(every), P(None, every), P(None, every), P(None, every), P(every)),
        out_specs=P(None, "h", ("x", "z", "c")),
        check_vma=False,
    )
```

```python
import math

import jax
import jax.numpy as jnp
import numpy as np
from jax import lax
from jax.experimental import pallas as pl
from jax.experimental.pallas import tpu as pltpu
from jax.sharding import Mesh
from jax.sharding import PartitionSpec as P

HARMONICS = 33
COEFS = 2 * HARMONICS + 1
SAMPLES = 256
NODE_DEV = 32
CAP = 3
SIZES = {"x": 4, "z": 16, "c": 2, "h": 4}
FIRST = ("x", "z")
REST = tuple(axis for axis in ("x", "z", "c") if axis not in FIRST)
N_FIRST = math.prod(SIZES[axis] for axis in FIRST)
N_REST = math.prod(SIZES[axis] for axis in REST)
N_HARM = SIZES["h"]
GROUP = N_REST * CAP
SLOTS = N_FIRST * GROUP

LANES = 128
W_LANES = 66
F_LOW = 34
MEAN, EXP_W, EXP_F, NODE = 100, 101, 102, 103
RECORD = 104
F_START = 64
ROWS = GROUP - 1
FREE = LANES - RECORD
W_HIGH = 72
STEPS = 16.0
TOP = 32766.0
MEAN_PAIR = 2.0**21
MEAN_NODE = 2.0**31 / (1024.0 * CAP * N_FIRST)
PER = (COEFS + 1) // N_HARM
PAD = 72
T_ROWS = PER * PAD


def analysis_table():
    k = np.arange(HARMONICS * 2 + 1)[:, None]
    angle = (k * np.arange(SAMPLES)[None, :] % SAMPLES) * (2.0 * np.pi / SAMPLES)
    cosine, sine = np.cos(angle), np.sin(angle)
    basis = np.zeros((COEFS, SAMPLES))
    basis[0] = 1.0
    basis[1::2] = cosine[1 : HARMONICS + 1]
    basis[2::2] = sine[1 : HARMONICS + 1]
    w_low = np.zeros((RECORD, SAMPLES))
    w_low[:W_LANES] = cosine[1:]
    w_low[MEAN] = 1.0
    w_high = np.zeros((W_HIGH, SAMPLES))
    w_high[:W_LANES] = sine[1:]
    f_low = np.zeros((RECORD - F_START, SAMPLES))
    f_low[W_LANES - F_START : MEAN - F_START] = basis[:F_LOW]
    f_high = np.zeros_like(f_low)
    f_high[W_LANES - F_START : W_LANES - F_START + COEFS - F_LOW] = basis[F_LOW:]
    table = np.concatenate([w_low, w_high, f_low, f_high], axis=0)
    first = table.astype(jnp.bfloat16)
    second = (table - first.astype(np.float64)).astype(jnp.bfloat16)
    return np.concatenate([first, second], axis=0)


def synthesis_table():
    table = np.zeros((N_HARM, PER, PAD, 2 * LANES), np.float32)

    def add(row, kind, k, value):
        if kind == "s":
            if k == 0:
                return
            row[LANES + abs(k) - 1] += value if k > 0 else -value
        elif k == 0:
            row[MEAN] += value
        else:
            row[abs(k) - 1] += value

    for i in range(COEFS):
        a, i_sine = (i + 1) // 2, i > 0 and i % 2 == 0
        for j in range(COEFS + 1):
            row = table[j // PER, j % PER, i]
            if j == COEFS:
                lane = W_LANES + i if i < F_LOW else LANES + W_LANES + i - F_LOW
                row[lane] = 1.0 / math.sqrt(SAMPLES)
                continue
            b, j_sine = (j + 1) // 2, j > 0 and j % 2 == 0
            half = 1.0 / SAMPLES
            if i_sine and j_sine:
                add(row, "c", a - b, half)
                add(row, "c", a + b, -half)
            elif not i_sine and not j_sine:
                add(row, "c", a - b, half)
                add(row, "c", a + b, half)
            elif i_sine:
                add(row, "s", a + b, half)
                add(row, "s", a - b, half)
            else:
                add(row, "s", a + b, half)
                add(row, "s", b - a, half)
    return table.reshape(N_HARM, T_ROWS, 2 * LANES).astype(jnp.bfloat16)


def index_along(axes, part):
    index = 0
    for axis in axes:
        index = index * SIZES[axis] + part[axis]
    return index


def scale_step(largest):
    return jnp.ceil(jnp.log2(jnp.maximum(largest, 1e-30)) * STEPS + 0.01)


def transform(table_ref, start, stop, samples):
    total = table_ref.shape[0] // 2
    first, second = split_terms(samples, 2)
    large = jnp.dot(
        table_ref[start:stop],
        jnp.concatenate([first, second], axis=1),
        preferred_element_type=jnp.float32,
    )
    small = jnp.dot(
        table_ref[total + start : total + stop], first, preferred_element_type=jnp.float32
    )
    pairs = samples.shape[1]
    return large[:, :pairs] + (large[:, pairs:] + small)


def send_kernel(
    live_ref, stick_hbm, stiff_hbm, slip_hbm, force_hbm, owner_hbm, table_hbm, synthesis_hbm,
    out_ref, synthesis_ref,
    stick_ref, stiff_ref, slip_ref, force_ref, owner_ref, table_ref, sems,
):
    copies = [
        pltpu.make_async_copy(source, held, sems.at[n])
        for n, (source, held) in enumerate(
            (
                (owner_hbm, owner_ref),
                (stiff_hbm, stiff_ref),
                (stick_hbm, stick_ref),
                (slip_hbm, slip_ref),
                (table_hbm, table_ref),
                (force_hbm, force_ref),
                (synthesis_hbm.at[lax.axis_index("h")], synthesis_ref),
            )
        )
    ]
    for copy in copies:
        copy.start()
    pairs = stick_ref.shape[1]
    copies[0].wait()
    owner = owner_ref[...]
    local = owner & (NODE_DEV - 1)
    target = owner // (N_HARM * NODE_DEV)
    first, second = target[0:1], target[1:2]
    square = (pairs, pairs)
    row_first = jnp.broadcast_to(first, square)
    row_second = jnp.broadcast_to(second, square)
    column_first = row_first.T
    column_second = row_second.T
    before = lax.broadcasted_iota(jnp.int32, square, 0) < lax.broadcasted_iota(jnp.int32, square, 1)
    count_first = jnp.where(before & (column_first == row_first), 1, 0)
    count_second = jnp.where(column_first == row_second, 1, 0) + jnp.where(
        before & (column_second == row_second), 1, 0
    )
    place_first = jnp.sum(count_first, axis=0, keepdims=True)
    place_second = jnp.sum(count_second, axis=0, keepdims=True)

    def slot_of(dest, place):
        part = {
            "x": dest // (SIZES["z"] * SIZES["c"]),
            "z": dest // SIZES["c"] % SIZES["z"],
            "c": dest % SIZES["c"],
        }
        return (index_along(REST, part) * CAP + place) * N_FIRST + index_along(FIRST, part)

    slot = lax.broadcasted_iota(jnp.int32, (SLOTS, pairs), 0)
    hit_first = slot == slot_of(first, place_first)
    hit_second = slot == slot_of(second, place_second)
    node = jnp.where(hit_first, local[0:1] + 1, 0) + jnp.where(hit_second, local[1:2] + 1, 0)
    node = jnp.sum(node, axis=1, keepdims=True) - 1
    pick = jnp.where(hit_first | hit_second, 1.0, 0.0).astype(jnp.bfloat16)
    for copy in copies[1:-2]:
        copy.wait()
    live = (lax.broadcasted_iota(jnp.int32, (1, pairs), 1) < live_ref[0]).astype(jnp.float32)
    stick = stick_ref[...].astype(jnp.float32)
    weights = (stiff_ref[...] * live) * (stick + (1.0 - stick) * slip_ref[...])
    w_rows = RECORD + W_HIGH
    w_sums = transform(table_ref, 0, w_rows, weights)
    copies[-2].wait()
    forces = force_ref[...] * live
    f_rows = RECORD - F_START
    f_sums = transform(table_ref, w_rows, w_rows + 2 * f_rows, forces)

    def rows(count):
        return jnp.zeros((count, pairs), jnp.float32)

    low = w_sums[:RECORD] + jnp.concatenate([rows(F_START), f_sums[:f_rows]], axis=0)
    high = jnp.concatenate([w_sums[RECORD:], rows(RECORD - W_HIGH)], axis=0) + jnp.concatenate(
        [rows(F_START), f_sums[f_rows:]], axis=0
    )
    lane = lax.broadcasted_iota(jnp.int32, (RECORD, pairs), 0)
    is_w, is_value = lane < W_LANES, lane < MEAN
    size = jnp.maximum(jnp.abs(low), jnp.abs(high))
    step_w = scale_step(jnp.max(jnp.where(is_w, size, 0.0), axis=0, keepdims=True))
    step_f = scale_step(jnp.max(jnp.where(is_value & ~is_w, size, 0.0), axis=0, keepdims=True))
    factor = jnp.where(
        is_w, jnp.exp2(step_w * (-1.0 / STEPS)) * TOP, jnp.exp2(step_f * (-1.0 / STEPS)) * TOP
    )
    factor = jnp.where(is_value, factor, 0.0)
    mean = jnp.round(low[MEAN : MEAN + 1] * MEAN_PAIR).astype(jnp.int32)
    low = jnp.round(low * factor).astype(jnp.int32)
    low = jnp.where(lane == MEAN, ((mean & 0xFFFF) ^ 0x8000) - 0x8000, low)
    low = jnp.where(lane == EXP_W, step_w.astype(jnp.int32), low)
    low = jnp.where(lane == EXP_F, step_f.astype(jnp.int32), low)
    high = jnp.round(high * factor).astype(jnp.int32)
    high = jnp.where(lane == MEAN, mean >> 16, high)
    free = jnp.zeros((FREE, pairs), jnp.int32)
    both = jnp.concatenate([low, free, high, free], axis=0)
    digits = jnp.concatenate([both >> 8, both & 255], axis=0).astype(jnp.float32).astype(jnp.bfloat16)
    sent = lax.dot_general(
        pick, digits, (((1,), (1,)), ((), ())), preferred_element_type=jnp.float32
    )
    value_low = (sent[:, :LANES] * 256.0 + sent[:, 2 * LANES : 3 * LANES]).astype(jnp.int32)
    value_high = (sent[:, LANES : 2 * LANES] * 256.0 + sent[:, 3 * LANES :]).astype(jnp.int32)
    words = (value_high << 16) | (value_low & 0xFFFF)
    words = jnp.where(lax.broadcasted_iota(jnp.int32, (SLOTS, LANES), 1) == NODE, node, words)
    last = words[ROWS * N_FIRST :]
    own = lax.broadcasted_iota(jnp.int32, (N_FIRST, LANES), 1) < RECORD
    for k in range(ROWS):
        spread = pltpu.roll(last, RECORD - FREE * k, 1)
        out_ref[pl.ds(k, N_FIRST, stride=ROWS), :] = jnp.where(
            own, words[k * N_FIRST : (k + 1) * N_FIRST], spread
        )
    copies[-1].wait()


def decode(words, mean_unit):
    lane = lax.broadcasted_iota(jnp.int32, words.shape, words.ndim - 1)
    low = ((words & 0xFFFF) ^ 0x8000) - 0x8000
    high = words >> 16
    step = jnp.where(
        lane < W_LANES, ((words[:, EXP_W : EXP_W + 1] & 0xFFFF) ^ 0x8000) - 0x8000,
        ((words[:, EXP_F : EXP_F + 1] & 0xFFFF) ^ 0x8000) - 0x8000,
    )
    scale = jnp.exp2(step.astype(jnp.float32) * (1.0 / STEPS)) * (1.0 / TOP)
    scale = jnp.where(lane < MEAN, scale, jnp.where(lane == MEAN, 1.0 / mean_unit, 0.0))
    low = jnp.where(lane == MEAN, words, low).astype(jnp.float32) * scale
    high = high.astype(jnp.float32) * jnp.where(lane < MEAN, scale, 0.0)
    return jnp.concatenate([low, high], axis=1)


def split_terms(values, count):
    terms = []
    for _ in range(count):
        term = values.astype(jnp.bfloat16)
        terms.append(term)
        values = values - term.astype(jnp.float32)
    return terms


def merge_kernel(words_ref, out_ref):
    lane = lax.broadcasted_iota(jnp.int32, (N_FIRST, LANES), 1)
    records = [words_ref[pl.ds(k, N_FIRST, stride=ROWS), :] for k in range(ROWS)]
    last = pltpu.roll(records[0], FREE, 1)
    for k in range(1, ROWS):
        last = jnp.where(lane < FREE * k, last, pltpu.roll(records[k], FREE * (k + 1), 1))
    words = jnp.concatenate(records + [last], axis=0)
    values = decode(words, MEAN_PAIR)
    rows = N_REST * NODE_DEV
    place = lax.broadcasted_iota(jnp.int32, (SLOTS, 1), 0) // (CAP * N_FIRST)
    node = words[:, NODE : NODE + 1]
    node = jnp.where(node >= 0, node + place * NODE_DEV, -1)
    owner = lax.broadcasted_iota(jnp.int32, (SLOTS, rows), 1) == node
    owner = jnp.where(owner, 1.0, 0.0).astype(jnp.bfloat16)
    terms = jnp.concatenate(split_terms(values, 3), axis=1)
    total = lax.dot_general(
        owner, terms, (((0,), (0,)), ((), ())), preferred_element_type=jnp.float32
    )
    low = total[:, :LANES] + (total[:, 2 * LANES : 3 * LANES] + total[:, 4 * LANES : 5 * LANES])
    high = total[:, LANES : 2 * LANES] + (total[:, 3 * LANES : 4 * LANES] + total[:, 5 * LANES :])
    size = jnp.maximum(jnp.abs(low), jnp.abs(high))
    lane = lax.broadcasted_iota(jnp.int32, size.shape, 1)
    step_w = scale_step(jnp.max(jnp.where(lane < W_LANES, size, 0.0), axis=1, keepdims=True))
    step_f = scale_step(
        jnp.max(jnp.where((lane >= W_LANES) & (lane < MEAN), size, 0.0), axis=1, keepdims=True)
    )
    factor = jnp.exp2(jnp.where(lane < W_LANES, step_w, step_f) * (-1.0 / STEPS)) * TOP
    factor = jnp.where(lane < MEAN, factor, 0.0)
    words = (jnp.round(high * factor).astype(jnp.int32) << 16) | (
        jnp.round(low * factor).astype(jnp.int32) & 0xFFFF
    )
    words = jnp.where(lane == MEAN, jnp.round(low * MEAN_NODE).astype(jnp.int32), words)
    words = jnp.where(lane == EXP_W, step_w.astype(jnp.int32), words)
    words = jnp.where(lane == EXP_F, step_f.astype(jnp.int32), words)
    for part in range(N_REST):
        for harm in range(N_HARM):
            start = (part * N_HARM + harm) * NODE_DEV
            out_ref[start : start + NODE_DEV] = words[part * NODE_DEV : (part + 1) * NODE_DEV]


def expand_kernel(words_ref, table_ref, out_ref):
    nodes = N_HARM * NODE_DEV
    values = decode(words_ref[:nodes], MEAN_NODE)
    for part in range(1, N_REST):
        values += decode(words_ref[part * nodes : (part + 1) * nodes], MEAN_NODE)
    terms = jnp.concatenate(split_terms(values, 2), axis=0)
    blocks = lax.dot_general(
        table_ref[...], terms, (((1,), (1,)), ((), ())), preferred_element_type=jnp.float32
    )
    blocks = (blocks[:, :nodes] + blocks[:, nodes:]).reshape(PER, PAD, nodes)
    out_ref[...] = blocks[:, :COEFS].astype(jnp.bfloat16)


def in_hbm(array):
    return pltpu.with_memory_space_constraint(array, pltpu.HBM)


def on_device(stick, stiffness, slip_tangent, contact_force, owner_node, live_pairs):
    pairs = stick.shape[1]
    vmem = pl.BlockSpec(memory_space=pltpu.VMEM)
    hbm = pl.BlockSpec(memory_space=pltpu.HBM)
    params = pltpu.CompilerParams(vmem_limit_bytes=32 * 1024 * 1024)
    analysis = analysis_table()
    slots, synthesis = pl.pallas_call(
        send_kernel,
        out_shape=(
            jax.ShapeDtypeStruct((ROWS * N_FIRST, LANES), jnp.int32),
            jax.ShapeDtypeStruct((T_ROWS, 2 * LANES), jnp.bfloat16),
        ),
        in_specs=[pl.BlockSpec(memory_space=pltpu.SMEM)] + [hbm] * 7,
        out_specs=(vmem, vmem),
        scratch_shapes=[
            pltpu.VMEM((SAMPLES, pairs), jnp.int32),
            pltpu.VMEM((1, pairs), jnp.float32),
            pltpu.VMEM((SAMPLES, pairs), jnp.float32),
            pltpu.VMEM((SAMPLES, pairs), jnp.float32),
            pltpu.VMEM((2, pairs), jnp.int32),
            pltpu.VMEM(analysis.shape, jnp.bfloat16),
            pltpu.SemaphoreType.DMA((7,)),
        ],
        compiler_params=params,
    )(
        live_pairs,
        in_hbm(stick),
        in_hbm(stiffness.reshape(1, pairs)),
        in_hbm(slip_tangent),
        in_hbm(contact_force),
        in_hbm(owner_node),
        in_hbm(jnp.asarray(analysis)),
        in_hbm(jnp.asarray(synthesis_table())),
    )
    slots = lax.all_to_all(slots.reshape(N_FIRST, 1, ROWS * LANES), FIRST, 0, 0, tiled=True)
    sums = pl.pallas_call(
        merge_kernel,
        out_shape=jax.ShapeDtypeStruct((N_REST * N_HARM * NODE_DEV, LANES), jnp.int32),
        in_specs=[vmem],
        out_specs=vmem,
        compiler_params=params,
    )(slots.reshape(ROWS * N_FIRST, LANES))
    sums = lax.all_to_all(
        sums.reshape(N_REST * N_HARM, NODE_DEV, LANES), REST + ("h",), 0, 0, tiled=True
    )
    blocks = pl.pallas_call(
        expand_kernel,
        out_shape=jax.ShapeDtypeStruct((PER, COEFS, N_HARM * NODE_DEV), jnp.bfloat16),
        in_specs=[vmem, vmem],
        out_specs=vmem,
        compiler_params=params,
    )(sums.reshape(N_REST * N_HARM * NODE_DEV, LANES), synthesis)
    return jnp.transpose(blocks, (1, 0, 2))


def solution(mesh):
    fine = Mesh(mesh.devices.reshape(tuple(SIZES.values())), tuple(SIZES))
    every = ("x", "z", "c", "h")
    return jax.shard_map(
        on_device,
        mesh=fine,
        in_specs=(P(None, every), P(every), P(None, every), P(None, every), P(None, every), P(every)),
        out_specs=P(None, "h", ("x", "z", "c")),
        check_vma=False,
    )
```

```python
import math

import jax
import jax.numpy as jnp
import numpy as np
from jax import lax
from jax.experimental import pallas as pl
from jax.experimental.pallas import tpu as pltpu
from jax.sharding import Mesh
from jax.sharding import PartitionSpec as P

HARMONICS = 33
COEFS = 2 * HARMONICS + 1
SAMPLES = 256
NODE_DEV = 32
CAP = 3
N_X, N_Z, N_REST, N_HARM = 4, 16, 2, 4
N_FIRST = N_X * N_Z
Z_STEP = 9
PEERS = [x * N_Z + place * Z_STEP % N_Z for place in range(N_Z) for x in range(N_X)]
GROUP = N_REST * CAP
SLOTS = N_FIRST * GROUP

LANES = 128
W_LANES = 66
F_LOW = 34
MEAN, EXP_W, EXP_F, NODE = 100, 101, 102, 103
RECORD = 104
F_START = 64
ROWS = GROUP - 1
FREE = LANES - RECORD
W_HIGH = 72
STEPS = 16.0
TOP = 32766.0
MEAN_PAIR = 2.0**21
MEAN_NODE = 2.0**31 / (1024.0 * CAP * N_FIRST)
PER = (COEFS + 1) // N_HARM
PAD = 72
T_ROWS = PER * PAD


def analysis_table():
    k = np.arange(HARMONICS * 2 + 1)[:, None]
    angle = (k * np.arange(SAMPLES)[None, :] % SAMPLES) * (2.0 * np.pi / SAMPLES)
    cosine, sine = np.cos(angle), np.sin(angle)
    basis = np.zeros((COEFS, SAMPLES))
    basis[0] = 1.0
    basis[1::2] = cosine[1 : HARMONICS + 1]
    basis[2::2] = sine[1 : HARMONICS + 1]
    w_low = np.zeros((RECORD, SAMPLES))
    w_low[:W_LANES] = cosine[1:]
    w_low[MEAN] = 1.0
    w_high = np.zeros((W_HIGH, SAMPLES))
    w_high[:W_LANES] = sine[1:]
    f_low = np.zeros((RECORD - F_START, SAMPLES))
    f_low[W_LANES - F_START : MEAN - F_START] = basis[:F_LOW]
    f_high = np.zeros_like(f_low)
    f_high[W_LANES - F_START : W_LANES - F_START + COEFS - F_LOW] = basis[F_LOW:]
    table = np.concatenate([w_low, w_high, f_low, f_high], axis=0)
    first = table.astype(jnp.bfloat16)
    second = (table - first.astype(np.float64)).astype(jnp.bfloat16)
    return np.concatenate([first, second], axis=0)


def synthesis_table():
    table = np.zeros((N_HARM, PER, PAD, 2 * LANES), np.float32)

    def add(row, kind, k, value):
        if kind == "s":
            if k == 0:
                return
            row[LANES + abs(k) - 1] += value if k > 0 else -value
        elif k == 0:
            row[MEAN] += value
        else:
            row[abs(k) - 1] += value

    for i in range(COEFS):
        a, i_sine = (i + 1) // 2, i > 0 and i % 2 == 0
        for j in range(COEFS + 1):
            row = table[j // PER, j % PER, i]
            if j == COEFS:
                lane = W_LANES + i if i < F_LOW else LANES + W_LANES + i - F_LOW
                row[lane] = 1.0 / math.sqrt(SAMPLES)
                continue
            b, j_sine = (j + 1) // 2, j > 0 and j % 2 == 0
            half = 1.0 / SAMPLES
            if i_sine and j_sine:
                add(row, "c", a - b, half)
                add(row, "c", a + b, -half)
            elif not i_sine and not j_sine:
                add(row, "c", a - b, half)
                add(row, "c", a + b, half)
            elif i_sine:
                add(row, "s", a + b, half)
                add(row, "s", a - b, half)
            else:
                add(row, "s", a + b, half)
                add(row, "s", b - a, half)
    return table.reshape(N_HARM, T_ROWS, 2 * LANES).astype(jnp.bfloat16)


def scale_step(largest):
    return jnp.ceil(jnp.log2(jnp.maximum(largest, 1e-30)) * STEPS + 0.01)


def transform(table_ref, start, stop, samples):
    total = table_ref.shape[0] // 2
    first, second = split_terms(samples, 2)
    large = jnp.dot(
        table_ref[start:stop],
        jnp.concatenate([first, second], axis=1),
        preferred_element_type=jnp.float32,
    )
    small = jnp.dot(
        table_ref[total + start : total + stop], first, preferred_element_type=jnp.float32
    )
    pairs = samples.shape[1]
    return large[:, :pairs] + (large[:, pairs:] + small)


def send_kernel(
    live_ref, stick_hbm, stiff_hbm, slip_hbm, force_hbm, owner_hbm, table_hbm, synthesis_hbm,
    out_ref, synthesis_ref,
    stick_ref, stiff_ref, slip_ref, force_ref, owner_ref, table_ref, sems,
):
    copies = [
        pltpu.make_async_copy(source, held, sems.at[n])
        for n, (source, held) in enumerate(
            (
                (owner_hbm, owner_ref),
                (stiff_hbm, stiff_ref),
                (stick_hbm, stick_ref),
                (slip_hbm, slip_ref),
                (table_hbm, table_ref),
                (force_hbm, force_ref),
                (synthesis_hbm.at[lax.axis_index("h")], synthesis_ref),
            )
        )
    ]
    for copy in copies:
        copy.start()
    pairs = stick_ref.shape[1]
    copies[0].wait()
    owner = owner_ref[...]
    local = owner & (NODE_DEV - 1)
    target = owner // (N_HARM * NODE_DEV)
    first, second = target[0:1], target[1:2]
    square = (pairs, pairs)
    row_first = jnp.broadcast_to(first, square)
    row_second = jnp.broadcast_to(second, square)
    column_first = row_first.T
    column_second = row_second.T
    before = lax.broadcasted_iota(jnp.int32, square, 0) < lax.broadcasted_iota(jnp.int32, square, 1)
    count_first = jnp.where(before & (column_first == row_first), 1, 0)
    count_second = jnp.where(column_first == row_second, 1, 0) + jnp.where(
        before & (column_second == row_second), 1, 0
    )
    place_first = jnp.sum(count_first, axis=0, keepdims=True)
    place_second = jnp.sum(count_second, axis=0, keepdims=True)

    def slot_of(dest, place):
        x, z, core = dest // (N_Z * N_REST), dest // N_REST % N_Z, dest % N_REST
        return (core * CAP + place) * N_FIRST + z * Z_STEP % N_Z * N_X + x

    slot = lax.broadcasted_iota(jnp.int32, (SLOTS, pairs), 0)
    hit_first = slot == slot_of(first, place_first)
    hit_second = slot == slot_of(second, place_second)
    node = jnp.where(hit_first, local[0:1] + 1, 0) + jnp.where(hit_second, local[1:2] + 1, 0)
    node = jnp.sum(node, axis=1, keepdims=True) - 1
    pick = jnp.where(hit_first | hit_second, 1.0, 0.0).astype(jnp.bfloat16)
    for copy in copies[1:-2]:
        copy.wait()
    live = (lax.broadcasted_iota(jnp.int32, (1, pairs), 1) < live_ref[0]).astype(jnp.float32)
    stick = stick_ref[...].astype(jnp.float32)
    weights = (stiff_ref[...] * live) * (stick + (1.0 - stick) * slip_ref[...])
    w_rows = RECORD + W_HIGH
    w_sums = transform(table_ref, 0, w_rows, weights)
    copies[-2].wait()
    forces = force_ref[...] * live
    f_rows = RECORD - F_START
    f_sums = transform(table_ref, w_rows, w_rows + 2 * f_rows, forces)

    def rows(count):
        return jnp.zeros((count, pairs), jnp.float32)

    low = w_sums[:RECORD] + jnp.concatenate([rows(F_START), f_sums[:f_rows]], axis=0)
    high = jnp.concatenate([w_sums[RECORD:], rows(RECORD - W_HIGH)], axis=0) + jnp.concatenate(
        [rows(F_START), f_sums[f_rows:]], axis=0
    )
    lane = lax.broadcasted_iota(jnp.int32, (RECORD, pairs), 0)
    is_w, is_value = lane < W_LANES, lane < MEAN
    size = jnp.maximum(jnp.abs(low), jnp.abs(high))
    step_w = scale_step(jnp.max(jnp.where(is_w, size, 0.0), axis=0, keepdims=True))
    step_f = scale_step(jnp.max(jnp.where(is_value & ~is_w, size, 0.0), axis=0, keepdims=True))
    factor = jnp.where(
        is_w, jnp.exp2(step_w * (-1.0 / STEPS)) * TOP, jnp.exp2(step_f * (-1.0 / STEPS)) * TOP
    )
    factor = jnp.where(is_value, factor, 0.0)
    mean = jnp.round(low[MEAN : MEAN + 1] * MEAN_PAIR).astype(jnp.int32)
    low = jnp.round(low * factor).astype(jnp.int32)
    low = jnp.where(lane == MEAN, ((mean & 0xFFFF) ^ 0x8000) - 0x8000, low)
    low = jnp.where(lane == EXP_W, step_w.astype(jnp.int32), low)
    low = jnp.where(lane == EXP_F, step_f.astype(jnp.int32), low)
    high = jnp.round(high * factor).astype(jnp.int32)
    high = jnp.where(lane == MEAN, mean >> 16, high)
    free = jnp.zeros((FREE, pairs), jnp.int32)
    both = jnp.concatenate([low, free, high, free], axis=0)
    digits = jnp.concatenate([both >> 8, both & 255], axis=0).astype(jnp.float32).astype(jnp.bfloat16)
    sent = lax.dot_general(
        pick, digits, (((1,), (1,)), ((), ())), preferred_element_type=jnp.float32
    )
    value_low = (sent[:, :LANES] * 256.0 + sent[:, 2 * LANES : 3 * LANES]).astype(jnp.int32)
    value_high = (sent[:, LANES : 2 * LANES] * 256.0 + sent[:, 3 * LANES :]).astype(jnp.int32)
    words = (value_high << 16) | (value_low & 0xFFFF)
    words = jnp.where(lax.broadcasted_iota(jnp.int32, (SLOTS, LANES), 1) == NODE, node, words)
    last = words[ROWS * N_FIRST :]
    own = lax.broadcasted_iota(jnp.int32, (N_FIRST, LANES), 1) < RECORD
    for k in range(ROWS):
        spread = pltpu.roll(last, RECORD - FREE * k, 1)
        out_ref[pl.ds(k, N_FIRST, stride=ROWS), :] = jnp.where(
            own, words[k * N_FIRST : (k + 1) * N_FIRST], spread
        )
    copies[-1].wait()


def decode(words, mean_unit):
    lane = lax.broadcasted_iota(jnp.int32, words.shape, words.ndim - 1)
    low = ((words & 0xFFFF) ^ 0x8000) - 0x8000
    high = words >> 16
    step = jnp.where(
        lane < W_LANES, ((words[:, EXP_W : EXP_W + 1] & 0xFFFF) ^ 0x8000) - 0x8000,
        ((words[:, EXP_F : EXP_F + 1] & 0xFFFF) ^ 0x8000) - 0x8000,
    )
    scale = jnp.exp2(step.astype(jnp.float32) * (1.0 / STEPS)) * (1.0 / TOP)
    scale = jnp.where(lane < MEAN, scale, jnp.where(lane == MEAN, 1.0 / mean_unit, 0.0))
    low = jnp.where(lane == MEAN, words, low).astype(jnp.float32) * scale
    high = high.astype(jnp.float32) * jnp.where(lane < MEAN, scale, 0.0)
    return jnp.concatenate([low, high], axis=1)


def split_terms(values, count):
    terms = []
    for _ in range(count):
        term = values.astype(jnp.bfloat16)
        terms.append(term)
        values = values - term.astype(jnp.float32)
    return terms


def merge_kernel(words_ref, out_ref):
    lane = lax.broadcasted_iota(jnp.int32, (N_FIRST, LANES), 1)
    records = [words_ref[pl.ds(k, N_FIRST, stride=ROWS), :] for k in range(ROWS)]
    last = pltpu.roll(records[0], FREE, 1)
    for k in range(1, ROWS):
        last = jnp.where(lane < FREE * k, last, pltpu.roll(records[k], FREE * (k + 1), 1))
    words = jnp.concatenate(records + [last], axis=0)
    values = decode(words, MEAN_PAIR)
    rows = N_REST * NODE_DEV
    place = lax.broadcasted_iota(jnp.int32, (SLOTS, 1), 0) // (CAP * N_FIRST)
    node = words[:, NODE : NODE + 1]
    node = jnp.where(node >= 0, node + place * NODE_DEV, -1)
    owner = lax.broadcasted_iota(jnp.int32, (SLOTS, rows), 1) == node
    owner = jnp.where(owner, 1.0, 0.0).astype(jnp.bfloat16)
    terms = jnp.concatenate(split_terms(values, 3), axis=1)
    total = lax.dot_general(
        owner, terms, (((0,), (0,)), ((), ())), preferred_element_type=jnp.float32
    )
    low = total[:, :LANES] + (total[:, 2 * LANES : 3 * LANES] + total[:, 4 * LANES : 5 * LANES])
    high = total[:, LANES : 2 * LANES] + (total[:, 3 * LANES : 4 * LANES] + total[:, 5 * LANES :])
    size = jnp.maximum(jnp.abs(low), jnp.abs(high))
    lane = lax.broadcasted_iota(jnp.int32, size.shape, 1)
    step_w = scale_step(jnp.max(jnp.where(lane < W_LANES, size, 0.0), axis=1, keepdims=True))
    step_f = scale_step(
        jnp.max(jnp.where((lane >= W_LANES) & (lane < MEAN), size, 0.0), axis=1, keepdims=True)
    )
    factor = jnp.exp2(jnp.where(lane < W_LANES, step_w, step_f) * (-1.0 / STEPS)) * TOP
    factor = jnp.where(lane < MEAN, factor, 0.0)
    words = (jnp.round(high * factor).astype(jnp.int32) << 16) | (
        jnp.round(low * factor).astype(jnp.int32) & 0xFFFF
    )
    words = jnp.where(lane == MEAN, jnp.round(low * MEAN_NODE).astype(jnp.int32), words)
    words = jnp.where(lane == EXP_W, step_w.astype(jnp.int32), words)
    words = jnp.where(lane == EXP_F, step_f.astype(jnp.int32), words)
    for part in range(N_REST):
        for harm in range(N_HARM):
            start = (part * N_HARM + harm) * NODE_DEV
            out_ref[start : start + NODE_DEV] = words[part * NODE_DEV : (part + 1) * NODE_DEV]


def expand_kernel(words_ref, table_ref, out_ref):
    nodes = N_HARM * NODE_DEV
    values = decode(words_ref[:nodes], MEAN_NODE)
    for part in range(1, N_REST):
        values += decode(words_ref[part * nodes : (part + 1) * nodes], MEAN_NODE)
    terms = jnp.concatenate(split_terms(values, 2), axis=0)
    blocks = lax.dot_general(
        table_ref[...], terms, (((1,), (1,)), ((), ())), preferred_element_type=jnp.float32
    )
    blocks = (blocks[:, :nodes] + blocks[:, nodes:]).reshape(PER, PAD, nodes)
    out_ref[...] = blocks[:, :COEFS].astype(jnp.bfloat16)


def in_hbm(array):
    return pltpu.with_memory_space_constraint(array, pltpu.HBM)


def on_device(stick, stiffness, slip_tangent, contact_force, owner_node, live_pairs):
    pairs = stick.shape[1]
    vmem = pl.BlockSpec(memory_space=pltpu.VMEM)
    hbm = pl.BlockSpec(memory_space=pltpu.HBM)
    params = pltpu.CompilerParams(vmem_limit_bytes=32 * 1024 * 1024)
    analysis = analysis_table()
    slots, synthesis = pl.pallas_call(
        send_kernel,
        out_shape=(
            jax.ShapeDtypeStruct((ROWS * N_FIRST, LANES), jnp.int32),
            jax.ShapeDtypeStruct((T_ROWS, 2 * LANES), jnp.bfloat16),
        ),
        in_specs=[pl.BlockSpec(memory_space=pltpu.SMEM)] + [hbm] * 7,
        out_specs=(vmem, vmem),
        scratch_shapes=[
            pltpu.VMEM((SAMPLES, pairs), jnp.int32),
            pltpu.VMEM((1, pairs), jnp.float32),
            pltpu.VMEM((SAMPLES, pairs), jnp.float32),
            pltpu.VMEM((SAMPLES, pairs), jnp.float32),
            pltpu.VMEM((2, pairs), jnp.int32),
            pltpu.VMEM(analysis.shape, jnp.bfloat16),
            pltpu.SemaphoreType.DMA((7,)),
        ],
        compiler_params=params,
    )(
        live_pairs,
        in_hbm(stick),
        in_hbm(stiffness.reshape(1, pairs)),
        in_hbm(slip_tangent),
        in_hbm(contact_force),
        in_hbm(owner_node),
        in_hbm(jnp.asarray(analysis)),
        in_hbm(jnp.asarray(synthesis_table())),
    )
    slots = lax.all_to_all(
        slots.reshape(N_FIRST, 1, ROWS * LANES), "xz", 0, 0, tiled=True, axis_index_groups=[PEERS]
    )
    sums = pl.pallas_call(
        merge_kernel,
        out_shape=jax.ShapeDtypeStruct((N_REST * N_HARM * NODE_DEV, LANES), jnp.int32),
        in_specs=[vmem],
        out_specs=vmem,
        compiler_params=params,
    )(slots.reshape(ROWS * N_FIRST, LANES))
    sums = lax.all_to_all(
        sums.reshape(N_REST * N_HARM, NODE_DEV, LANES), ("c", "h"), 0, 0, tiled=True
    )
    blocks = pl.pallas_call(
        expand_kernel,
        out_shape=jax.ShapeDtypeStruct((PER, COEFS, N_HARM * NODE_DEV), jnp.bfloat16),
        in_specs=[vmem, vmem],
        out_specs=vmem,
        compiler_params=params,
    )(sums.reshape(N_REST * N_HARM * NODE_DEV, LANES), synthesis)
    return jnp.transpose(blocks, (1, 0, 2))


def solution(mesh):
    fine = Mesh(mesh.devices.reshape(N_FIRST, N_REST, N_HARM), ("xz", "c", "h"))
    every = ("xz", "c", "h")
    return jax.shard_map(
        on_device,
        mesh=fine,
        in_specs=(P(None, every), P(every), P(None, every), P(None, every), P(None, every), P(every)),
        out_specs=P(None, "h", ("xz", "c")),
        check_vma=False,
    )
```

```python
import math

import jax
import jax.numpy as jnp
import numpy as np
from jax import lax
from jax.experimental import pallas as pl
from jax.experimental.pallas import tpu as pltpu
from jax.sharding import Mesh
from jax.sharding import PartitionSpec as P

HARMONICS = 33
COEFS = 2 * HARMONICS + 1
SAMPLES = 256
NODE_DEV = 32
CAP = 3
N_X, N_Z, N_REST, N_HARM = 4, 16, 2, 4
N_FIRST = N_X * N_Z
X_FIRST, Z_FIRST = 2, 9
PEERS = [
    (X_FIRST + x) % N_X * N_Z + (Z_FIRST + z) % N_Z for x in range(N_X) for z in range(N_Z)
]
GROUP = N_REST * CAP
SLOTS = N_FIRST * GROUP

LANES = 128
W_LANES = 66
MEAN, EXP_W, EXP_F, NODE = 100, 101, 102, 103
RECORD = 104
F_START = 64
ROWS = GROUP - 1
FREE = LANES - RECORD
HALF = SAMPLES // 2
W_LOW, F_ROWS, W_HIGH = 80, 48, 112
TABLE = W_LOW + F_ROWS + W_HIGH + F_ROWS
STEPS = 16.0
TOP = 32766.0
MEAN_PAIR = 2.0**21
MEAN_NODE = 2.0**31 / (1024.0 * CAP * N_FIRST)
PER = (COEFS + 1) // N_HARM
PAD = 72
T_ROWS = PER * PAD


def weight_lane(sine, k):
    return (k % 2 == 0) * LANES + (k - 1) // 2 + sine * HARMONICS


def force_lane(sine, k):
    if k % 2:
        return W_LANES + (k - 1) // 2 + sine * (HARMONICS // 2 + 1)
    return LANES + W_LANES + k // 2 + sine * (HARMONICS // 2)


def analysis_table():
    k = np.arange(HARMONICS * 2 + 1)[:, None]
    angle = (k * np.arange(HALF)[None, :] % SAMPLES) * (2.0 * np.pi / SAMPLES)
    basis = np.cos(angle), np.sin(angle)
    weights = np.zeros((2 * LANES, HALF))
    forces = np.zeros((2 * LANES, HALF))
    weights[LANES + MEAN] = 1.0
    for n in range(1, 2 * HARMONICS + 1):
        for sine in range(2):
            weights[weight_lane(sine, n)] = basis[sine][n]
    forces[force_lane(0, 0)] = 1.0
    for n in range(1, HARMONICS + 1):
        for sine in range(2):
            forces[force_lane(sine, n)] = basis[sine][n]
    table = np.concatenate(
        [
            weights[:W_LOW],
            forces[F_START : F_START + F_ROWS],
            weights[LANES : LANES + W_HIGH],
            forces[LANES + F_START : LANES + F_START + F_ROWS],
        ],
        axis=0,
    )
    first = table.astype(jnp.bfloat16)
    second = (table - first.astype(np.float64)).astype(jnp.bfloat16)
    return np.concatenate([first, second], axis=0)


def synthesis_table():
    table = np.zeros((N_HARM, PER, PAD, 2 * LANES), np.float32)

    def add(row, kind, k, value):
        if k == 0:
            row[MEAN] += value * (kind == "c")
        else:
            row[weight_lane(int(kind == "s"), abs(k))] += value if k > 0 or kind == "c" else -value

    for i in range(COEFS):
        a, i_sine = (i + 1) // 2, i > 0 and i % 2 == 0
        for j in range(COEFS + 1):
            row = table[j // PER, j % PER, i]
            if j == COEFS:
                row[force_lane(int(i_sine), a)] = 1.0 / math.sqrt(SAMPLES)
                continue
            b, j_sine = (j + 1) // 2, j > 0 and j % 2 == 0
            half = 1.0 / SAMPLES
            if i_sine and j_sine:
                add(row, "c", a - b, half)
                add(row, "c", a + b, -half)
            elif not i_sine and not j_sine:
                add(row, "c", a - b, half)
                add(row, "c", a + b, half)
            elif i_sine:
                add(row, "s", a + b, half)
                add(row, "s", a - b, half)
            else:
                add(row, "s", a + b, half)
                add(row, "s", b - a, half)
    return table.reshape(N_HARM, T_ROWS, 2 * LANES).astype(jnp.bfloat16)


def scale_step(largest):
    return jnp.ceil(jnp.log2(jnp.maximum(largest, 1e-30)) * STEPS + 0.01)


def transform(table_ref, start, rows, samples):
    first, second = split_terms(samples, 2)
    large = jnp.dot(
        table_ref[start : start + rows],
        jnp.concatenate([first, second], axis=1),
        preferred_element_type=jnp.float32,
    )
    small = jnp.dot(
        table_ref[TABLE + start : TABLE + start + rows], first, preferred_element_type=jnp.float32
    )
    pairs = samples.shape[1]
    return large[:, :pairs] + (large[:, pairs:] + small)


def send_kernel(
    live_ref, stick_hbm, stiff_hbm, slip_hbm, force_hbm, owner_hbm, table_hbm, synthesis_hbm,
    out_ref, synthesis_ref,
    stick_ref, stiff_ref, slip_ref, force_ref, owner_ref, table_ref, sems,
):
    copies = [
        pltpu.make_async_copy(source, held, sems.at[n])
        for n, (source, held) in enumerate(
            (
                (owner_hbm, owner_ref),
                (stiff_hbm, stiff_ref),
                (stick_hbm, stick_ref),
                (slip_hbm, slip_ref),
                (table_hbm, table_ref),
                (force_hbm, force_ref),
                (synthesis_hbm.at[lax.axis_index("h")], synthesis_ref),
            )
        )
    ]
    for copy in copies:
        copy.start()
    pairs = stick_ref.shape[1]
    copies[0].wait()
    owner = owner_ref[...]
    local = owner & (NODE_DEV - 1)
    target = owner // (N_HARM * NODE_DEV)
    first, second = target[0:1], target[1:2]
    square = (pairs, pairs)
    row_first = jnp.broadcast_to(first, square)
    row_second = jnp.broadcast_to(second, square)
    column_first = row_first.T
    column_second = row_second.T
    before = lax.broadcasted_iota(jnp.int32, square, 0) < lax.broadcasted_iota(jnp.int32, square, 1)
    count_first = jnp.where(before & (column_first == row_first), 1, 0)
    count_second = jnp.where(column_first == row_second, 1, 0) + jnp.where(
        before & (column_second == row_second), 1, 0
    )
    place_first = jnp.sum(count_first, axis=0, keepdims=True)
    place_second = jnp.sum(count_second, axis=0, keepdims=True)

    def slot_of(dest, place):
        x, z, core = dest // (N_Z * N_REST), dest // N_REST % N_Z, dest % N_REST
        rank = (x + (N_X - X_FIRST)) % N_X * N_Z + (z + (N_Z - Z_FIRST)) % N_Z
        return (core * CAP + place) * N_FIRST + rank

    slot = lax.broadcasted_iota(jnp.int32, (SLOTS, pairs), 0)
    hit_first = slot == slot_of(first, place_first)
    hit_second = slot == slot_of(second, place_second)
    node = jnp.where(hit_first, local[0:1] + 1, 0) + jnp.where(hit_second, local[1:2] + 1, 0)
    node = jnp.sum(node, axis=1, keepdims=True) - 1
    pick = jnp.where(hit_first | hit_second, 1.0, 0.0).astype(jnp.bfloat16)
    for copy in copies[1:-2]:
        copy.wait()
    live = (lax.broadcasted_iota(jnp.int32, (1, pairs), 1) < live_ref[0]).astype(jnp.float32)
    stick = stick_ref[...].astype(jnp.float32)
    weights = (stiff_ref[...] * live) * (stick + (1.0 - stick) * slip_ref[...])
    low = transform(table_ref, 0, W_LOW, weights[:HALF] - weights[HALF:])
    high = transform(table_ref, W_LOW + F_ROWS, W_HIGH, weights[:HALF] + weights[HALF:])
    copies[-2].wait()
    forces = force_ref[...] * live
    f_low = transform(table_ref, W_LOW, F_ROWS, forces[:HALF] - forces[HALF:])
    f_high = transform(
        table_ref, W_LOW + F_ROWS + W_HIGH, F_ROWS, forces[:HALF] + forces[HALF:]
    )

    def rows(count):
        return jnp.zeros((count, pairs), jnp.float32)

    f_end = RECORD - F_START
    low = jnp.concatenate([low, rows(RECORD - W_LOW)], axis=0) + jnp.concatenate(
        [rows(F_START), f_low[:f_end]], axis=0
    )
    high = high[:RECORD] + jnp.concatenate([rows(F_START), f_high[:f_end]], axis=0)
    lane = lax.broadcasted_iota(jnp.int32, (RECORD, pairs), 0)
    is_w, is_value = lane < W_LANES, lane < MEAN
    size = jnp.maximum(jnp.abs(low), jnp.abs(high))
    step_w = scale_step(jnp.max(jnp.where(is_w, size, 0.0), axis=0, keepdims=True))
    step_f = scale_step(jnp.max(jnp.where(is_value & ~is_w, size, 0.0), axis=0, keepdims=True))
    factor = jnp.where(
        is_w, jnp.exp2(step_w * (-1.0 / STEPS)) * TOP, jnp.exp2(step_f * (-1.0 / STEPS)) * TOP
    )
    factor = jnp.where(is_value, factor, 0.0)
    mean = jnp.round(high[MEAN : MEAN + 1] * MEAN_PAIR).astype(jnp.int32)
    low = jnp.round(low * factor).astype(jnp.int32)
    low = jnp.where(lane == MEAN, ((mean & 0xFFFF) ^ 0x8000) - 0x8000, low)
    low = jnp.where(lane == EXP_W, step_w.astype(jnp.int32), low)
    low = jnp.where(lane == EXP_F, step_f.astype(jnp.int32), low)
    high = jnp.round(high * factor).astype(jnp.int32)
    high = jnp.where(lane == MEAN, mean >> 16, high)
    free = jnp.zeros((FREE, pairs), jnp.int32)
    both = jnp.concatenate([low, free, high, free], axis=0)
    digits = jnp.concatenate([both >> 8, both & 255], axis=0).astype(jnp.float32).astype(jnp.bfloat16)
    sent = lax.dot_general(
        pick, digits, (((1,), (1,)), ((), ())), preferred_element_type=jnp.float32
    )
    value_low = (sent[:, :LANES] * 256.0 + sent[:, 2 * LANES : 3 * LANES]).astype(jnp.int32)
    value_high = (sent[:, LANES : 2 * LANES] * 256.0 + sent[:, 3 * LANES :]).astype(jnp.int32)
    words = (value_high << 16) | (value_low & 0xFFFF)
    words = jnp.where(lax.broadcasted_iota(jnp.int32, (SLOTS, LANES), 1) == NODE, node, words)
    last = words[ROWS * N_FIRST :]
    own = lax.broadcasted_iota(jnp.int32, (N_FIRST, LANES), 1) < RECORD
    for k in range(ROWS):
        spread = pltpu.roll(last, RECORD - FREE * k, 1)
        out_ref[pl.ds(k, N_FIRST, stride=ROWS), :] = jnp.where(
            own, words[k * N_FIRST : (k + 1) * N_FIRST], spread
        )
    copies[-1].wait()


def decode(words, mean_unit):
    lane = lax.broadcasted_iota(jnp.int32, words.shape, words.ndim - 1)
    low = ((words & 0xFFFF) ^ 0x8000) - 0x8000
    high = words >> 16
    step = jnp.where(
        lane < W_LANES, ((words[:, EXP_W : EXP_W + 1] & 0xFFFF) ^ 0x8000) - 0x8000,
        ((words[:, EXP_F : EXP_F + 1] & 0xFFFF) ^ 0x8000) - 0x8000,
    )
    scale = jnp.exp2(step.astype(jnp.float32) * (1.0 / STEPS)) * (1.0 / TOP)
    scale = jnp.where(lane < MEAN, scale, jnp.where(lane == MEAN, 1.0 / mean_unit, 0.0))
    low = jnp.where(lane == MEAN, words, low).astype(jnp.float32) * scale
    high = high.astype(jnp.float32) * jnp.where(lane < MEAN, scale, 0.0)
    return jnp.concatenate([low, high], axis=1)


def split_terms(values, count):
    terms = []
    for _ in range(count):
        term = values.astype(jnp.bfloat16)
        terms.append(term)
        values = values - term.astype(jnp.float32)
    return terms


def merge_kernel(words_ref, out_ref):
    lane = lax.broadcasted_iota(jnp.int32, (N_FIRST, LANES), 1)
    records = [words_ref[pl.ds(k, N_FIRST, stride=ROWS), :] for k in range(ROWS)]
    last = pltpu.roll(records[0], FREE, 1)
    for k in range(1, ROWS):
        last = jnp.where(lane < FREE * k, last, pltpu.roll(records[k], FREE * (k + 1), 1))
    words = jnp.concatenate(records + [last], axis=0)
    values = decode(words, MEAN_PAIR)
    rows = N_REST * NODE_DEV
    place = lax.broadcasted_iota(jnp.int32, (SLOTS, 1), 0) // (CAP * N_FIRST)
    node = words[:, NODE : NODE + 1]
    node = jnp.where(node >= 0, node + place * NODE_DEV, -1)
    owner = lax.broadcasted_iota(jnp.int32, (SLOTS, rows), 1) == node
    owner = jnp.where(owner, 1.0, 0.0).astype(jnp.bfloat16)
    terms = jnp.concatenate(split_terms(values, 2), axis=1)
    total = lax.dot_general(
        owner, terms, (((0,), (0,)), ((), ())), preferred_element_type=jnp.float32
    )
    low = total[:, :LANES] + total[:, 2 * LANES : 3 * LANES]
    high = total[:, LANES : 2 * LANES] + total[:, 3 * LANES :]
    size = jnp.maximum(jnp.abs(low), jnp.abs(high))
    lane = lax.broadcasted_iota(jnp.int32, size.shape, 1)
    step_w = scale_step(jnp.max(jnp.where(lane < W_LANES, size, 0.0), axis=1, keepdims=True))
    step_f = scale_step(
        jnp.max(jnp.where((lane >= W_LANES) & (lane < MEAN), size, 0.0), axis=1, keepdims=True)
    )
    factor = jnp.exp2(jnp.where(lane < W_LANES, step_w, step_f) * (-1.0 / STEPS)) * TOP
    factor = jnp.where(lane < MEAN, factor, 0.0)
    words = (jnp.round(high * factor).astype(jnp.int32) << 16) | (
        jnp.round(low * factor).astype(jnp.int32) & 0xFFFF
    )
    words = jnp.where(lane == MEAN, jnp.round(low * MEAN_NODE).astype(jnp.int32), words)
    words = jnp.where(lane == EXP_W, step_w.astype(jnp.int32), words)
    words = jnp.where(lane == EXP_F, step_f.astype(jnp.int32), words)
    for part in range(N_REST):
        for harm in range(N_HARM):
            start = (part * N_HARM + harm) * NODE_DEV
            out_ref[start : start + NODE_DEV] = words[part * NODE_DEV : (part + 1) * NODE_DEV]


def expand_kernel(words_ref, table_ref, out_ref):
    nodes = N_HARM * NODE_DEV
    values = decode(words_ref[:nodes], MEAN_NODE)
    for part in range(1, N_REST):
        values += decode(words_ref[part * nodes : (part + 1) * nodes], MEAN_NODE)
    terms = jnp.concatenate(split_terms(values, 2), axis=0)
    blocks = lax.dot_general(
        table_ref[...], terms, (((1,), (1,)), ((), ())), preferred_element_type=jnp.float32
    )
    blocks = (blocks[:, :nodes] + blocks[:, nodes:]).reshape(PER, PAD, nodes)
    out_ref[...] = blocks[:, :COEFS].astype(jnp.bfloat16)


def in_hbm(array):
    return pltpu.with_memory_space_constraint(array, pltpu.HBM)


def on_device(stick, stiffness, slip_tangent, contact_force, owner_node, live_pairs):
    pairs = stick.shape[1]
    vmem = pl.BlockSpec(memory_space=pltpu.VMEM)
    hbm = pl.BlockSpec(memory_space=pltpu.HBM)
    params = pltpu.CompilerParams(vmem_limit_bytes=32 * 1024 * 1024)
    analysis = analysis_table()
    slots, synthesis = pl.pallas_call(
        send_kernel,
        out_shape=(
            jax.ShapeDtypeStruct((ROWS * N_FIRST, LANES), jnp.int32),
            jax.ShapeDtypeStruct((T_ROWS, 2 * LANES), jnp.bfloat16),
        ),
        in_specs=[pl.BlockSpec(memory_space=pltpu.SMEM)] + [hbm] * 7,
        out_specs=(vmem, vmem),
        scratch_shapes=[
            pltpu.VMEM((SAMPLES, pairs), jnp.int32),
            pltpu.VMEM((1, pairs), jnp.float32),
            pltpu.VMEM((SAMPLES, pairs), jnp.float32),
            pltpu.VMEM((SAMPLES, pairs), jnp.float32),
            pltpu.VMEM((2, pairs), jnp.int32),
            pltpu.VMEM(analysis.shape, jnp.bfloat16),
            pltpu.SemaphoreType.DMA((7,)),
        ],
        compiler_params=params,
    )(
        live_pairs,
        in_hbm(stick),
        in_hbm(stiffness.reshape(1, pairs)),
        in_hbm(slip_tangent),
        in_hbm(contact_force),
        in_hbm(owner_node),
        in_hbm(jnp.asarray(analysis)),
        in_hbm(jnp.asarray(synthesis_table())),
    )
    slots = lax.all_to_all(
        slots.reshape(N_FIRST, 1, ROWS * LANES), "xz", 0, 0, tiled=True, axis_index_groups=[PEERS]
    )
    sums = pl.pallas_call(
        merge_kernel,
        out_shape=jax.ShapeDtypeStruct((N_REST * N_HARM * NODE_DEV, LANES), jnp.int32),
        in_specs=[vmem],
        out_specs=vmem,
        compiler_params=params,
    )(slots.reshape(ROWS * N_FIRST, LANES))
    sums = lax.all_to_all(
        sums.reshape(N_REST * N_HARM, NODE_DEV, LANES), ("c", "h"), 0, 0, tiled=True
    )
    blocks = pl.pallas_call(
        expand_kernel,
        out_shape=jax.ShapeDtypeStruct((PER, COEFS, N_HARM * NODE_DEV), jnp.bfloat16),
        in_specs=[vmem, vmem],
        out_specs=vmem,
        compiler_params=params,
    )(sums.reshape(N_REST * N_HARM * NODE_DEV, LANES), synthesis)
    return jnp.transpose(blocks, (1, 0, 2))


def solution(mesh):
    fine = Mesh(mesh.devices.reshape(N_FIRST, N_REST, N_HARM), ("xz", "c", "h"))
    every = ("xz", "c", "h")
    return jax.shard_map(
        on_device,
        mesh=fine,
        in_specs=(P(None, every), P(every), P(None, every), P(None, every), P(None, every), P(every)),
        out_specs=P(None, "h", ("xz", "c")),
        check_vma=False,
    )
```

```python
import math

import jax
import jax.numpy as jnp
import numpy as np
from jax import lax
from jax.experimental import pallas as pl
from jax.experimental.pallas import tpu as pltpu
from jax.sharding import Mesh
from jax.sharding import PartitionSpec as P

HARMONICS = 33
COEFS = 2 * HARMONICS + 1
SAMPLES = 256
NODE_DEV = 32
CAP = 3
N_X, N_Z, N_REST, N_HARM = 4, 16, 2, 4
N_FIRST = N_X * N_Z
X_FIRST, Z_FIRST = 2, 9
PEERS = [
    (X_FIRST + x) % N_X * N_Z + (Z_FIRST + z) % N_Z for x in range(N_X) for z in range(N_Z)
]
H_FIRST = 2
CORES = (1, 0)
MEMBERS = [core * N_HARM + (H_FIRST + h) % N_HARM for core in CORES for h in range(N_HARM)]
GROUP = N_REST * CAP
SLOTS = N_FIRST * GROUP

LANES = 128
W_LANES = 66
MEAN, EXP_W, EXP_F, NODE = 100, 101, 102, 103
RECORD = 104
F_START = 64
ROWS = GROUP - 1
FREE = LANES - RECORD
HALF = SAMPLES // 2
W_LOW, F_ROWS, W_HIGH = 80, 48, 112
TABLE = W_LOW + F_ROWS + W_HIGH + F_ROWS
STEPS = 16.0
TOP = 32766.0
MEAN_PAIR = 2.0**21
MEAN_NODE = 2.0**31 / (1024.0 * CAP * N_FIRST)
PER = (COEFS + 1) // N_HARM
PAD = 72
T_ROWS = PER * PAD


def weight_lane(sine, k):
    return (k % 2 == 0) * LANES + (k - 1) // 2 + sine * HARMONICS


def force_lane(sine, k):
    if k % 2:
        return W_LANES + (k - 1) // 2 + sine * (HARMONICS // 2 + 1)
    return LANES + W_LANES + k // 2 + sine * (HARMONICS // 2)


def analysis_table():
    k = np.arange(HARMONICS * 2 + 1)[:, None]
    angle = (k * np.arange(HALF)[None, :] % SAMPLES) * (2.0 * np.pi / SAMPLES)
    basis = np.cos(angle), np.sin(angle)
    weights = np.zeros((2 * LANES, HALF))
    forces = np.zeros((2 * LANES, HALF))
    weights[LANES + MEAN] = 1.0
    for n in range(1, 2 * HARMONICS + 1):
        for sine in range(2):
            weights[weight_lane(sine, n)] = basis[sine][n]
    forces[force_lane(0, 0)] = 1.0
    for n in range(1, HARMONICS + 1):
        for sine in range(2):
            forces[force_lane(sine, n)] = basis[sine][n]
    table = np.concatenate(
        [
            weights[:W_LOW],
            forces[F_START : F_START + F_ROWS],
            weights[LANES : LANES + W_HIGH],
            forces[LANES + F_START : LANES + F_START + F_ROWS],
        ],
        axis=0,
    )
    first = table.astype(jnp.bfloat16)
    second = (table - first.astype(np.float64)).astype(jnp.bfloat16)
    return np.concatenate([first, second], axis=0)


def synthesis_table():
    table = np.zeros((N_HARM, PER, PAD, 2 * LANES), np.float32)

    def add(row, kind, k, value):
        if k == 0:
            row[MEAN] += value * (kind == "c")
        else:
            row[weight_lane(int(kind == "s"), abs(k))] += value if k > 0 or kind == "c" else -value

    for i in range(COEFS):
        a, i_sine = (i + 1) // 2, i > 0 and i % 2 == 0
        for j in range(COEFS + 1):
            row = table[j // PER, j % PER, i]
            if j == COEFS:
                row[force_lane(int(i_sine), a)] = 1.0 / math.sqrt(SAMPLES)
                continue
            b, j_sine = (j + 1) // 2, j > 0 and j % 2 == 0
            half = 1.0 / SAMPLES
            if i_sine and j_sine:
                add(row, "c", a - b, half)
                add(row, "c", a + b, -half)
            elif not i_sine and not j_sine:
                add(row, "c", a - b, half)
                add(row, "c", a + b, half)
            elif i_sine:
                add(row, "s", a + b, half)
                add(row, "s", a - b, half)
            else:
                add(row, "s", a + b, half)
                add(row, "s", b - a, half)
    return table.reshape(N_HARM, T_ROWS, 2 * LANES).astype(jnp.bfloat16)


def scale_step(largest):
    return jnp.ceil(jnp.log2(jnp.maximum(largest, 1e-30)) * STEPS + 0.01)


def transform(table_ref, start, rows, samples):
    first, second = split_terms(samples, 2)
    large = jnp.dot(
        table_ref[start : start + rows],
        jnp.concatenate([first, second], axis=1),
        preferred_element_type=jnp.float32,
    )
    small = jnp.dot(
        table_ref[TABLE + start : TABLE + start + rows], first, preferred_element_type=jnp.float32
    )
    pairs = samples.shape[1]
    return large[:, :pairs] + (large[:, pairs:] + small)


def send_kernel(
    live_ref, stick_hbm, stiff_hbm, slip_hbm, force_hbm, owner_hbm, table_hbm, synthesis_hbm,
    out_ref, synthesis_ref,
    stick_ref, stiff_ref, slip_ref, force_ref, owner_ref, table_ref, sems,
):
    copies = [
        pltpu.make_async_copy(source, held, sems.at[n])
        for n, (source, held) in enumerate(
            (
                (owner_hbm, owner_ref),
                (stiff_hbm, stiff_ref),
                (stick_hbm, stick_ref),
                (slip_hbm, slip_ref),
                (table_hbm, table_ref),
                (force_hbm, force_ref),
                (synthesis_hbm.at[lax.axis_index("h")], synthesis_ref),
            )
        )
    ]
    for copy in copies:
        copy.start()
    pairs = stick_ref.shape[1]
    copies[0].wait()
    owner = owner_ref[...]
    local = owner & (NODE_DEV - 1)
    target = owner // (N_HARM * NODE_DEV)
    first, second = target[0:1], target[1:2]
    square = (pairs, pairs)
    row_first = jnp.broadcast_to(first, square)
    row_second = jnp.broadcast_to(second, square)
    column_first = row_first.T
    column_second = row_second.T
    before = lax.broadcasted_iota(jnp.int32, square, 0) < lax.broadcasted_iota(jnp.int32, square, 1)
    count_first = jnp.where(before & (column_first == row_first), 1, 0)
    count_second = jnp.where(column_first == row_second, 1, 0) + jnp.where(
        before & (column_second == row_second), 1, 0
    )
    place_first = jnp.sum(count_first, axis=0, keepdims=True)
    place_second = jnp.sum(count_second, axis=0, keepdims=True)

    def slot_of(dest, place):
        x, z, core = dest // (N_Z * N_REST), dest // N_REST % N_Z, dest % N_REST
        rank = (x + (N_X - X_FIRST)) % N_X * N_Z + (z + (N_Z - Z_FIRST)) % N_Z
        return (core * CAP + place) * N_FIRST + rank

    slot = lax.broadcasted_iota(jnp.int32, (SLOTS, pairs), 0)
    hit_first = slot == slot_of(first, place_first)
    hit_second = slot == slot_of(second, place_second)
    node = jnp.where(hit_first, local[0:1] + 1, 0) + jnp.where(hit_second, local[1:2] + 1, 0)
    node = jnp.sum(node, axis=1, keepdims=True) - 1
    pick = jnp.where(hit_first | hit_second, 1.0, 0.0).astype(jnp.bfloat16)
    for copy in copies[1:-2]:
        copy.wait()
    live = (lax.broadcasted_iota(jnp.int32, (1, pairs), 1) < live_ref[0]).astype(jnp.float32)
    stick = stick_ref[...].astype(jnp.float32)
    weights = (stiff_ref[...] * live) * (stick + (1.0 - stick) * slip_ref[...])
    low = transform(table_ref, 0, W_LOW, weights[:HALF] - weights[HALF:])
    high = transform(table_ref, W_LOW + F_ROWS, W_HIGH, weights[:HALF] + weights[HALF:])
    copies[-2].wait()
    forces = force_ref[...] * live
    f_low = transform(table_ref, W_LOW, F_ROWS, forces[:HALF] - forces[HALF:])
    f_high = transform(
        table_ref, W_LOW + F_ROWS + W_HIGH, F_ROWS, forces[:HALF] + forces[HALF:]
    )

    def rows(count):
        return jnp.zeros((count, pairs), jnp.float32)

    f_end = RECORD - F_START
    low = jnp.concatenate([low, rows(RECORD - W_LOW)], axis=0) + jnp.concatenate(
        [rows(F_START), f_low[:f_end]], axis=0
    )
    high = high[:RECORD] + jnp.concatenate([rows(F_START), f_high[:f_end]], axis=0)
    lane = lax.broadcasted_iota(jnp.int32, (RECORD, pairs), 0)
    is_w, is_value = lane < W_LANES, lane < MEAN
    size = jnp.maximum(jnp.abs(low), jnp.abs(high))
    step_w = scale_step(jnp.max(jnp.where(is_w, size, 0.0), axis=0, keepdims=True))
    step_f = scale_step(jnp.max(jnp.where(is_value & ~is_w, size, 0.0), axis=0, keepdims=True))
    factor = jnp.where(
        is_w, jnp.exp2(step_w * (-1.0 / STEPS)) * TOP, jnp.exp2(step_f * (-1.0 / STEPS)) * TOP
    )
    factor = jnp.where(is_value, factor, 0.0)
    mean = jnp.round(high[MEAN : MEAN + 1] * MEAN_PAIR).astype(jnp.int32)
    low = jnp.round(low * factor).astype(jnp.int32)
    low = jnp.where(lane == MEAN, ((mean & 0xFFFF) ^ 0x8000) - 0x8000, low)
    low = jnp.where(lane == EXP_W, step_w.astype(jnp.int32), low)
    low = jnp.where(lane == EXP_F, step_f.astype(jnp.int32), low)
    high = jnp.round(high * factor).astype(jnp.int32)
    high = jnp.where(lane == MEAN, mean >> 16, high)
    free = jnp.zeros((FREE, pairs), jnp.int32)
    both = jnp.concatenate([low, free, high, free], axis=0)
    digits = jnp.concatenate([both >> 8, both & 255], axis=0).astype(jnp.float32).astype(jnp.bfloat16)
    sent = lax.dot_general(
        pick, digits, (((1,), (1,)), ((), ())), preferred_element_type=jnp.float32
    )
    value_low = (sent[:, :LANES] * 256.0 + sent[:, 2 * LANES : 3 * LANES]).astype(jnp.int32)
    value_high = (sent[:, LANES : 2 * LANES] * 256.0 + sent[:, 3 * LANES :]).astype(jnp.int32)
    words = (value_high << 16) | (value_low & 0xFFFF)
    words = jnp.where(lax.broadcasted_iota(jnp.int32, (SLOTS, LANES), 1) == NODE, node, words)
    last = words[ROWS * N_FIRST :]
    own = lax.broadcasted_iota(jnp.int32, (N_FIRST, LANES), 1) < RECORD
    for k in range(ROWS):
        spread = pltpu.roll(last, RECORD - FREE * k, 1)
        out_ref[pl.ds(k, N_FIRST, stride=ROWS), :] = jnp.where(
            own, words[k * N_FIRST : (k + 1) * N_FIRST], spread
        )
    copies[-1].wait()


def decode(words, mean_unit):
    lane = lax.broadcasted_iota(jnp.int32, words.shape, words.ndim - 1)
    low = ((words & 0xFFFF) ^ 0x8000) - 0x8000
    high = words >> 16
    step = jnp.where(
        lane < W_LANES, ((words[:, EXP_W : EXP_W + 1] & 0xFFFF) ^ 0x8000) - 0x8000,
        ((words[:, EXP_F : EXP_F + 1] & 0xFFFF) ^ 0x8000) - 0x8000,
    )
    scale = jnp.exp2(step.astype(jnp.float32) * (1.0 / STEPS)) * (1.0 / TOP)
    scale = jnp.where(lane < MEAN, scale, jnp.where(lane == MEAN, 1.0 / mean_unit, 0.0))
    low = jnp.where(lane == MEAN, words, low).astype(jnp.float32) * scale
    high = high.astype(jnp.float32) * jnp.where(lane < MEAN, scale, 0.0)
    return jnp.concatenate([low, high], axis=1)


def split_terms(values, count):
    terms = []
    for _ in range(count):
        term = values.astype(jnp.bfloat16)
        terms.append(term)
        values = values - term.astype(jnp.float32)
    return terms


def merge_kernel(words_ref, out_ref):
    lane = lax.broadcasted_iota(jnp.int32, (N_FIRST, LANES), 1)
    records = [words_ref[pl.ds(k, N_FIRST, stride=ROWS), :] for k in range(ROWS)]
    last = pltpu.roll(records[0], FREE, 1)
    for k in range(1, ROWS):
        last = jnp.where(lane < FREE * k, last, pltpu.roll(records[k], FREE * (k + 1), 1))
    words = jnp.concatenate(records + [last], axis=0)
    values = decode(words, MEAN_PAIR)
    rows = N_REST * NODE_DEV
    place = lax.broadcasted_iota(jnp.int32, (SLOTS, 1), 0) // (CAP * N_FIRST)
    node = words[:, NODE : NODE + 1]
    node = jnp.where(node >= 0, node + place * NODE_DEV, -1)
    owner = lax.broadcasted_iota(jnp.int32, (SLOTS, rows), 1) == node
    owner = jnp.where(owner, 1.0, 0.0).astype(jnp.bfloat16)
    terms = jnp.concatenate(split_terms(values, 2), axis=1)
    total = lax.dot_general(
        owner, terms, (((0,), (0,)), ((), ())), preferred_element_type=jnp.float32
    )
    low = total[:, :LANES] + total[:, 2 * LANES : 3 * LANES]
    high = total[:, LANES : 2 * LANES] + total[:, 3 * LANES :]
    size = jnp.maximum(jnp.abs(low), jnp.abs(high))
    lane = lax.broadcasted_iota(jnp.int32, size.shape, 1)
    step_w = scale_step(jnp.max(jnp.where(lane < W_LANES, size, 0.0), axis=1, keepdims=True))
    step_f = scale_step(
        jnp.max(jnp.where((lane >= W_LANES) & (lane < MEAN), size, 0.0), axis=1, keepdims=True)
    )
    factor = jnp.exp2(jnp.where(lane < W_LANES, step_w, step_f) * (-1.0 / STEPS)) * TOP
    factor = jnp.where(lane < MEAN, factor, 0.0)
    words = (jnp.round(high * factor).astype(jnp.int32) << 16) | (
        jnp.round(low * factor).astype(jnp.int32) & 0xFFFF
    )
    words = jnp.where(lane == MEAN, jnp.round(low * MEAN_NODE).astype(jnp.int32), words)
    words = jnp.where(lane == EXP_W, step_w.astype(jnp.int32), words)
    words = jnp.where(lane == EXP_F, step_f.astype(jnp.int32), words)
    for rank, member in enumerate(MEMBERS):
        start = member // N_HARM * NODE_DEV
        out_ref[rank * NODE_DEV : (rank + 1) * NODE_DEV] = words[start : start + NODE_DEV]


def expand_kernel(words_ref, table_ref, out_ref):
    nodes = N_HARM * NODE_DEV
    values = decode(words_ref[:nodes], MEAN_NODE)
    for part in range(1, N_REST):
        values += decode(words_ref[part * nodes : (part + 1) * nodes], MEAN_NODE)
    wrap = (N_HARM - H_FIRST) * NODE_DEV
    values = jnp.concatenate([values[wrap:], values[:wrap]], axis=0)
    terms = jnp.concatenate(split_terms(values, 2), axis=0)
    blocks = lax.dot_general(
        table_ref[...], terms, (((1,), (1,)), ((), ())), preferred_element_type=jnp.float32
    )
    blocks = (blocks[:, :nodes] + blocks[:, nodes:]).reshape(PER, PAD, nodes)
    out_ref[...] = blocks[:, :COEFS].astype(jnp.bfloat16)


def in_hbm(array):
    return pltpu.with_memory_space_constraint(array, pltpu.HBM)


def on_device(stick, stiffness, slip_tangent, contact_force, owner_node, live_pairs):
    pairs = stick.shape[1]
    vmem = pl.BlockSpec(memory_space=pltpu.VMEM)
    hbm = pl.BlockSpec(memory_space=pltpu.HBM)
    params = pltpu.CompilerParams(vmem_limit_bytes=32 * 1024 * 1024)
    analysis = analysis_table()
    slots, synthesis = pl.pallas_call(
        send_kernel,
        out_shape=(
            jax.ShapeDtypeStruct((ROWS * N_FIRST, LANES), jnp.int32),
            jax.ShapeDtypeStruct((T_ROWS, 2 * LANES), jnp.bfloat16),
        ),
        in_specs=[pl.BlockSpec(memory_space=pltpu.SMEM)] + [hbm] * 7,
        out_specs=(vmem, vmem),
        scratch_shapes=[
            pltpu.VMEM((SAMPLES, pairs), jnp.int32),
            pltpu.VMEM((1, pairs), jnp.float32),
            pltpu.VMEM((SAMPLES, pairs), jnp.float32),
            pltpu.VMEM((SAMPLES, pairs), jnp.float32),
            pltpu.VMEM((2, pairs), jnp.int32),
            pltpu.VMEM(analysis.shape, jnp.bfloat16),
            pltpu.SemaphoreType.DMA((7,)),
        ],
        compiler_params=params,
    )(
        live_pairs,
        in_hbm(stick),
        in_hbm(stiffness.reshape(1, pairs)),
        in_hbm(slip_tangent),
        in_hbm(contact_force),
        in_hbm(owner_node),
        in_hbm(jnp.asarray(analysis)),
        in_hbm(jnp.asarray(synthesis_table())),
    )
    slots = lax.all_to_all(
        slots.reshape(N_FIRST, 1, ROWS * LANES), "xz", 0, 0, tiled=True, axis_index_groups=[PEERS]
    )
    sums = pl.pallas_call(
        merge_kernel,
        out_shape=jax.ShapeDtypeStruct((N_REST * N_HARM * NODE_DEV, LANES), jnp.int32),
        in_specs=[vmem],
        out_specs=vmem,
        compiler_params=params,
    )(slots.reshape(ROWS * N_FIRST, LANES))
    sums = lax.all_to_all(
        sums.reshape(N_REST * N_HARM, NODE_DEV, LANES),
        ("c", "h"),
        0,
        0,
        tiled=True,
        axis_index_groups=[MEMBERS],
    )
    blocks = pl.pallas_call(
        expand_kernel,
        out_shape=jax.ShapeDtypeStruct((PER, COEFS, N_HARM * NODE_DEV), jnp.bfloat16),
        in_specs=[vmem, vmem],
        out_specs=vmem,
        compiler_params=params,
    )(sums.reshape(N_REST * N_HARM * NODE_DEV, LANES), synthesis)
    return jnp.transpose(blocks, (1, 0, 2))


def solution(mesh):
    fine = Mesh(mesh.devices.reshape(N_FIRST, N_REST, N_HARM), ("xz", "c", "h"))
    every = ("xz", "c", "h")
    return jax.shard_map(
        on_device,
        mesh=fine,
        in_specs=(P(None, every), P(every), P(None, every), P(None, every), P(None, every), P(every)),
        out_specs=P(None, "h", ("xz", "c")),
        check_vma=False,
    )
```

```python
import math

import jax
import jax.numpy as jnp
import numpy as np
from jax import lax
from jax.experimental import pallas as pl
from jax.experimental.pallas import tpu as pltpu
from jax.sharding import Mesh
from jax.sharding import PartitionSpec as P

HARMONICS = 33
COEFS = 2 * HARMONICS + 1
SAMPLES = 256
NODE_DEV = 32
CAP = 3
N_X, N_Z, N_REST, N_HARM = 4, 16, 2, 4
N_FIRST = N_X * N_Z
X_FIRST, Z_FIRST = 2, 9
PEERS = [
    (X_FIRST + x) % N_X * N_Z + (Z_FIRST + z) % N_Z for x in range(N_X) for z in range(N_Z)
]
H_FIRST = 2
CORES = (1, 0)
MEMBERS = [core * N_HARM + (H_FIRST + h) % N_HARM for core in CORES for h in range(N_HARM)]
GROUP = N_REST * CAP
SLOTS = N_FIRST * GROUP

LANES = 128
W_LANES = 66
MEAN, EXP_W, EXP_F, NODE = 100, 101, 102, 103
RECORD = 104
F_START = 64
ROWS = GROUP - 1
FREE = LANES - RECORD
HALF = SAMPLES // 2
W_LOW, F_ROWS, W_HIGH = 80, 48, 112
STEPS = 16.0
TOP = 32766.0
MEAN_PAIR = 2.0**21
MEAN_NODE = 2.0**31 / (1024.0 * CAP * N_FIRST)
PER = (COEFS + 1) // N_HARM
PAD = 72
T_ROWS = PER * PAD


def weight_lane(sine, k):
    return (k % 2 == 0) * LANES + (k - 1) // 2 + sine * HARMONICS


def force_lane(sine, k):
    if k % 2:
        return W_LANES + (k - 1) // 2 + sine * (HARMONICS // 2 + 1)
    return LANES + W_LANES + k // 2 + sine * (HARMONICS // 2)


def analysis_table():
    k = np.arange(HARMONICS * 2 + 1)[:, None]
    angle = (k * np.arange(HALF)[None, :] % SAMPLES) * (2.0 * np.pi / SAMPLES)
    basis = np.cos(angle), np.sin(angle)
    weights = np.zeros((2 * LANES, HALF))
    forces = np.zeros((2 * LANES, HALF))
    weights[LANES + MEAN] = 1.0
    for n in range(1, 2 * HARMONICS + 1):
        for sine in range(2):
            weights[weight_lane(sine, n)] = basis[sine][n]
    forces[force_lane(0, 0)] = 1.0
    for n in range(1, HARMONICS + 1):
        for sine in range(2):
            forces[force_lane(sine, n)] = basis[sine][n]
    table = np.concatenate(
        [
            weights[:W_LOW],
            forces[F_START : F_START + F_ROWS],
            weights[LANES : LANES + W_HIGH],
            forces[LANES + F_START : LANES + F_START + F_ROWS],
        ],
        axis=0,
    )
    first = table.astype(jnp.bfloat16)
    second = (table - first.astype(np.float64)).astype(jnp.bfloat16)
    return np.concatenate([first, second], axis=1)


def synthesis_table():
    table = np.zeros((N_HARM, PER, PAD, 2 * LANES), np.float32)

    def add(row, kind, k, value):
        if k == 0:
            row[MEAN] += value * (kind == "c")
        else:
            row[weight_lane(int(kind == "s"), abs(k))] += value if k > 0 or kind == "c" else -value

    for i in range(COEFS):
        a, i_sine = (i + 1) // 2, i > 0 and i % 2 == 0
        for j in range(COEFS + 1):
            row = table[j // PER, j % PER, i]
            if j == COEFS:
                row[force_lane(int(i_sine), a)] = 1.0 / math.sqrt(SAMPLES)
                continue
            b, j_sine = (j + 1) // 2, j > 0 and j % 2 == 0
            half = 1.0 / SAMPLES
            if i_sine and j_sine:
                add(row, "c", a - b, half)
                add(row, "c", a + b, -half)
            elif not i_sine and not j_sine:
                add(row, "c", a - b, half)
                add(row, "c", a + b, half)
            elif i_sine:
                add(row, "s", a + b, half)
                add(row, "s", a - b, half)
            else:
                add(row, "s", a + b, half)
                add(row, "s", b - a, half)
    return table.reshape(N_HARM, T_ROWS, 2 * LANES).astype(jnp.bfloat16)


def scale_step(largest):
    return jnp.ceil(jnp.log2(jnp.maximum(largest, 1e-30)) * STEPS + 0.01)


def transform(table_ref, start, rows, samples):
    first, second = split_terms(samples, 2)
    upper = jnp.concatenate([first, second], axis=1)
    lower = jnp.concatenate([first, jnp.zeros_like(first)], axis=1)
    sums = jnp.dot(
        table_ref[start : start + rows],
        jnp.concatenate([upper, lower], axis=0),
        preferred_element_type=jnp.float32,
    )
    pairs = samples.shape[1]
    return sums[:, :pairs] + sums[:, pairs:]


def send_kernel(
    live_ref, stick_hbm, stiff_hbm, slip_hbm, force_hbm, owner_hbm, table_hbm, synthesis_hbm,
    out_ref, synthesis_ref,
    stick_ref, stiff_ref, slip_ref, force_ref, owner_ref, table_ref, sems,
):
    copies = [
        pltpu.make_async_copy(source, held, sems.at[n])
        for n, (source, held) in enumerate(
            (
                (owner_hbm, owner_ref),
                (stiff_hbm, stiff_ref),
                (stick_hbm, stick_ref),
                (slip_hbm, slip_ref),
                (table_hbm, table_ref),
                (force_hbm, force_ref),
                (synthesis_hbm.at[lax.axis_index("h")], synthesis_ref),
            )
        )
    ]
    for copy in copies:
        copy.start()
    pairs = stick_ref.shape[1]
    copies[0].wait()
    owner = owner_ref[...]
    local = owner & (NODE_DEV - 1)
    target = owner // (N_HARM * NODE_DEV)
    first, second = target[0:1], target[1:2]
    square = (pairs, pairs)
    row_first = jnp.broadcast_to(first, square)
    row_second = jnp.broadcast_to(second, square)
    column_first = row_first.T
    column_second = row_second.T
    before = lax.broadcasted_iota(jnp.int32, square, 0) < lax.broadcasted_iota(jnp.int32, square, 1)
    count_first = jnp.where(before & (column_first == row_first), 1, 0)
    count_second = jnp.where(column_first == row_second, 1, 0) + jnp.where(
        before & (column_second == row_second), 1, 0
    )
    place_first = jnp.sum(count_first, axis=0, keepdims=True)
    place_second = jnp.sum(count_second, axis=0, keepdims=True)

    def slot_of(dest, place):
        x, z, core = dest // (N_Z * N_REST), dest // N_REST % N_Z, dest % N_REST
        rank = (x + (N_X - X_FIRST)) % N_X * N_Z + (z + (N_Z - Z_FIRST)) % N_Z
        return (core * CAP + place) * N_FIRST + rank

    slot = lax.broadcasted_iota(jnp.int32, (SLOTS, pairs), 0)
    hit_first = slot == slot_of(first, place_first)
    hit_second = slot == slot_of(second, place_second)
    node = jnp.where(hit_first, local[0:1] + 1, 0) + jnp.where(hit_second, local[1:2] + 1, 0)
    node = jnp.sum(node, axis=1, keepdims=True) - 1
    hit = hit_first | hit_second
    pick = jnp.concatenate([jnp.where(hit, 256.0, 0.0), jnp.where(hit, 1.0, 0.0)], axis=1)
    pick = pick.astype(jnp.bfloat16)
    for copy in copies[1:-2]:
        copy.wait()
    live = (lax.broadcasted_iota(jnp.int32, (1, pairs), 1) < live_ref[0]).astype(jnp.float32)
    stick = stick_ref[...].astype(jnp.float32)
    weights = (stiff_ref[...] * live) * (stick + (1.0 - stick) * slip_ref[...])
    low = transform(table_ref, 0, W_LOW, weights[:HALF] - weights[HALF:])
    high = transform(table_ref, W_LOW + F_ROWS, W_HIGH, weights[:HALF] + weights[HALF:])
    copies[-2].wait()
    forces = force_ref[...] * live
    f_low = transform(table_ref, W_LOW, F_ROWS, forces[:HALF] - forces[HALF:])
    f_high = transform(
        table_ref, W_LOW + F_ROWS + W_HIGH, F_ROWS, forces[:HALF] + forces[HALF:]
    )

    def rows(count):
        return jnp.zeros((count, pairs), jnp.float32)

    f_end = RECORD - F_START
    low = jnp.concatenate([low, rows(RECORD - W_LOW)], axis=0) + jnp.concatenate(
        [rows(F_START), f_low[:f_end]], axis=0
    )
    high = high[:RECORD] + jnp.concatenate([rows(F_START), f_high[:f_end]], axis=0)
    lane = lax.broadcasted_iota(jnp.int32, (RECORD, pairs), 0)
    is_w, is_value = lane < W_LANES, lane < MEAN
    size = jnp.maximum(jnp.abs(low), jnp.abs(high))
    step_w = scale_step(jnp.max(jnp.where(is_w, size, 0.0), axis=0, keepdims=True))
    step_f = scale_step(jnp.max(jnp.where(is_value & ~is_w, size, 0.0), axis=0, keepdims=True))
    factor = jnp.where(
        is_w, jnp.exp2(step_w * (-1.0 / STEPS)) * TOP, jnp.exp2(step_f * (-1.0 / STEPS)) * TOP
    )
    factor = jnp.where(is_value, factor, 0.0)
    mean = jnp.round(high[MEAN : MEAN + 1] * MEAN_PAIR).astype(jnp.int32)
    low = jnp.round(low * factor).astype(jnp.int32)
    low = jnp.where(lane == MEAN, ((mean & 0xFFFF) ^ 0x8000) - 0x8000, low)
    low = jnp.where(lane == EXP_W, step_w.astype(jnp.int32), low)
    low = jnp.where(lane == EXP_F, step_f.astype(jnp.int32), low)
    high = jnp.round(high * factor).astype(jnp.int32)
    high = jnp.where(lane == MEAN, mean >> 16, high)
    free = jnp.zeros((FREE, pairs), jnp.int32)
    both = jnp.concatenate([low, free, high, free], axis=0)
    digits = jnp.concatenate([both >> 8, both & 255], axis=1).astype(jnp.float32).astype(jnp.bfloat16)
    sent = lax.dot_general(
        pick, digits, (((1,), (1,)), ((), ())), preferred_element_type=jnp.float32
    )
    sent = sent.astype(jnp.int32)
    words = (sent[:, LANES:] << 16) | (sent[:, :LANES] & 0xFFFF)
    words = jnp.where(lax.broadcasted_iota(jnp.int32, (SLOTS, LANES), 1) == NODE, node, words)
    last = words[ROWS * N_FIRST :]
    own = lax.broadcasted_iota(jnp.int32, (N_FIRST, LANES), 1) < RECORD
    for k in range(ROWS):
        spread = pltpu.roll(last, RECORD - FREE * k, 1)
        out_ref[pl.ds(k, N_FIRST, stride=ROWS), :] = jnp.where(
            own, words[k * N_FIRST : (k + 1) * N_FIRST], spread
        )
    copies[-1].wait()


def decode(words, mean_unit):
    lane = lax.broadcasted_iota(jnp.int32, words.shape, words.ndim - 1)
    low = ((words & 0xFFFF) ^ 0x8000) - 0x8000
    high = words >> 16
    step = jnp.where(
        lane < W_LANES, ((words[:, EXP_W : EXP_W + 1] & 0xFFFF) ^ 0x8000) - 0x8000,
        ((words[:, EXP_F : EXP_F + 1] & 0xFFFF) ^ 0x8000) - 0x8000,
    )
    scale = jnp.exp2(step.astype(jnp.float32) * (1.0 / STEPS)) * (1.0 / TOP)
    scale = jnp.where(lane < MEAN, scale, jnp.where(lane == MEAN, 1.0 / mean_unit, 0.0))
    low = jnp.where(lane == MEAN, words, low).astype(jnp.float32) * scale
    high = high.astype(jnp.float32) * jnp.where(lane < MEAN, scale, 0.0)
    return jnp.concatenate([low, high], axis=1)


def split_terms(values, count):
    terms = []
    for _ in range(count):
        term = values.astype(jnp.bfloat16)
        terms.append(term)
        values = values - term.astype(jnp.float32)
    return terms


def merge_kernel(words_ref, out_ref):
    lane = lax.broadcasted_iota(jnp.int32, (N_FIRST, LANES), 1)
    records = [words_ref[pl.ds(k, N_FIRST, stride=ROWS), :] for k in range(ROWS)]
    last = pltpu.roll(records[0], FREE, 1)
    for k in range(1, ROWS):
        last = jnp.where(lane < FREE * k, last, pltpu.roll(records[k], FREE * (k + 1), 1))
    words = jnp.concatenate(records + [last], axis=0)
    values = decode(words, MEAN_PAIR)
    rows = N_REST * NODE_DEV
    place = lax.broadcasted_iota(jnp.int32, (SLOTS, 1), 0) // (CAP * N_FIRST)
    node = words[:, NODE : NODE + 1]
    node = jnp.where(node >= 0, node + place * NODE_DEV, -1)
    owner = lax.broadcasted_iota(jnp.int32, (SLOTS, rows), 1) == node
    owner = jnp.where(owner, 1.0, 0.0).astype(jnp.bfloat16)
    terms = jnp.concatenate(split_terms(values, 2), axis=1)
    total = lax.dot_general(
        owner, terms, (((0,), (0,)), ((), ())), preferred_element_type=jnp.float32
    )
    low = total[:, :LANES] + total[:, 2 * LANES : 3 * LANES]
    high = total[:, LANES : 2 * LANES] + total[:, 3 * LANES :]
    size = jnp.maximum(jnp.abs(low), jnp.abs(high))
    lane = lax.broadcasted_iota(jnp.int32, size.shape, 1)
    step_w = scale_step(jnp.max(jnp.where(lane < W_LANES, size, 0.0), axis=1, keepdims=True))
    step_f = scale_step(
        jnp.max(jnp.where((lane >= W_LANES) & (lane < MEAN), size, 0.0), axis=1, keepdims=True)
    )
    factor = jnp.exp2(jnp.where(lane < W_LANES, step_w, step_f) * (-1.0 / STEPS)) * TOP
    factor = jnp.where(lane < MEAN, factor, 0.0)
    words = (jnp.round(high * factor).astype(jnp.int32) << 16) | (
        jnp.round(low * factor).astype(jnp.int32) & 0xFFFF
    )
    words = jnp.where(lane == MEAN, jnp.round(low * MEAN_NODE).astype(jnp.int32), words)
    words = jnp.where(lane == EXP_W, step_w.astype(jnp.int32), words)
    words = jnp.where(lane == EXP_F, step_f.astype(jnp.int32), words)
    for rank, member in enumerate(MEMBERS):
        start = member // N_HARM * NODE_DEV
        out_ref[rank * NODE_DEV : (rank + 1) * NODE_DEV] = words[start : start + NODE_DEV]


def expand_kernel(words_ref, table_ref, out_ref):
    nodes = N_HARM * NODE_DEV
    values = decode(words_ref[:nodes], MEAN_NODE)
    for part in range(1, N_REST):
        values += decode(words_ref[part * nodes : (part + 1) * nodes], MEAN_NODE)
    wrap = (N_HARM - H_FIRST) * NODE_DEV
    values = jnp.concatenate([values[wrap:], values[:wrap]], axis=0)
    terms = jnp.concatenate(split_terms(values, 2), axis=0)
    blocks = lax.dot_general(
        table_ref[...], terms, (((1,), (1,)), ((), ())), preferred_element_type=jnp.float32
    )
    blocks = (blocks[:, :nodes] + blocks[:, nodes:]).reshape(PER, PAD, nodes)
    out_ref[...] = blocks[:, :COEFS].astype(jnp.bfloat16)


def in_hbm(array):
    return pltpu.with_memory_space_constraint(array, pltpu.HBM)


def on_device(stick, stiffness, slip_tangent, contact_force, owner_node, live_pairs):
    pairs = stick.shape[1]
    vmem = pl.BlockSpec(memory_space=pltpu.VMEM)
    hbm = pl.BlockSpec(memory_space=pltpu.HBM)
    params = pltpu.CompilerParams(vmem_limit_bytes=32 * 1024 * 1024)
    analysis = analysis_table()
    slots, synthesis = pl.pallas_call(
        send_kernel,
        out_shape=(
            jax.ShapeDtypeStruct((ROWS * N_FIRST, LANES), jnp.int32),
            jax.ShapeDtypeStruct((T_ROWS, 2 * LANES), jnp.bfloat16),
        ),
        in_specs=[pl.BlockSpec(memory_space=pltpu.SMEM)] + [hbm] * 7,
        out_specs=(vmem, vmem),
        scratch_shapes=[
            pltpu.VMEM((SAMPLES, pairs), jnp.int32),
            pltpu.VMEM((1, pairs), jnp.float32),
            pltpu.VMEM((SAMPLES, pairs), jnp.float32),
            pltpu.VMEM((SAMPLES, pairs), jnp.float32),
            pltpu.VMEM((2, pairs), jnp.int32),
            pltpu.VMEM(analysis.shape, jnp.bfloat16),
            pltpu.SemaphoreType.DMA((7,)),
        ],
        compiler_params=params,
    )(
        live_pairs,
        in_hbm(stick),
        in_hbm(stiffness.reshape(1, pairs)),
        in_hbm(slip_tangent),
        in_hbm(contact_force),
        in_hbm(owner_node),
        in_hbm(jnp.asarray(analysis)),
        in_hbm(jnp.asarray(synthesis_table())),
    )
    slots = lax.all_to_all(
        slots.reshape(N_FIRST, 1, ROWS * LANES), "xz", 0, 0, tiled=True, axis_index_groups=[PEERS]
    )
    sums = pl.pallas_call(
        merge_kernel,
        out_shape=jax.ShapeDtypeStruct((N_REST * N_HARM * NODE_DEV, LANES), jnp.int32),
        in_specs=[vmem],
        out_specs=vmem,
        compiler_params=params,
    )(slots.reshape(ROWS * N_FIRST, LANES))
    sums = lax.all_to_all(
        sums.reshape(N_REST * N_HARM, NODE_DEV, LANES),
        ("c", "h"),
        0,
        0,
        tiled=True,
        axis_index_groups=[MEMBERS],
    )
    blocks = pl.pallas_call(
        expand_kernel,
        out_shape=jax.ShapeDtypeStruct((PER, COEFS, N_HARM * NODE_DEV), jnp.bfloat16),
        in_specs=[vmem, vmem],
        out_specs=vmem,
        compiler_params=params,
    )(sums.reshape(N_REST * N_HARM * NODE_DEV, LANES), synthesis)
    return jnp.transpose(blocks, (1, 0, 2))


def solution(mesh):
    fine = Mesh(mesh.devices.reshape(N_FIRST, N_REST, N_HARM), ("xz", "c", "h"))
    every = ("xz", "c", "h")
    return jax.shard_map(
        on_device,
        mesh=fine,
        in_specs=(P(None, every), P(every), P(None, every), P(None, every), P(None, every), P(every)),
        out_specs=P(None, "h", ("xz", "c")),
        check_vma=False,
    )
```

```python
import math

import jax
import jax.numpy as jnp
import numpy as np
from jax import lax
from jax.experimental import pallas as pl
from jax.experimental.pallas import tpu as pltpu
from jax.sharding import Mesh
from jax.sharding import PartitionSpec as P

HARMONICS = 33
COEFS = 2 * HARMONICS + 1
SAMPLES = 256
NODE_DEV = 32
CAP = 3
N_X, N_Z, N_REST, N_HARM = 4, 16, 2, 4
N_FIRST = N_X * N_Z
X_FIRST = 2
Z_FIRST = (8, 9)


def peers(core):
    return [
        ((X_FIRST + x) % N_X * N_Z + (Z_FIRST[core] + z) % N_Z) * N_REST + core
        for x in range(N_X)
        for z in range(N_Z)
    ]


H_FIRST = 2
CORES = (1, 0)
MEMBERS = [core * N_HARM + (H_FIRST + h) % N_HARM for core in CORES for h in range(N_HARM)]
GROUP = N_REST * CAP
SLOTS = N_FIRST * GROUP

LANES = 128
W_LANES = 66
MEAN, EXP_W, EXP_F, NODE = 100, 101, 102, 103
RECORD = 104
F_START = 64
ROWS = GROUP - 1
FREE = LANES - RECORD
HALF = SAMPLES // 2
W_LOW, F_ROWS, W_HIGH = 80, 48, 112
STEPS = 16.0
TOP = 32766.0
MEAN_PAIR = 2.0**21
MEAN_NODE = 2.0**31 / (1024.0 * CAP * N_FIRST)
PER = (COEFS + 1) // N_HARM
PAD = 72
T_ROWS = PER * PAD


def weight_lane(sine, k):
    return (k % 2 == 0) * LANES + (k - 1) // 2 + sine * HARMONICS


def force_lane(sine, k):
    if k % 2:
        return W_LANES + (k - 1) // 2 + sine * (HARMONICS // 2 + 1)
    return LANES + W_LANES + k // 2 + sine * (HARMONICS // 2)


def analysis_table():
    k = np.arange(HARMONICS * 2 + 1)[:, None]
    angle = (k * np.arange(HALF)[None, :] % SAMPLES) * (2.0 * np.pi / SAMPLES)
    basis = np.cos(angle), np.sin(angle)
    weights = np.zeros((2 * LANES, HALF))
    forces = np.zeros((2 * LANES, HALF))
    weights[LANES + MEAN] = 1.0
    for n in range(1, 2 * HARMONICS + 1):
        for sine in range(2):
            weights[weight_lane(sine, n)] = basis[sine][n]
    forces[force_lane(0, 0)] = 1.0
    for n in range(1, HARMONICS + 1):
        for sine in range(2):
            forces[force_lane(sine, n)] = basis[sine][n]
    table = np.concatenate(
        [
            weights[:W_LOW],
            forces[F_START : F_START + F_ROWS],
            weights[LANES : LANES + W_HIGH],
            forces[LANES + F_START : LANES + F_START + F_ROWS],
        ],
        axis=0,
    )
    first = table.astype(jnp.bfloat16)
    second = (table - first.astype(np.float64)).astype(jnp.bfloat16)
    return np.concatenate([first, second], axis=1)


def synthesis_table():
    table = np.zeros((N_HARM, PER, PAD, 2 * LANES), np.float32)

    def add(row, kind, k, value):
        if k == 0:
            row[MEAN] += value * (kind == "c")
        else:
            row[weight_lane(int(kind == "s"), abs(k))] += value if k > 0 or kind == "c" else -value

    for i in range(COEFS):
        a, i_sine = (i + 1) // 2, i > 0 and i % 2 == 0
        for j in range(COEFS + 1):
            row = table[j // PER, j % PER, i]
            if j == COEFS:
                row[force_lane(int(i_sine), a)] = 1.0 / math.sqrt(SAMPLES)
                continue
            b, j_sine = (j + 1) // 2, j > 0 and j % 2 == 0
            half = 1.0 / SAMPLES
            if i_sine and j_sine:
                add(row, "c", a - b, half)
                add(row, "c", a + b, -half)
            elif not i_sine and not j_sine:
                add(row, "c", a - b, half)
                add(row, "c", a + b, half)
            elif i_sine:
                add(row, "s", a + b, half)
                add(row, "s", a - b, half)
            else:
                add(row, "s", a + b, half)
                add(row, "s", b - a, half)
    return table.reshape(N_HARM, T_ROWS, 2 * LANES).astype(jnp.bfloat16)


def scale_step(largest):
    return jnp.ceil(jnp.log2(jnp.maximum(largest, 1e-30)) * STEPS + 0.01)


def transform(table_ref, start, rows, samples):
    first, second = split_terms(samples, 2)
    upper = jnp.concatenate([first, second], axis=1)
    lower = jnp.concatenate([first, jnp.zeros_like(first)], axis=1)
    sums = jnp.dot(
        table_ref[start : start + rows],
        jnp.concatenate([upper, lower], axis=0),
        preferred_element_type=jnp.float32,
    )
    pairs = samples.shape[1]
    return sums[:, :pairs] + sums[:, pairs:]


def send_kernel(
    live_ref, stick_hbm, stiff_hbm, slip_hbm, force_hbm, owner_hbm, table_hbm, synthesis_hbm,
    out_ref, synthesis_ref,
    stick_ref, stiff_ref, slip_ref, force_ref, owner_ref, table_ref, sems,
):
    copies = [
        pltpu.make_async_copy(source, held, sems.at[n])
        for n, (source, held) in enumerate(
            (
                (owner_hbm, owner_ref),
                (stiff_hbm, stiff_ref),
                (stick_hbm, stick_ref),
                (slip_hbm, slip_ref),
                (table_hbm, table_ref),
                (force_hbm, force_ref),
                (synthesis_hbm.at[lax.axis_index("h")], synthesis_ref),
            )
        )
    ]
    for copy in copies:
        copy.start()
    pairs = stick_ref.shape[1]
    copies[0].wait()
    owner = owner_ref[...]
    local = owner & (NODE_DEV - 1)
    target = owner // (N_HARM * NODE_DEV)
    first, second = target[0:1], target[1:2]
    square = (pairs, pairs)
    row_first = jnp.broadcast_to(first, square)
    row_second = jnp.broadcast_to(second, square)
    column_first = row_first.T
    column_second = row_second.T
    before = lax.broadcasted_iota(jnp.int32, square, 0) < lax.broadcasted_iota(jnp.int32, square, 1)
    count_first = jnp.where(before & (column_first == row_first), 1, 0)
    count_second = jnp.where(column_first == row_second, 1, 0) + jnp.where(
        before & (column_second == row_second), 1, 0
    )
    place_first = jnp.sum(count_first, axis=0, keepdims=True)
    place_second = jnp.sum(count_second, axis=0, keepdims=True)

    def slot_of(dest, place):
        x, z, core = dest // (N_Z * N_REST), dest // N_REST % N_Z, dest % N_REST
        shift = jnp.where(lax.axis_index("c") == 0, N_Z - Z_FIRST[0], N_Z - Z_FIRST[1])
        rank = (x + (N_X - X_FIRST)) % N_X * N_Z + (z + shift) % N_Z
        return (core * CAP + place) * N_FIRST + rank

    slot = lax.broadcasted_iota(jnp.int32, (SLOTS, pairs), 0)
    hit_first = slot == slot_of(first, place_first)
    hit_second = slot == slot_of(second, place_second)
    node = jnp.where(hit_first, local[0:1] + 1, 0) + jnp.where(hit_second, local[1:2] + 1, 0)
    node = jnp.sum(node, axis=1, keepdims=True) - 1
    hit = hit_first | hit_second
    pick = jnp.concatenate([jnp.where(hit, 256.0, 0.0), jnp.where(hit, 1.0, 0.0)], axis=1)
    pick = pick.astype(jnp.bfloat16)
    for copy in copies[1:-2]:
        copy.wait()
    live = (lax.broadcasted_iota(jnp.int32, (1, pairs), 1) < live_ref[0]).astype(jnp.float32)
    stick = stick_ref[...].astype(jnp.float32)
    weights = (stiff_ref[...] * live) * (stick + (1.0 - stick) * slip_ref[...])
    low = transform(table_ref, 0, W_LOW, weights[:HALF] - weights[HALF:])
    high = transform(table_ref, W_LOW + F_ROWS, W_HIGH, weights[:HALF] + weights[HALF:])
    copies[-2].wait()
    forces = force_ref[...] * live
    f_low = transform(table_ref, W_LOW, F_ROWS, forces[:HALF] - forces[HALF:])
    f_high = transform(
        table_ref, W_LOW + F_ROWS + W_HIGH, F_ROWS, forces[:HALF] + forces[HALF:]
    )

    def rows(count):
        return jnp.zeros((count, pairs), jnp.float32)

    f_end = RECORD - F_START
    low = jnp.concatenate([low, rows(RECORD - W_LOW)], axis=0) + jnp.concatenate(
        [rows(F_START), f_low[:f_end]], axis=0
    )
    high = high[:RECORD] + jnp.concatenate([rows(F_START), f_high[:f_end]], axis=0)
    lane = lax.broadcasted_iota(jnp.int32, (RECORD, pairs), 0)
    is_w, is_value = lane < W_LANES, lane < MEAN
    size = jnp.maximum(jnp.abs(low), jnp.abs(high))
    step_w = scale_step(jnp.max(jnp.where(is_w, size, 0.0), axis=0, keepdims=True))
    step_f = scale_step(jnp.max(jnp.where(is_value & ~is_w, size, 0.0), axis=0, keepdims=True))
    factor = jnp.where(
        is_w, jnp.exp2(step_w * (-1.0 / STEPS)) * TOP, jnp.exp2(step_f * (-1.0 / STEPS)) * TOP
    )
    factor = jnp.where(is_value, factor, 0.0)
    mean = jnp.round(high[MEAN : MEAN + 1] * MEAN_PAIR).astype(jnp.int32)
    low = jnp.round(low * factor).astype(jnp.int32)
    low = jnp.where(lane == MEAN, ((mean & 0xFFFF) ^ 0x8000) - 0x8000, low)
    low = jnp.where(lane == EXP_W, step_w.astype(jnp.int32), low)
    low = jnp.where(lane == EXP_F, step_f.astype(jnp.int32), low)
    high = jnp.round(high * factor).astype(jnp.int32)
    high = jnp.where(lane == MEAN, mean >> 16, high)
    free = jnp.zeros((FREE, pairs), jnp.int32)
    both = jnp.concatenate([low, free, high, free], axis=0)
    digits = jnp.concatenate([both >> 8, both & 255], axis=1).astype(jnp.float32).astype(jnp.bfloat16)
    sent = lax.dot_general(
        pick, digits, (((1,), (1,)), ((), ())), preferred_element_type=jnp.float32
    )
    sent = sent.astype(jnp.int32)
    words = (sent[:, LANES:] << 16) | (sent[:, :LANES] & 0xFFFF)
    words = jnp.where(lax.broadcasted_iota(jnp.int32, (SLOTS, LANES), 1) == NODE, node, words)
    last = words[ROWS * N_FIRST :]
    own = lax.broadcasted_iota(jnp.int32, (N_FIRST, LANES), 1) < RECORD
    for k in range(ROWS):
        spread = pltpu.roll(last, RECORD - FREE * k, 1)
        out_ref[pl.ds(k, N_FIRST, stride=ROWS), :] = jnp.where(
            own, words[k * N_FIRST : (k + 1) * N_FIRST], spread
        )
    copies[-1].wait()


def decode(words, mean_unit):
    lane = lax.broadcasted_iota(jnp.int32, words.shape, words.ndim - 1)
    low = ((words & 0xFFFF) ^ 0x8000) - 0x8000
    high = words >> 16
    step = jnp.where(
        lane < W_LANES, ((words[:, EXP_W : EXP_W + 1] & 0xFFFF) ^ 0x8000) - 0x8000,
        ((words[:, EXP_F : EXP_F + 1] & 0xFFFF) ^ 0x8000) - 0x8000,
    )
    scale = jnp.exp2(step.astype(jnp.float32) * (1.0 / STEPS)) * (1.0 / TOP)
    scale = jnp.where(lane < MEAN, scale, jnp.where(lane == MEAN, 1.0 / mean_unit, 0.0))
    low = jnp.where(lane == MEAN, words, low).astype(jnp.float32) * scale
    high = high.astype(jnp.float32) * jnp.where(lane < MEAN, scale, 0.0)
    return jnp.concatenate([low, high], axis=1)


def split_terms(values, count):
    terms = []
    for _ in range(count):
        term = values.astype(jnp.bfloat16)
        terms.append(term)
        values = values - term.astype(jnp.float32)
    return terms


def merge_kernel(words_ref, out_ref):
    lane = lax.broadcasted_iota(jnp.int32, (N_FIRST, LANES), 1)
    records = [words_ref[pl.ds(k, N_FIRST, stride=ROWS), :] for k in range(ROWS)]
    last = pltpu.roll(records[0], FREE, 1)
    for k in range(1, ROWS):
        last = jnp.where(lane < FREE * k, last, pltpu.roll(records[k], FREE * (k + 1), 1))
    words = jnp.concatenate(records + [last], axis=0)
    values = decode(words, MEAN_PAIR)
    rows = N_REST * NODE_DEV
    place = lax.broadcasted_iota(jnp.int32, (SLOTS, 1), 0) // (CAP * N_FIRST)
    node = words[:, NODE : NODE + 1]
    node = jnp.where(node >= 0, node + place * NODE_DEV, -1)
    owner = lax.broadcasted_iota(jnp.int32, (SLOTS, rows), 1) == node
    owner = jnp.where(owner, 1.0, 0.0).astype(jnp.bfloat16)
    terms = jnp.concatenate(split_terms(values, 2), axis=1)
    total = lax.dot_general(
        owner, terms, (((0,), (0,)), ((), ())), preferred_element_type=jnp.float32
    )
    low = total[:, :LANES] + total[:, 2 * LANES : 3 * LANES]
    high = total[:, LANES : 2 * LANES] + total[:, 3 * LANES :]
    size = jnp.maximum(jnp.abs(low), jnp.abs(high))
    lane = lax.broadcasted_iota(jnp.int32, size.shape, 1)
    step_w = scale_step(jnp.max(jnp.where(lane < W_LANES, size, 0.0), axis=1, keepdims=True))
    step_f = scale_step(
        jnp.max(jnp.where((lane >= W_LANES) & (lane < MEAN), size, 0.0), axis=1, keepdims=True)
    )
    factor = jnp.exp2(jnp.where(lane < W_LANES, step_w, step_f) * (-1.0 / STEPS)) * TOP
    factor = jnp.where(lane < MEAN, factor, 0.0)
    words = (jnp.round(high * factor).astype(jnp.int32) << 16) | (
        jnp.round(low * factor).astype(jnp.int32) & 0xFFFF
    )
    words = jnp.where(lane == MEAN, jnp.round(low * MEAN_NODE).astype(jnp.int32), words)
    words = jnp.where(lane == EXP_W, step_w.astype(jnp.int32), words)
    words = jnp.where(lane == EXP_F, step_f.astype(jnp.int32), words)
    for rank, member in enumerate(MEMBERS):
        start = member // N_HARM * NODE_DEV
        out_ref[rank * NODE_DEV : (rank + 1) * NODE_DEV] = words[start : start + NODE_DEV]


def expand_kernel(words_ref, table_ref, out_ref):
    nodes = N_HARM * NODE_DEV
    values = decode(words_ref[:nodes], MEAN_NODE)
    for part in range(1, N_REST):
        values += decode(words_ref[part * nodes : (part + 1) * nodes], MEAN_NODE)
    wrap = (N_HARM - H_FIRST) * NODE_DEV
    values = jnp.concatenate([values[wrap:], values[:wrap]], axis=0)
    terms = jnp.concatenate(split_terms(values, 2), axis=0)
    blocks = lax.dot_general(
        table_ref[...], terms, (((1,), (1,)), ((), ())), preferred_element_type=jnp.float32
    )
    blocks = (blocks[:, :nodes] + blocks[:, nodes:]).reshape(PER, PAD, nodes)
    out_ref[...] = blocks[:, :COEFS].astype(jnp.bfloat16)


def in_hbm(array):
    return pltpu.with_memory_space_constraint(array, pltpu.HBM)


def on_device(stick, stiffness, slip_tangent, contact_force, owner_node, live_pairs):
    pairs = stick.shape[1]
    vmem = pl.BlockSpec(memory_space=pltpu.VMEM)
    hbm = pl.BlockSpec(memory_space=pltpu.HBM)
    params = pltpu.CompilerParams(vmem_limit_bytes=32 * 1024 * 1024)
    analysis = analysis_table()
    slots, synthesis = pl.pallas_call(
        send_kernel,
        out_shape=(
            jax.ShapeDtypeStruct((ROWS * N_FIRST, LANES), jnp.int32),
            jax.ShapeDtypeStruct((T_ROWS, 2 * LANES), jnp.bfloat16),
        ),
        in_specs=[pl.BlockSpec(memory_space=pltpu.SMEM)] + [hbm] * 7,
        out_specs=(vmem, vmem),
        scratch_shapes=[
            pltpu.VMEM((SAMPLES, pairs), jnp.int32),
            pltpu.VMEM((1, pairs), jnp.float32),
            pltpu.VMEM((SAMPLES, pairs), jnp.float32),
            pltpu.VMEM((SAMPLES, pairs), jnp.float32),
            pltpu.VMEM((2, pairs), jnp.int32),
            pltpu.VMEM(analysis.shape, jnp.bfloat16),
            pltpu.SemaphoreType.DMA((7,)),
        ],
        compiler_params=params,
    )(
        live_pairs,
        in_hbm(stick),
        in_hbm(stiffness.reshape(1, pairs)),
        in_hbm(slip_tangent),
        in_hbm(contact_force),
        in_hbm(owner_node),
        in_hbm(jnp.asarray(analysis)),
        in_hbm(jnp.asarray(synthesis_table())),
    )
    slots = lax.all_to_all(
        slots.reshape(N_FIRST, 1, ROWS * LANES),
        ("xz", "c"),
        0,
        0,
        tiled=True,
        axis_index_groups=[peers(core) for core in range(N_REST)],
    )
    sums = pl.pallas_call(
        merge_kernel,
        out_shape=jax.ShapeDtypeStruct((N_REST * N_HARM * NODE_DEV, LANES), jnp.int32),
        in_specs=[vmem],
        out_specs=vmem,
        compiler_params=params,
    )(slots.reshape(ROWS * N_FIRST, LANES))
    sums = lax.all_to_all(
        sums.reshape(N_REST * N_HARM, NODE_DEV, LANES),
        ("c", "h"),
        0,
        0,
        tiled=True,
        axis_index_groups=[MEMBERS],
    )
    blocks = pl.pallas_call(
        expand_kernel,
        out_shape=jax.ShapeDtypeStruct((PER, COEFS, N_HARM * NODE_DEV), jnp.bfloat16),
        in_specs=[vmem, vmem],
        out_specs=vmem,
        compiler_params=params,
    )(sums.reshape(N_REST * N_HARM * NODE_DEV, LANES), synthesis)
    return jnp.transpose(blocks, (1, 0, 2))


def solution(mesh):
    fine = Mesh(mesh.devices.reshape(N_FIRST, N_REST, N_HARM), ("xz", "c", "h"))
    every = ("xz", "c", "h")
    return jax.shard_map(
        on_device,
        mesh=fine,
        in_specs=(P(None, every), P(every), P(None, every), P(None, every), P(None, every), P(every)),
        out_specs=P(None, "h", ("xz", "c")),
        check_vma=False,
    )
```

```python
import math

import jax
import jax.numpy as jnp
import numpy as np
from jax import lax
from jax.experimental import pallas as pl
from jax.experimental.pallas import tpu as pltpu
from jax.sharding import Mesh
from jax.sharding import PartitionSpec as P

HARMONICS = 33
COEFS = 2 * HARMONICS + 1
SAMPLES = 256
NODE_DEV = 32
CAP = 3
N_X, N_Z, N_REST, N_HARM = 4, 16, 2, 4
N_FIRST = N_X * N_Z
X_FIRST = 2
Z_FIRST = (8, 9)


def peers(core):
    return [
        ((X_FIRST + x) % N_X * N_Z + (Z_FIRST[core] + z) % N_Z) * N_REST + core
        for x in range(N_X)
        for z in range(N_Z)
    ]


H_FIRST = 2
CORES = (1, 0)
MEMBERS = [core * N_HARM + (H_FIRST + h) % N_HARM for core in CORES for h in range(N_HARM)]
GROUP = N_REST * CAP
SLOTS = N_FIRST * GROUP

LANES = 128
W_LANES = 66
MEAN, EXP_W, EXP_F, NODE = 100, 101, 102, 103
RECORD = 104
F_START = 64
ROWS = GROUP - 1
FREE = LANES - RECORD
HALF = SAMPLES // 2
W_LOW, F_ROWS, W_HIGH = 80, 48, 112
STEPS = 16.0
TOP = 32766.0
MEAN_PAIR = 2.0**21
MEAN_NODE = 2.0**31 / (1024.0 * CAP * N_FIRST)
PER = (COEFS + 1) // N_HARM
PAD = 72
T_ROWS = PER * PAD


def weight_lane(sine, k):
    return (k % 2 == 0) * LANES + (k - 1) // 2 + sine * HARMONICS


def force_lane(sine, k):
    if k % 2:
        return W_LANES + (k - 1) // 2 + sine * (HARMONICS // 2 + 1)
    return LANES + W_LANES + k // 2 + sine * (HARMONICS // 2)


def analysis_table():
    k = np.arange(HARMONICS * 2 + 1)[:, None]
    angle = (k * np.arange(HALF)[None, :] % SAMPLES) * (2.0 * np.pi / SAMPLES)
    basis = np.cos(angle), np.sin(angle)
    weights = np.zeros((2 * LANES, HALF))
    forces = np.zeros((2 * LANES, HALF))
    weights[LANES + MEAN] = 1.0
    for n in range(1, 2 * HARMONICS + 1):
        for sine in range(2):
            weights[weight_lane(sine, n)] = basis[sine][n]
    forces[force_lane(0, 0)] = 1.0
    for n in range(1, HARMONICS + 1):
        for sine in range(2):
            forces[force_lane(sine, n)] = basis[sine][n]
    table = np.concatenate(
        [
            weights[:W_LOW],
            forces[F_START : F_START + F_ROWS],
            weights[LANES : LANES + W_HIGH],
            forces[LANES + F_START : LANES + F_START + F_ROWS],
        ],
        axis=0,
    )
    first = table.astype(jnp.bfloat16)
    second = (table - first.astype(np.float64)).astype(jnp.bfloat16)
    return np.concatenate([first, second], axis=1)


def synthesis_table():
    table = np.zeros((N_HARM, PER, PAD, 2 * LANES), np.float32)

    def add(row, kind, k, value):
        if k == 0:
            row[MEAN] += value * (kind == "c")
        else:
            row[weight_lane(int(kind == "s"), abs(k))] += value if k > 0 or kind == "c" else -value

    for i in range(COEFS):
        a, i_sine = (i + 1) // 2, i > 0 and i % 2 == 0
        for j in range(COEFS + 1):
            row = table[j // PER, j % PER, i]
            if j == COEFS:
                row[force_lane(int(i_sine), a)] = 1.0 / math.sqrt(SAMPLES)
                continue
            b, j_sine = (j + 1) // 2, j > 0 and j % 2 == 0
            half = 1.0 / SAMPLES
            if i_sine and j_sine:
                add(row, "c", a - b, half)
                add(row, "c", a + b, -half)
            elif not i_sine and not j_sine:
                add(row, "c", a - b, half)
                add(row, "c", a + b, half)
            elif i_sine:
                add(row, "s", a + b, half)
                add(row, "s", a - b, half)
            else:
                add(row, "s", a + b, half)
                add(row, "s", b - a, half)
    return table.reshape(N_HARM, T_ROWS, 2 * LANES).astype(jnp.bfloat16)


def scale_step(largest):
    return jnp.ceil(jnp.log2(jnp.maximum(largest, 1e-30)) * STEPS + 0.01)


def transform(table_ref, start, rows, samples):
    first, second = split_terms(samples, 2)
    upper = jnp.concatenate([first, second], axis=1)
    lower = jnp.concatenate([first, jnp.zeros_like(first)], axis=1)
    sums = jnp.dot(
        table_ref[start : start + rows],
        jnp.concatenate([upper, lower], axis=0),
        preferred_element_type=jnp.float32,
    )
    pairs = samples.shape[1]
    return sums[:, :pairs] + sums[:, pairs:]


def send_kernel(
    live_ref, stick_hbm, stiff_hbm, slip_hbm, force_hbm, owner_hbm, table_hbm, synthesis_hbm,
    out_ref, synthesis_ref,
    stick_ref, stiff_ref, slip_ref, force_ref, owner_ref, table_ref, sems,
):
    copies = [
        pltpu.make_async_copy(source, held, sems.at[n])
        for n, (source, held) in enumerate(
            (
                (owner_hbm, owner_ref),
                (stiff_hbm, stiff_ref),
                (stick_hbm, stick_ref),
                (slip_hbm, slip_ref),
                (table_hbm, table_ref),
                (force_hbm, force_ref),
                (synthesis_hbm.at[lax.axis_index("h")], synthesis_ref),
            )
        )
    ]
    for copy in copies:
        copy.start()
    pairs = stick_ref.shape[1]
    copies[0].wait()
    owner = owner_ref[...]
    local = owner & (NODE_DEV - 1)
    target = owner // (N_HARM * NODE_DEV)
    first, second = target[0:1], target[1:2]
    square = (pairs, pairs)
    row_first = jnp.broadcast_to(first, square)
    row_second = jnp.broadcast_to(second, square)
    column_first = row_first.T
    column_second = row_second.T
    before = lax.broadcasted_iota(jnp.int32, square, 0) < lax.broadcasted_iota(jnp.int32, square, 1)
    count_first = jnp.where(before & (column_first == row_first), 1, 0)
    count_second = jnp.where(column_first == row_second, 1, 0) + jnp.where(
        before & (column_second == row_second), 1, 0
    )
    place_first = jnp.sum(count_first, axis=0, keepdims=True)
    place_second = jnp.sum(count_second, axis=0, keepdims=True)

    def slot_of(dest, place):
        x, z, core = dest // (N_Z * N_REST), dest // N_REST % N_Z, dest % N_REST
        shift = jnp.where(lax.axis_index("c") == 0, N_Z - Z_FIRST[0], N_Z - Z_FIRST[1])
        rank = (x + (N_X - X_FIRST)) % N_X * N_Z + (z + shift) % N_Z
        return (core * CAP + place) * N_FIRST + rank

    slot = lax.broadcasted_iota(jnp.int32, (SLOTS, pairs), 0)
    hit_first = slot == slot_of(first, place_first)
    hit_second = slot == slot_of(second, place_second)
    node = jnp.where(hit_first, local[0:1] + 1, 0) + jnp.where(hit_second, local[1:2] + 1, 0)
    node = jnp.sum(node, axis=1, keepdims=True) - 1
    hit = hit_first | hit_second
    pick = jnp.concatenate([jnp.where(hit, 256.0, 0.0), jnp.where(hit, 1.0, 0.0)], axis=1)
    pick = pick.astype(jnp.bfloat16)
    for copy in copies[1:-2]:
        copy.wait()
    live = (lax.broadcasted_iota(jnp.int32, (1, pairs), 1) < live_ref[0:1]).astype(jnp.float32)
    stick = stick_ref[...].astype(jnp.float32)
    weights = (stiff_ref[...] * live) * (stick + (1.0 - stick) * slip_ref[...])
    low = transform(table_ref, 0, W_LOW, weights[:HALF] - weights[HALF:])
    high = transform(table_ref, W_LOW + F_ROWS, W_HIGH, weights[:HALF] + weights[HALF:])
    copies[-2].wait()
    forces = force_ref[...] * live
    f_low = transform(table_ref, W_LOW, F_ROWS, forces[:HALF] - forces[HALF:])
    f_high = transform(
        table_ref, W_LOW + F_ROWS + W_HIGH, F_ROWS, forces[:HALF] + forces[HALF:]
    )

    def rows(count):
        return jnp.zeros((count, pairs), jnp.float32)

    f_end = RECORD - F_START
    low = jnp.concatenate([low, rows(RECORD - W_LOW)], axis=0) + jnp.concatenate(
        [rows(F_START), f_low[:f_end]], axis=0
    )
    high = high[:RECORD] + jnp.concatenate([rows(F_START), f_high[:f_end]], axis=0)
    lane = lax.broadcasted_iota(jnp.int32, (RECORD, pairs), 0)
    is_w, is_value = lane < W_LANES, lane < MEAN
    size = jnp.maximum(jnp.abs(low), jnp.abs(high))
    step_w = scale_step(jnp.max(jnp.where(is_w, size, 0.0), axis=0, keepdims=True))
    step_f = scale_step(jnp.max(jnp.where(is_value & ~is_w, size, 0.0), axis=0, keepdims=True))
    factor = jnp.where(
        is_w, jnp.exp2(step_w * (-1.0 / STEPS)) * TOP, jnp.exp2(step_f * (-1.0 / STEPS)) * TOP
    )
    factor = jnp.where(is_value, factor, 0.0)
    mean = jnp.round(high[MEAN : MEAN + 1] * MEAN_PAIR).astype(jnp.int32)
    low = jnp.round(low * factor).astype(jnp.int32)
    low = jnp.where(lane == MEAN, ((mean & 0xFFFF) ^ 0x8000) - 0x8000, low)
    low = jnp.where(lane == EXP_W, step_w.astype(jnp.int32), low)
    low = jnp.where(lane == EXP_F, step_f.astype(jnp.int32), low)
    high = jnp.round(high * factor).astype(jnp.int32)
    high = jnp.where(lane == MEAN, mean >> 16, high)
    free = jnp.zeros((FREE, pairs), jnp.int32)
    both = jnp.concatenate([low, free, high, free], axis=0)
    digits = jnp.concatenate([both >> 8, both & 255], axis=1).astype(jnp.float32).astype(jnp.bfloat16)
    sent = lax.dot_general(
        pick, digits, (((1,), (1,)), ((), ())), preferred_element_type=jnp.float32
    )
    sent = sent.astype(jnp.int32)
    words = (sent[:, LANES:] << 16) | (sent[:, :LANES] & 0xFFFF)
    words = jnp.where(lax.broadcasted_iota(jnp.int32, (SLOTS, LANES), 1) == NODE, node, words)
    last = words[ROWS * N_FIRST :]
    own = lax.broadcasted_iota(jnp.int32, (N_FIRST, LANES), 1) < RECORD
    for k in range(ROWS):
        spread = pltpu.roll(last, RECORD - FREE * k, 1)
        out_ref[pl.ds(k, N_FIRST, stride=ROWS), :] = jnp.where(
            own, words[k * N_FIRST : (k + 1) * N_FIRST], spread
        )
    copies[-1].wait()


def decode(words, mean_unit):
    lane = lax.broadcasted_iota(jnp.int32, words.shape, words.ndim - 1)
    low = ((words & 0xFFFF) ^ 0x8000) - 0x8000
    high = words >> 16
    step = jnp.where(
        lane < W_LANES, ((words[:, EXP_W : EXP_W + 1] & 0xFFFF) ^ 0x8000) - 0x8000,
        ((words[:, EXP_F : EXP_F + 1] & 0xFFFF) ^ 0x8000) - 0x8000,
    )
    scale = jnp.exp2(step.astype(jnp.float32) * (1.0 / STEPS)) * (1.0 / TOP)
    scale = jnp.where(lane < MEAN, scale, jnp.where(lane == MEAN, 1.0 / mean_unit, 0.0))
    low = jnp.where(lane == MEAN, words, low).astype(jnp.float32) * scale
    high = high.astype(jnp.float32) * jnp.where(lane < MEAN, scale, 0.0)
    return jnp.concatenate([low, high], axis=1)


def split_terms(values, count):
    terms = []
    for _ in range(count):
        term = values.astype(jnp.bfloat16)
        terms.append(term)
        values = values - term.astype(jnp.float32)
    return terms


def merge_kernel(words_ref, out_ref):
    lane = lax.broadcasted_iota(jnp.int32, (N_FIRST, LANES), 1)
    records = [words_ref[pl.ds(k, N_FIRST, stride=ROWS), :] for k in range(ROWS)]
    last = pltpu.roll(records[0], FREE, 1)
    for k in range(1, ROWS):
        last = jnp.where(lane < FREE * k, last, pltpu.roll(records[k], FREE * (k + 1), 1))
    words = jnp.concatenate(records + [last], axis=0)
    values = decode(words, MEAN_PAIR)
    rows = N_REST * NODE_DEV
    place = lax.broadcasted_iota(jnp.int32, (SLOTS, 1), 0) // (CAP * N_FIRST)
    node = words[:, NODE : NODE + 1]
    node = jnp.where(node >= 0, node + place * NODE_DEV, -1)
    owner = lax.broadcasted_iota(jnp.int32, (SLOTS, rows), 1) == node
    owner = jnp.where(owner, 1.0, 0.0).astype(jnp.bfloat16)
    terms = jnp.concatenate(split_terms(values, 2), axis=1)
    total = lax.dot_general(
        owner, terms, (((0,), (0,)), ((), ())), preferred_element_type=jnp.float32
    )
    low = total[:, :LANES] + total[:, 2 * LANES : 3 * LANES]
    high = total[:, LANES : 2 * LANES] + total[:, 3 * LANES :]
    size = jnp.maximum(jnp.abs(low), jnp.abs(high))
    lane = lax.broadcasted_iota(jnp.int32, size.shape, 1)
    step_w = scale_step(jnp.max(jnp.where(lane < W_LANES, size, 0.0), axis=1, keepdims=True))
    step_f = scale_step(
        jnp.max(jnp.where((lane >= W_LANES) & (lane < MEAN), size, 0.0), axis=1, keepdims=True)
    )
    factor = jnp.exp2(jnp.where(lane < W_LANES, step_w, step_f) * (-1.0 / STEPS)) * TOP
    factor = jnp.where(lane < MEAN, factor, 0.0)
    words = (jnp.round(high * factor).astype(jnp.int32) << 16) | (
        jnp.round(low * factor).astype(jnp.int32) & 0xFFFF
    )
    words = jnp.where(lane == MEAN, jnp.round(low * MEAN_NODE).astype(jnp.int32), words)
    words = jnp.where(lane == EXP_W, step_w.astype(jnp.int32), words)
    words = jnp.where(lane == EXP_F, step_f.astype(jnp.int32), words)
    for rank, member in enumerate(MEMBERS):
        start = member // N_HARM * NODE_DEV
        out_ref[rank * NODE_DEV : (rank + 1) * NODE_DEV] = words[start : start + NODE_DEV]


def expand_kernel(words_ref, table_ref, out_ref):
    nodes = N_HARM * NODE_DEV
    values = decode(words_ref[:nodes], MEAN_NODE)
    for part in range(1, N_REST):
        values += decode(words_ref[part * nodes : (part + 1) * nodes], MEAN_NODE)
    wrap = (N_HARM - H_FIRST) * NODE_DEV
    values = jnp.concatenate([values[wrap:], values[:wrap]], axis=0)
    terms = jnp.concatenate(split_terms(values, 2), axis=0)
    blocks = lax.dot_general(
        table_ref[...], terms, (((1,), (1,)), ((), ())), preferred_element_type=jnp.float32
    )
    blocks = (blocks[:, :nodes] + blocks[:, nodes:]).reshape(PER, PAD, nodes)
    out_ref[...] = blocks[:, :COEFS].astype(jnp.bfloat16)


def in_hbm(array):
    return pltpu.with_memory_space_constraint(array, pltpu.HBM)


def on_device(stick, stiffness, slip_tangent, contact_force, owner_node, live_pairs):
    pairs = stick.shape[1]
    vmem = pl.BlockSpec(memory_space=pltpu.VMEM)
    hbm = pl.BlockSpec(memory_space=pltpu.HBM)
    params = pltpu.CompilerParams(vmem_limit_bytes=32 * 1024 * 1024)
    analysis = analysis_table()
    slots, synthesis = pl.pallas_call(
        send_kernel,
        out_shape=(
            jax.ShapeDtypeStruct((ROWS * N_FIRST, LANES), jnp.int32),
            jax.ShapeDtypeStruct((T_ROWS, 2 * LANES), jnp.bfloat16),
        ),
        in_specs=[vmem] + [hbm] * 7,
        out_specs=(vmem, vmem),
        scratch_shapes=[
            pltpu.VMEM((SAMPLES, pairs), jnp.int32),
            pltpu.VMEM((1, pairs), jnp.float32),
            pltpu.VMEM((SAMPLES, pairs), jnp.float32),
            pltpu.VMEM((SAMPLES, pairs), jnp.float32),
            pltpu.VMEM((2, pairs), jnp.int32),
            pltpu.VMEM(analysis.shape, jnp.bfloat16),
            pltpu.SemaphoreType.DMA((7,)),
        ],
        compiler_params=params,
    )(
        jnp.broadcast_to(live_pairs.reshape(1, 1), (8, pairs)),
        in_hbm(stick),
        in_hbm(stiffness.reshape(1, pairs)),
        in_hbm(slip_tangent),
        in_hbm(contact_force),
        in_hbm(owner_node),
        in_hbm(jnp.asarray(analysis)),
        in_hbm(jnp.asarray(synthesis_table())),
    )
    slots = lax.all_to_all(
        slots.reshape(N_FIRST, 1, ROWS * LANES),
        ("xz", "c"),
        0,
        0,
        tiled=True,
        axis_index_groups=[peers(core) for core in range(N_REST)],
    )
    sums = pl.pallas_call(
        merge_kernel,
        out_shape=jax.ShapeDtypeStruct((N_REST * N_HARM * NODE_DEV, LANES), jnp.int32),
        in_specs=[vmem],
        out_specs=vmem,
        compiler_params=params,
    )(slots.reshape(ROWS * N_FIRST, LANES))
    sums = lax.all_to_all(
        sums.reshape(N_REST * N_HARM, NODE_DEV, LANES),
        ("c", "h"),
        0,
        0,
        tiled=True,
        axis_index_groups=[MEMBERS],
    )
    blocks = pl.pallas_call(
        expand_kernel,
        out_shape=jax.ShapeDtypeStruct((PER, COEFS, N_HARM * NODE_DEV), jnp.bfloat16),
        in_specs=[vmem, vmem],
        out_specs=vmem,
        compiler_params=params,
    )(sums.reshape(N_REST * N_HARM * NODE_DEV, LANES), synthesis)
    return jnp.transpose(blocks, (1, 0, 2))


def solution(mesh):
    fine = Mesh(mesh.devices.reshape(N_FIRST, N_REST, N_HARM), ("xz", "c", "h"))
    every = ("xz", "c", "h")
    return jax.shard_map(
        on_device,
        mesh=fine,
        in_specs=(P(None, every), P(every), P(None, every), P(None, every), P(None, every), P(every)),
        out_specs=P(None, "h", ("xz", "c")),
        check_vma=False,
    )
```
